128 devices in a mesh: section: 2 (over z_hi), ctx: 8 (over y, core), fsdp: 8 (over z_lo, x).
Axes of the slice: x: 4, y: 4, z: 4 (z_hi: 2, z_lo: 2; z = z_hi * 2 + z_lo), core: 2. Of those that a mesh axis runs over, the one named last changes fastest.
Arguments:
- block_input: bfloat16 [2, 8, 1024, 576], P(None, 'fsdp', 'ctx'), may hold values from -6 to 6
- cotangent: bfloat16 [2, 8, 1024, 576], P(None, 'fsdp', 'ctx'), may hold values from -6 to 6
- segment_ids: int32 [2, 8, 1024], P(None, 'fsdp'), may hold values from 0 to 2, as said below
- attn_gain: bfloat16 [2, 576], P('section', ('ctx', 'fsdp')), may hold values from 0.25 to 1.75
- w_query: bfloat16 [2, 576, 576], P('section', ('ctx', 'fsdp')), may hold values from -0.25 to 0.25
- w_key: bfloat16 [2, 576, 192], P('section', ('ctx', 'fsdp')), may hold values from -0.25 to 0.25
- w_value: bfloat16 [2, 576, 192], P('section', ('ctx', 'fsdp')), may hold values from -0.25 to 0.25
- w_out: bfloat16 [2, 576, 576], P('section', ('ctx', 'fsdp')), may hold values from -1 to 1
- w_gate: bfloat16 [2, 576, 1536], P('section', ('ctx', 'fsdp')), may hold values from -0.25 to 0.25
- w_up: bfloat16 [2, 576, 1536], P('section', ('ctx', 'fsdp')), may hold values from -0.25 to 0.25
- w_down: bfloat16 [2, 1536, 576], P('section', ('ctx', 'fsdp')), may hold values from -0.15625 to 0.15625
- mlp_gain: bfloat16 [2, 576], P('section', ('ctx', 'fsdp')), may hold values from 0.25 to 1.75
Outputs:
- edges: float32 [2, 2, 8, 1024, 576], P('section', None, 'fsdp', 'ctx')
- grad_attn_gain: float32 [2, 576], P('section', ('ctx', 'fsdp'))
- grad_w_query: float32 [2, 576, 576], P('section', ('ctx', 'fsdp'))
- grad_w_key: float32 [2, 576, 192], P('section', ('ctx', 'fsdp'))
- grad_w_value: float32 [2, 576, 192], P('section', ('ctx', 'fsdp'))
- grad_w_out: float32 [2, 576, 576], P('section', ('ctx', 'fsdp'))
- grad_w_gate: float32 [2, 576, 1536], P('section', ('ctx', 'fsdp'))
- grad_w_up: float32 [2, 576, 1536], P('section', ('ctx', 'fsdp'))
- grad_w_down: float32 [2, 1536, 576], P('section', ('ctx', 'fsdp'))
- grad_mlp_gain: float32 [2, 576], P('section', ('ctx', 'fsdp'))
The draws below stay inside these ranges and needn't reach their ends.
Inputs may be any that keep to these rules, and one draw needn't show every extreme that they name: `segment_ids`: each sequence holds three documents numbered 0, 1, 2 in order; document 0 ends within the first 128 positions and document 2 begins within the last 128.
All inputs are finite; a program needn't handle non-finite values.
Results may differ from the reference program's by a relative error of at most 0.025.
Values may be sent and summed in bfloat16 or wider, within the bound.
A program may use at most 128 MiB of HBM per device.

```python
import jax
import jax.numpy as jnp
from jax import lax

D = 576
HEADS = 9
KV_HEADS = 3
HEAD_DIM = 64
FF = 1536
MICRO = 2
ROWS = 128
SEQ = 1024
BATCH = 8
LAYERS = 2
QD = 576
KVD = 192
GROUP = 3


def draw_segment_ids(key, part):
    key = jax.random.fold_in(key, 7)
    first_key, second_key = jax.random.split(key)
    starts = jax.random.randint(first_key, (MICRO, BATCH, 1), 1, ROWS)
    last_begin = jax.random.randint(second_key, (MICRO, BATCH, 1), SEQ - ROWS + 1, SEQ)
    places = jnp.arange(SEQ, dtype=jnp.int32)[None, None, :]
    return (places >= starts).astype(jnp.int32) + (places >= last_begin).astype(jnp.int32)


def block_levels(stream_key, shape, cuts, low, high):
    def one(axis_at, blocks):
        heights = jax.random.uniform(jax.random.fold_in(jax.random.fold_in(stream_key, 6), axis_at), (blocks,), jnp.float32, low / len(cuts), high / len(cuts))
        return jnp.repeat(jnp.exp(heights), shape[axis_at] // blocks).reshape((-1,) + (1,) * (len(shape) - axis_at - 1))

    loudness = one(*cuts[0])
    for cut in cuts[1:]:
        loudness = loudness * one(*cut)
    return loudness


def noise(own_key, extent, scale, reach, shards=(), kind=jnp.bfloat16):
    drawn = scale * jax.random.normal(own_key, extent, jnp.float32)
    if shards:
        drawn = drawn * block_levels(own_key, extent, shards, -0.22, 0.18)
    return jnp.clip(drawn, -reach, reach).astype(kind)


def setup_inputs(seed: int = 0) -> dict:
    arg_keys = jax.random.split(jax.random.key(seed), 13)
    return {
        "block_input": noise(arg_keys[0], (MICRO, BATCH, SEQ, D), 1.0, 6.0, ((1, 8), (2, 8))),
        "cotangent": noise(arg_keys[1], (MICRO, BATCH, SEQ, D), 1.0, 6.0, ((1, 8), (2, 8))),
        "segment_ids": draw_segment_ids(jax.random.fold_in(arg_keys[12], 71), 0),
        "attn_gain": jnp.clip(1.0 + 0.15 * jax.random.normal(arg_keys[3], (LAYERS, D), jnp.float32), 0.25, 1.75).astype(jnp.bfloat16),
        "w_query": noise(arg_keys[4], (LAYERS, D, QD), D ** -0.5, 0.25, ((0, 2), (1, 64))),
        "w_key": noise(arg_keys[5], (LAYERS, D, KVD), D ** -0.5, 0.25, ((0, 2), (1, 64))),
        "w_value": noise(arg_keys[6], (LAYERS, D, KVD), D ** -0.5, 0.25, ((0, 2), (1, 64))),
        "w_out": noise(arg_keys[7], (LAYERS, QD, D), (QD // 16) ** -0.5, 1.0, ((0, 2), (1, 64))),
        "w_gate": noise(arg_keys[8], (LAYERS, D, FF), D ** -0.5, 0.25, ((0, 2), (1, 64))),
        "w_up": noise(arg_keys[9], (LAYERS, D, FF), D ** -0.5, 0.25, ((0, 2), (1, 64))),
        "w_down": noise(arg_keys[10], (LAYERS, FF, D), FF ** -0.5, 0.15625, ((0, 2), (1, 64))),
        "mlp_gain": jnp.clip(1.0 + 0.15 * jax.random.normal(arg_keys[11], (LAYERS, D), jnp.float32), 0.25, 1.75).astype(jnp.bfloat16),
    }


norm_eps = 1e-05
rope_base = 100000.0
masked_score = -1e+30

@jax.custom_vjp
def low(v):
    return lax.optimization_barrier(v.astype(jnp.bfloat16)).astype(jnp.float32)

@jax.custom_vjp
def low_back(v):
    return v

def low_keep(v):
    return (low(v), None)

def low_pass(kept, grad):
    return (grad,)

def back_keep(v):
    return (v, None)

def back_low(kept, grad):
    return (low(grad),)
low.defvjp(low_keep, low_pass)
low_back.defvjp(back_keep, back_low)

def matmul(left, right):
    return jnp.dot(left, right, precision=lax.Precision.HIGHEST)

def rope_tables(places):
    pair_index = jnp.arange(HEAD_DIM // 2).astype(jnp.float32)
    frequency = rope_base ** (-2.0 * pair_index / HEAD_DIM)
    angles = places.astype(jnp.float32)[:, None] * frequency[None, :]
    return (jnp.cos(angles), jnp.sin(angles))

def rotate(vectors, cos_table, sin_table):
    half_dim = vectors.shape[-1] // 2
    lower_half = vectors[..., :half_dim]
    upper_half = vectors[..., half_dim:]
    cos_part = cos_table[:, None, :]
    sin_part = sin_table[:, None, :]
    return jnp.concatenate([lower_half * cos_part - upper_half * sin_part, upper_half * cos_part + lower_half * sin_part], axis=-1)

def decoder_layer(hidden_in, seg_row, params):
    attn_gain, w_query, w_key, w_value, w_out, w_gate, w_up, w_down, mlp_gain = params
    places = jnp.arange(SEQ, dtype=jnp.int32)
    cos_table, sin_table = rope_tables(places)
    scale_one = lax.rsqrt(lax.optimization_barrier(jnp.mean(hidden_in * hidden_in, axis=-1, keepdims=True)) + norm_eps)
    normed = low(hidden_in * scale_one * attn_gain)
    queries = low(rotate(low_back(matmul(normed, w_query)).reshape(SEQ, HEADS, HEAD_DIM), cos_table, sin_table))
    key_rows = low(rotate(low_back(matmul(normed, w_key)).reshape(SEQ, KV_HEADS, HEAD_DIM), cos_table, sin_table))
    values = low(low_back(matmul(normed, w_value))).reshape(SEQ, KV_HEADS, HEAD_DIM)
    grouped = queries.reshape(SEQ, KV_HEADS, GROUP, HEAD_DIM)
    block_rows = min(512, SEQ)

    def attend(block_index):
        first_row = block_index * block_rows
        query_block = lax.dynamic_slice_in_dim(grouped, first_row, block_rows, 0)
        own_places = first_row + jnp.arange(block_rows, dtype=jnp.int32)
        own_seg = lax.dynamic_slice_in_dim(seg_row, first_row, block_rows, 0)
        raw_scores = jnp.einsum('qgrd,kgd->grqk', query_block, key_rows, precision=lax.Precision.HIGHEST)
        scores = low_back(raw_scores * HEAD_DIM ** (-0.5))
        allowed = (places[None, :] <= own_places[:, None]) & (seg_row[None, :] == own_seg[:, None])
        scores = jnp.where(allowed, scores, masked_score)
        row_max = lax.optimization_barrier(jnp.max(scores, axis=-1, keepdims=True))
        shifted = jnp.exp(scores - row_max)
        prob_rows = shifted / lax.optimization_barrier(jnp.sum(shifted, axis=-1, keepdims=True))
        return jnp.einsum('grqk,kgd->qgrd', low(prob_rows), values, precision=lax.Precision.HIGHEST)
    mixture = lax.map(jax.checkpoint(attend), jnp.arange(SEQ // block_rows, dtype=jnp.int32))
    attended = low(low_back(mixture.reshape(SEQ, HEADS * HEAD_DIM)))
    midway = hidden_in + low_back(matmul(attended, w_out))
    scale_two = lax.rsqrt(lax.optimization_barrier(jnp.mean(midway * midway, axis=-1, keepdims=True)) + norm_eps)
    normed_two = low(midway * scale_two * mlp_gain)
    gate_act = low_back(matmul(normed_two, w_gate))
    up_act = low_back(matmul(normed_two, w_up))
    hidden = low(jax.nn.silu(gate_act) * up_act)
    return midway + low_back(matmul(hidden, w_down))

def layer_slice(params, layer_index):
    return tuple((weight[layer_index] for weight in params))

def forward_row(input_row, seg_row, params):
    first_out = decoder_layer(input_row, seg_row, layer_slice(params, 0))
    passed = low(low_back(first_out))
    return decoder_layer(passed, seg_row, layer_slice(params, 1))

def reference(block_input, cotangent, segment_ids, attn_gain, w_query, w_key, w_value, w_out, w_gate, w_up, w_down, mlp_gain):
    params = tuple((weight.astype(jnp.float32) for weight in (attn_gain, w_query, w_key, w_value, w_out, w_gate, w_up, w_down, mlp_gain)))
    row_total = MICRO * BATCH
    inputs = block_input.astype(jnp.float32).reshape(row_total, SEQ, D)
    cotangents = cotangent.astype(jnp.float32).reshape(row_total, SEQ, D)
    segments = segment_ids.reshape(row_total, SEQ)

    def one_row(totals, row_items):
        input_row, cot_row, seg_row = row_items

        def row_forward(input_vals, param_vals):
            return forward_row(input_vals, seg_row, param_vals)
        output_row, pull_back = jax.vjp(row_forward, input_row, params)
        input_grad, param_grads = pull_back(cot_row)
        totals = jax.tree.map(lambda running, addend: running + addend, totals, param_grads)
        return (totals, (input_grad, output_row))
    start_totals = jax.tree.map(jnp.zeros_like, params)
    totals, outcome = lax.scan(one_row, start_totals, (inputs, cotangents, segments))
    edges = jnp.stack([outcome[0], outcome[1]]).reshape(2, MICRO, BATCH, SEQ, D)
    return (edges, totals[0], totals[1], totals[2], totals[3], totals[4], totals[5], totals[6], totals[7], totals[8])
```

```python
import functools

import jax
import jax.numpy as jnp
from jax import lax
from jax.experimental import pallas as pl
from jax.experimental.pallas import tpu as pltpu
from jax.sharding import PartitionSpec as P

MESH = pl.DeviceIdType.MESH
F32 = jnp.float32
BF16 = jnp.bfloat16
ANY = pl.BlockSpec(memory_space=pl.ANY)
VMEM = pl.BlockSpec(memory_space=pltpu.VMEM)

D = 576
FF = 1536
KVD = 192
HEAD = 64
GROUP = 3
KV_HEADS = 3
ROWS = 128
SEQ = 1024
LANES = 128

norm_eps = 1e-05
rope_base = 100000.0
masked_score = -1e30

WIDE = 4608
GATE_AT = 768
UP_AT = GATE_AT + FF
OUT_AT = UP_AT + FF
VALUE_AT = OUT_AT + D
TAIL_AT = VALUE_AT - HEAD
BLOCKS = WIDE // LANES

DOWN_ROWS = 24
TAIL_ROW = 4 * DOWN_ROWS
WIDE_ROW = TAIL_ROW + DOWN_ROWS // 2
GAIN_ROW = WIDE_ROW + 9 * BLOCKS
PACKED = GAIN_ROW + 16
THIRDS = ((0, 160), (160, 144), (304, 144))
AXIS_ORDERS = (("z", "x", "y"), ("x", "y", "z"), ("y", "z", "x"))
VMEM_BYTES = 60 * 1024 * 1024


def params(collective_id=None):
    if collective_id is None:
        return pltpu.CompilerParams(vmem_limit_bytes=VMEM_BYTES)
    return pltpu.CompilerParams(
        vmem_limit_bytes=VMEM_BYTES, collective_id=collective_id, has_side_effects=True
    )


def dot(left, right):
    return jnp.dot(left, right, preferred_element_type=F32)


def dot_nt(left, right):
    return lax.dot_general(left, right, (((1,), (1,)), ((), ())), preferred_element_type=F32)


def dot_tn(left, right):
    return lax.dot_general(left, right, (((0,), (0,)), ((), ())), preferred_element_type=F32)


class Place:
    def __init__(self):
        self.section = lax.axis_index("section")
        ctx = lax.axis_index("ctx")
        fsdp = lax.axis_index("fsdp")
        self.core = lax.rem(ctx, 2)
        self.at = {
            "x": lax.rem(fsdp, 4),
            "y": ctx // 2,
            "z": self.section * 2 + fsdp // 4,
        }

    def device(self, core=None, **moved):
        at = dict(self.at, **moved)
        core = self.core if core is None else core
        return (at["z"] // 2, at["y"] * 2 + core, lax.rem(at["z"], 2) * 4 + at["x"])

    def shifted(self, axis, step):
        return lax.rem(self.at[axis] + step + 4, 4)

    def neighbour(self, axis, step):
        return self.device(**{axis: self.shifted(axis, step)})

    def partner(self):
        return self.device(core=1 - self.core)


def greet(devices):
    barrier = pltpu.get_barrier_semaphore()
    for device in devices:
        pl.semaphore_signal(barrier, inc=1, device_id=device, device_id_type=MESH)
    pl.semaphore_wait(barrier, len(devices))


def torus_neighbours(place):
    return [place.neighbour(axis, step) for axis in "xyz" for step in (1, -1)]


def region(ref, coords, whole, rows, core):
    first, count = rows
    z_hi = slice(None) if "z" in whole else coords["z"] // 2
    z_lo = slice(None) if "z" in whole else lax.rem(coords["z"], 2)
    y = slice(None) if "y" in whole else coords["y"]
    x = slice(None) if "x" in whole else coords["x"]
    if core is None:
        return ref.at[z_hi, y, z_lo, x, pl.ds(first, count)]
    return ref.at[z_hi, y, core, z_lo, x, pl.ds(first, count)]


def halves(rows):
    first, count = rows
    upper = (count // 2 + 15) // 16 * 16
    return (first, upper), (first + upper, count - upper)


def gather_kernel(mine_ref, out_ref, local_sem, send_sems, recv_sems):
    place = Place()
    core = place.core
    greet(torus_neighbours(place) + [place.partner()])

    own = out_ref.at[place.section, place.at["y"], core, lax.rem(place.at["z"], 2), place.at["x"]]
    seed = pltpu.make_async_copy(mine_ref, own, local_sem)
    seed.start()
    seed.wait()

    counter = [0]
    unsent = []

    def send(ref, device):
        slot = counter[0]
        counter[0] += 1
        copy = pltpu.make_async_remote_copy(
            src_ref=ref,
            dst_ref=ref,
            send_sem=send_sems.at[slot],
            recv_sem=recv_sems.at[slot],
            device_id=device,
            device_id_type=MESH,
        )
        copy.start()
        unsent.append(copy)
        return copy

    to_partner = []
    for phase in range(3):
        arriving = []
        for third, rows in enumerate(THIRDS):
            axis = AXIS_ORDERS[third][phase]
            whole = AXIS_ORDERS[third][:phase]
            block = region(out_ref, place.at, whole, rows, core)
            arriving.append(
                [send(block, place.neighbour(axis, 1)), send(block, place.neighbour(axis, -1))]
            )
            if phase == 2:
                to_partner.append(send(block, place.partner()))
        second = []
        for third, rows in enumerate(THIRDS):
            axis = AXIS_ORDERS[third][phase]
            whole = AXIS_ORDERS[third][:phase]
            for copy in arriving[third]:
                copy.wait_recv()
            upper, lower = halves(rows)
            left = dict(place.at, **{axis: place.shifted(axis, -1)})
            right = dict(place.at, **{axis: place.shifted(axis, 1)})
            second.append(
                [
                    send(region(out_ref, left, whole, upper, core), place.neighbour(axis, 1)),
                    send(region(out_ref, right, whole, lower, core), place.neighbour(axis, -1)),
                ]
            )
            if phase == 2:
                for coords in (left, right):
                    to_partner.append(
                        send(region(out_ref, coords, whole, rows, core), place.partner())
                    )
        for third, rows in enumerate(THIRDS):
            axis = AXIS_ORDERS[third][phase]
            whole = AXIS_ORDERS[third][:phase]
            for copy in second[third]:
                copy.wait_recv()
            if phase == 2:
                far = dict(place.at, **{axis: place.shifted(axis, 2)})
                to_partner.append(send(region(out_ref, far, whole, rows, core), place.partner()))
    for copy in to_partner:
        copy.wait_recv()
    for copy in unsent:
        copy.wait_send()


def gather_weights(packed):
    slots = 3 * 3 * 4 + 3 * 4
    return pl.pallas_call(
        gather_kernel,
        out_shape=jax.ShapeDtypeStruct((2, 4, 2, 2, 4, PACKED, LANES), BF16),
        in_specs=[ANY],
        out_specs=ANY,
        scratch_shapes=[
            pltpu.SemaphoreType.DMA,
            pltpu.SemaphoreType.DMA((slots,)),
            pltpu.SemaphoreType.DMA((slots,)),
        ],
        compiler_params=params(0),
        name="gather_weights",
    )(packed)


def scatter_kernel(
    first_ref,
    second_ref,
    edge_ref,
    out_ref,
    edge_out_ref,
    total,
    swapped,
    arrivals_0,
    arrivals_1,
    arrivals_2,
    local_sems,
    swap_send,
    swap_recv,
    send_sems,
    recv_sems,
    edge_send,
    edge_recv,
):
    place = Place()
    core = place.core
    across = (1 - place.section, lax.axis_index("ctx"), lax.axis_index("fsdp"))
    greet(torus_neighbours(place) + [place.partner(), across])

    swaps = []
    loads = []
    for third, (first, count) in enumerate(THIRDS):
        rows = pl.ds(first, count)
        for layer, part_ref in enumerate((first_ref, second_ref)):
            slot = third * 2 + layer
            swap = pltpu.make_async_remote_copy(
                src_ref=part_ref.at[:, 1 - core, :, :, rows],
                dst_ref=swapped.at[layer, :, :, :, rows],
                send_sem=swap_send.at[slot],
                recv_sem=swap_recv.at[slot],
                device_id=place.partner(),
                device_id_type=MESH,
            )
            swap.start()
            load = pltpu.make_async_copy(
                part_ref.at[:, core, :, :, rows],
                total.at[layer, :, :, :, rows],
                local_sems.at[slot],
            )
            load.start()
            swaps.append(swap)
            loads.append(load)
    edge = pltpu.make_async_remote_copy(
        src_ref=edge_ref,
        dst_ref=edge_out_ref,
        send_sem=edge_send,
        recv_sem=edge_recv,
        device_id=across,
        device_id_type=MESH,
    )
    edge.start()

    counter = [0]
    unsent = []

    def send(source, target, device):
        slot = counter[0]
        counter[0] += 1
        copy = pltpu.make_async_remote_copy(
            src_ref=source,
            dst_ref=target,
            send_sem=send_sems.at[slot],
            recv_sem=recv_sems.at[slot],
            device_id=device,
            device_id_type=MESH,
        )
        copy.start()
        unsent.append(copy)
        return copy

    def add(coords, whole, rows, source, first=0):
        at, count = rows
        sizes = [4 if axis in whole else 1 for axis in "zyx"]

        def body(step, carry):
            z = step // (sizes[1] * sizes[2])
            y = lax.rem(step // sizes[2], sizes[1])
            x = lax.rem(step, sizes[2])
            spot = (
                z if "z" in whole else coords["z"],
                y if "y" in whole else coords["y"],
                x if "x" in whole else coords["x"],
            )
            here = (spot[0] // 2, spot[1], lax.rem(spot[0], 2), spot[2], pl.ds(at, count))
            total[here] = (
                total[here].astype(F32) + source(z, y, x, first, count).astype(F32)
            ).astype(BF16)
            return carry

        lax.fori_loop(0, sizes[0] * sizes[1] * sizes[2], body, 0)

    def swapped_part(rows):
        def load(z, y, x, first, count):
            return swapped[z // 2, y, lax.rem(z, 2), x, pl.ds(rows[0], count)]

        return load

    arrivals = (arrivals_0, arrivals_1, arrivals_2)
    used = [0, 0, 0]

    def ring(third, phase, step):
        rows = THIRDS[third]
        order = AXIS_ORDERS[third][::-1]
        axis = order[phase]
        whole = order[phase + 1 :]
        upper, lower = halves(rows)
        right = dict(place.at, **{axis: place.shifted(axis, 1)})
        left = dict(place.at, **{axis: place.shifted(axis, -1)})
        far = dict(place.at, **{axis: place.shifted(axis, 2)})
        if step == 0:
            plan = ((far, upper, 1, right), (far, lower, -1, left))
        else:
            plan = ((right, rows, 1, place.at), (left, rows, -1, place.at))
        started = []
        for source_at, part, way, lands in plan:
            device = place.neighbour(axis, way)
            first = used[third]
            used[third] += 1
            copy = send(
                region(total, source_at, whole, part, None),
                landing(third, first, whole, part[1]),
                device,
            )
            started.append((copy, lands, part, first, whole))
        return started

    def landing(third, slot, whole, count):
        z_hi = slice(None) if "z" in whole else 0
        z_lo = slice(None) if "z" in whole else 0
        y = slice(None) if "y" in whole else 0
        x = slice(None) if "x" in whole else 0
        return arrivals[third].at[slot, z_hi, y, z_lo, x, pl.ds(0, count)]

    def arrived_part(third, slot):
        def load(z, y, x, first, count):
            return arrivals[third][slot, z // 2, y, lax.rem(z, 2), x, pl.ds(0, count)]

        return load

    def finish(third, started):
        for copy, lands, part, slot, whole in started:
            copy.wait()
            add(lands, whole, part, arrived_part(third, slot))

    flights = []
    for third, rows in enumerate(THIRDS):
        for layer in range(2):
            loads[third * 2 + layer].wait()
            swaps[third * 2 + layer].wait()
        add(place.at, ("z", "y", "x"), rows, swapped_part(rows))
        flights.append(ring(third, 0, 0))
    for phase in range(3):
        for step in range(2):
            for third in range(3):
                finish(third, flights[third])
                if step == 0:
                    flights[third] = ring(third, phase, 1)
                elif phase < 2:
                    flights[third] = ring(third, phase + 1, 0)

    z, y, x = place.at["z"], place.at["y"], place.at["x"]
    out_ref[...] = total[z // 2, y, lax.rem(z, 2), x].astype(F32)
    edge.wait()


def scatter_grads(first, second, edge):
    slots = 3 * 3 * 4
    return pl.pallas_call(
        scatter_kernel,
        out_shape=(
            jax.ShapeDtypeStruct((PACKED, LANES), F32),
            jax.ShapeDtypeStruct((ROWS, D), F32),
        ),
        in_specs=[ANY, ANY, VMEM],
        out_specs=(VMEM, VMEM),
        scratch_shapes=[
            pltpu.VMEM((2, 4, 2, 4, PACKED, LANES), BF16),
            pltpu.VMEM((2, 4, 2, 4, PACKED, LANES), BF16),
            pltpu.VMEM((12, 2, 1, 2, 4, 160, LANES), BF16),
            pltpu.VMEM((12, 1, 4, 1, 4, 144, LANES), BF16),
            pltpu.VMEM((12, 2, 4, 2, 1, 144, LANES), BF16),
            pltpu.SemaphoreType.DMA((6,)),
            pltpu.SemaphoreType.DMA((6,)),
            pltpu.SemaphoreType.DMA((6,)),
            pltpu.SemaphoreType.DMA((slots,)),
            pltpu.SemaphoreType.DMA((slots,)),
            pltpu.SemaphoreType.DMA,
            pltpu.SemaphoreType.DMA,
        ],
        compiler_params=params(1),
        name="scatter_grads",
    )(first, second, edge)


def ctx_device(index):
    return (lax.axis_index("section"), index, lax.axis_index("fsdp"))


def greet_ctx(mine):
    greet([ctx_device(lax.rem(mine + away, 8)) for away in range(1, 8)])


def keys_kernel(mine_ref, out_ref, send_sems, recv_sems):
    mine = lax.axis_index("ctx")
    greet_ctx(mine)

    def copy_to(away):
        return pltpu.make_async_remote_copy(
            src_ref=mine_ref,
            dst_ref=out_ref.at[mine],
            send_sem=send_sems.at[away],
            recv_sem=recv_sems.at[away],
            device_id=ctx_device(lax.rem(mine + away, 8)),
            device_id_type=MESH,
        )

    for away in range(1, 8):

        @pl.when(mine + away < 8)
        def _():
            copy_to(away).start()

    out_ref[mine] = mine_ref[...]
    for away in range(1, 8):

        @pl.when(mine + away < 8)
        def _():
            out_ref[mine + away] = jnp.zeros(out_ref.shape[1:], out_ref.dtype)

    for away in range(1, 8):

        @pl.when(mine - away >= 0)
        def _():
            copy_to(away).wait_recv()

    for away in range(1, 8):

        @pl.when(mine + away < 8)
        def _():
            copy_to(away).wait_send()


def gather_keys(joined, collective_id):
    return pl.pallas_call(
        keys_kernel,
        out_shape=jax.ShapeDtypeStruct((8, ROWS, 2 * KVD), BF16),
        in_specs=[VMEM],
        out_specs=VMEM,
        scratch_shapes=[pltpu.SemaphoreType.DMA((8,)), pltpu.SemaphoreType.DMA((8,))],
        compiler_params=params(collective_id),
        name="gather_keys",
    )(joined)


def key_grads_kernel(parts_ref, out_ref, arrived, send_sems, recv_sems):
    mine = lax.axis_index("ctx")
    greet_ctx(mine)

    def copy_to(away):
        return pltpu.make_async_remote_copy(
            src_ref=parts_ref.at[lax.rem(mine - away + 8, 8)],
            dst_ref=arrived.at[away],
            send_sem=send_sems.at[away],
            recv_sem=recv_sems.at[away],
            device_id=ctx_device(lax.rem(mine - away + 8, 8)),
            device_id_type=MESH,
        )

    for away in range(1, 8):

        @pl.when(mine - away >= 0)
        def _():
            copy_to(away).start()

    out_ref[...] = parts_ref[mine].astype(F32)
    for away in range(1, 8):

        @pl.when(mine + away < 8)
        def _():
            copy_to(away).wait_recv()
            out_ref[...] += arrived[away].astype(F32)

    for away in range(1, 8):

        @pl.when(mine - away >= 0)
        def _():
            copy_to(away).wait_send()


def scatter_key_grads(parts, collective_id):
    return pl.pallas_call(
        key_grads_kernel,
        out_shape=jax.ShapeDtypeStruct((2 * KVD, ROWS), F32),
        in_specs=[VMEM],
        out_specs=VMEM,
        scratch_shapes=[
            pltpu.VMEM((8, 2 * KVD, ROWS), BF16),
            pltpu.SemaphoreType.DMA((8,)),
            pltpu.SemaphoreType.DMA((8,)),
        ],
        compiler_params=params(collective_id),
        name="scatter_key_grads",
    )(parts)


def pack_kernel(
    attn_ref, query_ref, key_ref, value_ref, w_out_ref, gate_ref, up_ref, down_ref, mlp_ref, out_ref
):
    def wide(ref):
        return ref[0].astype(F32)

    joined = jnp.concatenate(
        [wide(r) for r in (query_ref, key_ref, gate_ref, up_ref, w_out_ref, value_ref)], axis=1
    )
    down = wide(down_ref)
    pieces = [down[:, i * LANES : (i + 1) * LANES] for i in range(4)]
    half = DOWN_ROWS // 2
    pieces.append(jnp.concatenate([down[:half, 4 * LANES :], down[half:, 4 * LANES :]], axis=1))
    pieces += [joined[:, i * LANES : (i + 1) * LANES] for i in range(BLOCKS)]
    for ref in (attn_ref, mlp_ref):
        gain = ref[...].astype(F32)
        pieces.append(jnp.concatenate([gain, jnp.zeros((1, LANES - 9), F32)], axis=1))
    pieces.append(jnp.zeros((14, LANES), F32))
    out_ref[...] = jnp.concatenate(pieces, axis=0).astype(BF16)


def pack_shards(shards):
    return pl.pallas_call(
        pack_kernel,
        out_shape=jax.ShapeDtypeStruct((PACKED, LANES), BF16),
        in_specs=[VMEM] * 9,
        out_specs=VMEM,
        compiler_params=params(),
        name="pack_shards",
    )(*shards)


def gain_masks(first_device, devices, rows_each):
    shape = (devices * rows_each, D)
    row = lax.broadcasted_iota(jnp.int32, shape, 0)
    owner = lax.broadcasted_iota(jnp.int32, shape, 1) // 9
    same = owner == first_device + row // rows_each
    place = lax.rem(row, rows_each)
    return same & (place == 0), same & (place == 1)


def lane_spread():
    lane = lax.broadcasted_iota(jnp.int32, (LANES, D), 0)
    feature = lax.broadcasted_iota(jnp.int32, (LANES, D), 1)
    return (lane == lax.rem(feature, 9)).astype(BF16)


def unpack_kernel(packed_ref, wide_ref, down_ref, gains_ref):
    block = pl.program_id(1)
    count = packed_ref.shape[0]
    held = [packed_ref[i].astype(F32) for i in range(count)]
    for column in range(BLOCKS):
        at = WIDE_ROW + 9 * column
        wide_ref[0, :, column * LANES : (column + 1) * LANES] = jnp.concatenate(
            [h[at : at + 9] for h in held], axis=0
        ).astype(BF16)
    for column in range(4):
        at = DOWN_ROWS * column
        down_ref[0, :, column * LANES : (column + 1) * LANES] = jnp.concatenate(
            [h[at : at + DOWN_ROWS] for h in held], axis=0
        ).astype(BF16)
    tails = []
    for h in held:
        tail = h[TAIL_ROW:WIDE_ROW]
        tails += [tail[:, :HEAD], tail[:, HEAD:]]
    down_ref[0, :, 4 * LANES :] = jnp.concatenate(tails, axis=0).astype(BF16)
    rows = packed_ref[:, GAIN_ROW:, :].reshape(count * 16, LANES)
    spread = dot(rows, lane_spread())
    first, second = gain_masks(block * count, count, 16)
    gains = [
        jnp.sum(jnp.where(mask, spread, 0.0), axis=0, keepdims=True) for mask in (first, second)
    ]

    @pl.when(block == 0)
    def _():
        gains_ref[...] = jnp.zeros_like(gains_ref)

    gains_ref[0, 0:1] += gains[0]
    gains_ref[0, 1:2] += gains[1]


def unpack_weights(gathered):
    count = 16
    return pl.pallas_call(
        unpack_kernel,
        grid=(2, 4),
        out_shape=(
            jax.ShapeDtypeStruct((2, D, WIDE), BF16),
            jax.ShapeDtypeStruct((2, FF, D), BF16),
            jax.ShapeDtypeStruct((2, 8, D), F32),
        ),
        in_specs=[pl.BlockSpec((count, PACKED, LANES), lambda s, y: (s * 4 + y, 0, 0))],
        out_specs=(
            pl.BlockSpec((1, 9 * count, WIDE), lambda s, y: (s, y, 0)),
            pl.BlockSpec((1, DOWN_ROWS * count, D), lambda s, y: (s, y, 0)),
            pl.BlockSpec((1, 8, D), lambda s, y: (s, 0, 0)),
        ),
        compiler_params=params(),
        name="unpack_weights",
    )(gathered.reshape(128, PACKED, LANES))


def finish_kernel(
    packed_ref,
    kept_ref,
    came_ref,
    edges_ref,
    attn_ref,
    query_ref,
    key_ref,
    value_ref,
    w_out_ref,
    gate_ref,
    up_ref,
    down_ref,
    mlp_ref,
):
    section = lax.axis_index("section")
    edges_ref[0, section, 0] = kept_ref[...]
    edges_ref[0, 1 - section, 0] = came_ref[...]
    packed = packed_ref[...]
    joined = jnp.concatenate(
        [packed[WIDE_ROW + 9 * i : WIDE_ROW + 9 * i + 9] for i in range(BLOCKS)], axis=1
    )
    query_ref[0] = joined[:, :D]
    key_ref[0] = joined[:, D:GATE_AT]
    gate_ref[0] = joined[:, GATE_AT:UP_AT]
    up_ref[0] = joined[:, UP_AT:OUT_AT]
    w_out_ref[0] = joined[:, OUT_AT:VALUE_AT]
    value_ref[0] = joined[:, VALUE_AT:]
    tail = packed[TAIL_ROW:WIDE_ROW]
    down_ref[0] = jnp.concatenate(
        [packed[DOWN_ROWS * i : DOWN_ROWS * (i + 1)] for i in range(4)]
        + [jnp.concatenate([tail[:, :HEAD], tail[:, HEAD:]], axis=0)],
        axis=1,
    )
    attn_ref[...] = packed[GAIN_ROW : GAIN_ROW + 1, :9]
    mlp_ref[...] = packed[GAIN_ROW + 1 : GAIN_ROW + 2, :9]


def finish(packed, kept, came):
    shapes = (
        (1, 2, 1, ROWS, D),
        (1, 9),
        (1, 9, D),
        (1, 9, KVD),
        (1, 9, KVD),
        (1, 9, D),
        (1, 9, FF),
        (1, 9, FF),
        (1, DOWN_ROWS, D),
        (1, 9),
    )
    return pl.pallas_call(
        finish_kernel,
        out_shape=tuple(jax.ShapeDtypeStruct(shape, F32) for shape in shapes),
        in_specs=[VMEM] * 3,
        out_specs=(VMEM,) * len(shapes),
        compiler_params=params(),
        name="finish",
    )(packed, kept, came)


def swap_halves(block):
    lane = lax.broadcasted_iota(jnp.int32, block.shape, 1)
    return jnp.where(
        lax.rem(lane, HEAD) < HEAD // 2,
        pltpu.roll(block, LANES - HEAD // 2, 1),
        pltpu.roll(block, HEAD // 2, 1),
    )


def rotated(block, cos, sin):
    return block * cos + swap_halves(block) * sin


def project(current, gain, weights, cos, sin, normed_ref, query_ref, joined_ref):
    scale = lax.rsqrt(jnp.mean(current * current, axis=1, keepdims=True) + norm_eps)
    normed = (current * scale * gain).astype(BF16)
    normed_ref[...] = normed
    raw = dot(normed, weights.get("qk"))
    turned = [
        rotated(raw[:, i * LANES : (i + 1) * LANES], cos, sin).astype(BF16) for i in range(6)
    ]
    for i in range(4):
        query_ref[:, i * LANES : (i + 1) * LANES] = turned[i]
    query_ref[:, 4 * LANES :] = turned[4][:, :HEAD]
    values = dot(normed, weights.get("tail"))[:, HEAD:]
    joined_ref[...] = jnp.concatenate(
        [turned[4][:, HEAD:].astype(F32), turned[5].astype(F32), values], axis=1
    ).astype(BF16)


def heads_of(rows, group):
    return jnp.concatenate(
        [rows[:, (group * GROUP + r) * HEAD : (group * GROUP + r + 1) * HEAD] for r in range(GROUP)],
        axis=0,
    )


def attend(query_ref, keys_ref, own_seg_ref, seg_ref, probs_ref):
    first = lax.axis_index("ctx") * ROWS
    rows = first + lax.broadcasted_iota(jnp.int32, (ROWS, SEQ), 0)
    columns = lax.broadcasted_iota(jnp.int32, (ROWS, SEQ), 1)
    allowed = (columns <= rows) & (seg_ref[...] == own_seg_ref[...])
    bias = jnp.where(allowed, 0.0, masked_score)
    bias = jnp.concatenate([bias] * GROUP, axis=0)
    queries = query_ref[...]
    mixed = []
    for group in range(KV_HEADS):
        keys = keys_ref[:, :, group * HEAD : (group + 1) * HEAD].reshape(SEQ, HEAD)
        values = keys_ref[:, :, KVD + group * HEAD : KVD + (group + 1) * HEAD].reshape(SEQ, HEAD)
        scores = dot_nt(heads_of(queries, group), keys) * HEAD**-0.5 + bias
        shifted = jnp.exp(scores - jnp.max(scores, axis=1, keepdims=True))
        probs = (shifted / jnp.sum(shifted, axis=1, keepdims=True)).astype(BF16)
        probs_ref[group] = probs
        mixture = dot(probs, values)
        mixed += [mixture[r * ROWS : (r + 1) * ROWS] for r in range(GROUP)]
    return jnp.concatenate(mixed, axis=1).astype(BF16)


def feed_forward(current, attended, gain, weights):
    midway = current + dot(attended, weights.out())
    scale = lax.rsqrt(jnp.mean(midway * midway, axis=1, keepdims=True) + norm_eps)
    normed = (midway * scale * gain).astype(BF16)
    gate = dot(normed, weights.get("gate"))
    up = dot(normed, weights.get("up"))
    hidden = (gate / (1.0 + jnp.exp(-gate)) * up).astype(BF16)
    result = midway + dot(hidden, weights.get("down"))
    return midway, scale, normed, gate, up, hidden, result


def norm_backward(scaled, values, scale):
    return scale * scaled - values * scale**3 * jnp.mean(scaled * values, axis=1, keepdims=True)


def feed_forward_back(
    incoming, midway, gate, up, gain, weights
):
    scale = lax.rsqrt(jnp.mean(midway * midway, axis=1, keepdims=True) + norm_eps)
    down_grad = incoming.astype(BF16)
    hidden_grad = dot_nt(down_grad, weights.get("down"))
    sigmoid = 1.0 / (1.0 + jnp.exp(-gate))
    gate_grad = (hidden_grad * up * sigmoid * (1.0 + gate * (1.0 - sigmoid))).astype(BF16)
    up_grad = (hidden_grad * gate * sigmoid).astype(BF16)
    normed_grad = dot_nt(gate_grad, weights.get("gate")) + dot_nt(
        up_grad, weights.get("up")
    )
    gain_grad = jnp.sum(normed_grad * midway * scale, axis=0, keepdims=True)
    midway_grad = incoming + norm_backward(normed_grad * gain, midway, scale)
    out_grad = midway_grad.astype(BF16)
    mixed_grad = dot_nt(out_grad, weights.out()).astype(BF16)
    return down_grad, gate_grad, up_grad, gain_grad, midway_grad, out_grad, mixed_grad


def attend_back(mixed_grad, attended, query_ref, keys_ref, probs_ref, parts_ref):
    queries = query_ref[...]
    query_grads = []
    for group in range(KV_HEADS):
        keys = keys_ref[:, :, group * HEAD : (group + 1) * HEAD].reshape(SEQ, HEAD)
        values = keys_ref[:, :, KVD + group * HEAD : KVD + (group + 1) * HEAD].reshape(SEQ, HEAD)
        grads = heads_of(mixed_grad, group)
        delta = jnp.sum(
            grads.astype(F32) * heads_of(attended, group).astype(F32), axis=1, keepdims=True
        )
        probs = probs_ref[group]
        score_grad = (probs.astype(F32) * (dot_nt(grads, values) - delta)).astype(BF16)
        query_grad = dot(score_grad, keys) * HEAD**-0.5
        query_grads += [query_grad[r * ROWS : (r + 1) * ROWS] for r in range(GROUP)]
        key_part = (dot_tn(heads_of(queries, group), score_grad) * HEAD**-0.5).astype(BF16)
        value_part = dot_tn(grads, probs).astype(BF16)
        for block in range(8):
            columns = slice(block * ROWS, (block + 1) * ROWS)
            parts_ref[block, group * HEAD : (group + 1) * HEAD] = key_part[:, columns]
            parts_ref[block, KVD + group * HEAD : KVD + (group + 1) * HEAD] = value_part[:, columns]
    return jnp.concatenate(query_grads, axis=1)


def project_back(
    query_grad, key_grads, midway_grad, current, gain, cos, sin, weights
):
    key_grads = key_grads.T
    joined = jnp.concatenate([query_grad, key_grads[:, :KVD]], axis=1)
    turned = jnp.concatenate(
        [rotated(joined[:, i * LANES : (i + 1) * LANES], cos, -sin) for i in range(6)], axis=1
    ).astype(BF16)
    values = key_grads[:, KVD:].astype(BF16)
    padded = jnp.concatenate([jnp.zeros((ROWS, HEAD), F32), key_grads[:, KVD:]], axis=1)
    normed_grad = dot_nt(turned, weights.get("qk")) + dot_nt(
        padded.astype(BF16), weights.get("tail")
    )
    scale = lax.rsqrt(jnp.mean(current * current, axis=1, keepdims=True) + norm_eps)
    gain_grad = jnp.sum(normed_grad * current * scale, axis=0, keepdims=True)
    grad_in = midway_grad + norm_backward(normed_grad * gain, current, scale)
    return turned, values, gain_grad, grad_in


GRAD_DEVICES = 16


def weight_grads(
    normed,
    turned,
    values,
    attended,
    out_grad,
    normed_two,
    gate_grad,
    up_grad,
    hidden,
    down_grad,
    attn_gain_grad,
    mlp_gain_grad,
    out_ref,
    lhs_ref,
    hidden_ref,
    stage,
):
    lhs_ref[0] = normed.astype(F32).T.astype(BF16)
    lhs_ref[1] = normed_two.astype(F32).T.astype(BF16)
    lhs_ref[2] = attended.astype(F32).T.astype(BF16)
    hidden_ref[...] = hidden.astype(F32).T.astype(BF16)
    count = GRAD_DEVICES

    def body(step, carry):
        rows = pl.ds(pl.multiple_of(step * 9 * count, 16), 9 * count)

        def place_wide(column, product):
            for i in range(product.shape[1] // LANES):
                at = WIDE_ROW + 9 * (column + i)
                part = product[:, i * LANES : (i + 1) * LANES]
                for d in range(count):
                    stage[d, at : at + 9] = part[9 * d : 9 * d + 9]

        first = lhs_ref[0, rows]
        place_wide(0, dot(first, turned))
        second = lhs_ref[1, rows]
        place_wide(GATE_AT // LANES, dot(second, gate_grad))
        place_wide(UP_AT // LANES, dot(second, up_grad))
        place_wide(
            OUT_AT // LANES,
            jnp.concatenate([dot(lhs_ref[2, rows], out_grad), dot(first, values)], axis=1),
        )
        down_rows = pl.ds(pl.multiple_of(step * DOWN_ROWS * count, 16), DOWN_ROWS * count)
        down = dot(hidden_ref[down_rows], down_grad)
        half = DOWN_ROWS // 2
        for d in range(count):
            own = down[DOWN_ROWS * d : DOWN_ROWS * (d + 1)]
            for i in range(4):
                stage[d, DOWN_ROWS * i : DOWN_ROWS * (i + 1)] = own[:, i * LANES : (i + 1) * LANES]
            stage[d, TAIL_ROW:WIDE_ROW] = jnp.concatenate(
                [own[:half, 4 * LANES :], own[half:, 4 * LANES :]], axis=1
            )
        out_ref[pl.ds(step * count, count), :GAIN_ROW] = stage[...].astype(BF16)
        return carry

    lax.fori_loop(0, 64 // count, body, 0)

    shape = (64 * 16, D)
    row = lax.broadcasted_iota(jnp.int32, shape, 0)
    first, second = gain_masks(0, 64, 16)
    chosen = jnp.where(first, attn_gain_grad, 0.0) + jnp.where(second, mlp_gain_grad, 0.0)
    gathered = dot_nt(chosen.astype(BF16), lane_spread())
    out_ref[:, GAIN_ROW:] = gathered.astype(BF16).reshape(64, 16, LANES)


GRAD_SCRATCH = [
    pltpu.VMEM((3, D, ROWS), BF16),
    pltpu.VMEM((FF, ROWS), BF16),
    pltpu.VMEM((GRAD_DEVICES, GAIN_ROW, LANES), F32),
]


COLUMNS = {
    "qk": (0, GATE_AT),
    "gate": (GATE_AT, FF),
    "up": (UP_AT, FF),
    "out": (OUT_AT, D + KVD),
    "tail": (TAIL_AT, HEAD + KVD),
}
PROJECTION = ("qk", "tail")
REST = ("out", "gate", "up", "down")


def weight_scratch(*names):
    shapes = [(FF, D) if name == "down" else (D, COLUMNS[name][1]) for name in names]
    return [pltpu.VMEM(shape, BF16) for shape in shapes] + [pltpu.SemaphoreType.DMA((len(names),))]


class Weights:
    def __init__(self, wide_ref, down_ref, layer, names, scratch):
        *buffers, sems = scratch
        self.copies = {}
        self.buffers = dict(zip(names, buffers))
        for i, name in enumerate(names):
            if name == "down":
                source = down_ref.at[layer]
            else:
                first, width = COLUMNS[name]
                source = wide_ref.at[layer, :, pl.ds(first, width)]
            self.copies[name] = pltpu.make_async_copy(source, buffers[i], sems.at[i])
            self.copies[name].start()

    def get(self, name):
        if name in self.copies:
            self.copies.pop(name).wait()
        return self.buffers[name][...]

    def out(self):
        return self.get("out")[:, :D]


def like(shape, dtype):
    return jax.ShapeDtypeStruct(shape, dtype)


def start_kernel(
    x_ref, gains_ref, wide_ref, cos_ref, sin_ref, normed_ref, query_ref, joined_ref, *scratch
):
    project(
        x_ref[...].astype(F32),
        gains_ref[0, 0:1],
        Weights(wide_ref, None, 0, PROJECTION, scratch),
        cos_ref[...],
        sin_ref[...],
        normed_ref,
        query_ref,
        joined_ref,
    )


def middle_kernel(
    x_ref,
    gains_ref,
    wide_ref,
    down_ref,
    cos_ref,
    sin_ref,
    query_ref,
    keys_ref,
    own_seg_ref,
    seg_ref,
    probs_ref,
    attended_ref,
    midway_ref,
    normed_two_ref,
    gate_ref,
    up_ref,
    hidden_ref,
    next_x_ref,
    normed_ref,
    next_query_ref,
    joined_ref,
    *scratch,
):
    own = Weights(wide_ref, down_ref, 0, REST, scratch[:5])
    later = Weights(wide_ref, None, 1, PROJECTION, scratch[5:])
    attended = attend(query_ref, keys_ref, own_seg_ref, seg_ref, probs_ref)
    attended_ref[...] = attended
    midway, scale, normed_two, gate, up, hidden, result = feed_forward(
        x_ref[...].astype(F32), attended, gains_ref[0, 1:2], own
    )
    midway_ref[...] = midway
    normed_two_ref[...] = normed_two
    gate_ref[...] = gate
    up_ref[...] = up
    hidden_ref[...] = hidden
    passed = result.astype(BF16)
    next_x_ref[...] = passed
    project(
        passed.astype(F32),
        gains_ref[1, 0:1],
        later,
        cos_ref[...],
        sin_ref[...],
        normed_ref,
        next_query_ref,
        joined_ref,
    )


def turn_kernel(
    x_ref,
    cotangent_ref,
    gains_ref,
    wide_ref,
    down_ref,
    query_ref,
    keys_ref,
    own_seg_ref,
    seg_ref,
    result_ref,
    attended_ref,
    normed_two_ref,
    hidden_ref,
    gate_grad_ref,
    up_grad_ref,
    gain_grad_ref,
    midway_grad_ref,
    out_grad_ref,
    query_grad_ref,
    parts_ref,
    probs,
    *scratch,
):
    own = Weights(wide_ref, down_ref, 1, REST, scratch)
    attended = attend(query_ref, keys_ref, own_seg_ref, seg_ref, probs)
    attended_ref[...] = attended
    gain = gains_ref[1, 1:2]
    midway, scale, normed_two, gate, up, hidden, result = feed_forward(
        x_ref[...].astype(F32), attended, gain, own
    )
    result_ref[...] = result
    normed_two_ref[...] = normed_two
    hidden_ref[...] = hidden
    down_grad, gate_grad, up_grad, gain_grad, midway_grad, out_grad, mixed_grad = feed_forward_back(
        cotangent_ref[...].astype(F32),
        midway,
        gate,
        up,
        gain,
        own,
    )
    gate_grad_ref[...] = gate_grad
    up_grad_ref[...] = up_grad
    gain_grad_ref[...] = gain_grad
    midway_grad_ref[...] = midway_grad
    out_grad_ref[...] = out_grad
    query_grad_ref[...] = attend_back(mixed_grad, attended, query_ref, keys_ref, probs, parts_ref)


def back_kernel(
    key_grads_ref,
    query_grad_ref,
    midway_grad_ref,
    x_ref,
    gains_ref,
    cos_ref,
    sin_ref,
    wide_ref,
    down_ref,
    midway_ref,
    gate_ref,
    up_ref,
    attended_ref,
    query_ref,
    keys_ref,
    probs_ref,
    turned_ref,
    values_ref,
    attn_gain_grad_ref,
    down_grad_ref,
    gate_grad_ref,
    up_grad_ref,
    mlp_gain_grad_ref,
    lower_midway_grad_ref,
    out_grad_ref,
    lower_query_grad_ref,
    parts_ref,
    *scratch,
):
    own = Weights(wide_ref, None, 1, PROJECTION, scratch[:3])
    lower = Weights(wide_ref, down_ref, 0, REST, scratch[3:])
    turned, values, gain_grad, grad_in = project_back(
        query_grad_ref[...],
        key_grads_ref[...],
        midway_grad_ref[...],
        x_ref[...].astype(F32),
        gains_ref[1, 0:1],
        cos_ref[...],
        sin_ref[...],
        own,
    )
    turned_ref[...] = turned
    values_ref[...] = values
    attn_gain_grad_ref[...] = gain_grad
    attended = attended_ref[...]
    down_grad, gate_grad, up_grad, gain_grad, midway_grad, out_grad, mixed_grad = feed_forward_back(
        grad_in.astype(BF16).astype(F32),
        midway_ref[...],
        gate_ref[...],
        up_ref[...],
        gains_ref[0, 1:2],
        lower,
    )
    down_grad_ref[...] = down_grad
    gate_grad_ref[...] = gate_grad
    up_grad_ref[...] = up_grad
    mlp_gain_grad_ref[...] = gain_grad
    lower_midway_grad_ref[...] = midway_grad
    out_grad_ref[...] = out_grad
    lower_query_grad_ref[...] = attend_back(
        mixed_grad, attended, query_ref, keys_ref, probs_ref, parts_ref
    )


def grads_kernel(
    normed_ref,
    turned_ref,
    values_ref,
    attended_ref,
    out_grad_ref,
    normed_two_ref,
    gate_grad_ref,
    up_grad_ref,
    hidden_ref,
    down_grad_ref,
    attn_gain_grad_ref,
    mlp_gain_grad_ref,
    out_ref,
    lhs,
    hidden_t,
    stage,
):
    weight_grads(
        normed_ref[...],
        turned_ref[...],
        values_ref[...],
        attended_ref[...],
        out_grad_ref[...],
        normed_two_ref[...],
        gate_grad_ref[...],
        up_grad_ref[...],
        hidden_ref[...],
        down_grad_ref[...],
        attn_gain_grad_ref[...],
        mlp_gain_grad_ref[...],
        out_ref,
        lhs,
        hidden_t,
        stage,
    )


def end_kernel(
    key_grads_ref,
    query_grad_ref,
    midway_grad_ref,
    x_ref,
    gains_ref,
    cos_ref,
    sin_ref,
    wide_ref,
    grad_in_ref,
    turned_ref,
    values_ref,
    gain_grad_ref,
    *scratch,
):
    own = Weights(wide_ref, None, 0, PROJECTION, scratch)
    turned, values, gain_grad, grad_in = project_back(
        query_grad_ref[...],
        key_grads_ref[...],
        midway_grad_ref[...],
        x_ref[...].astype(F32),
        gains_ref[0, 0:1],
        cos_ref[...],
        sin_ref[...],
        own,
    )
    grad_in_ref[...] = grad_in
    turned_ref[...] = turned
    values_ref[...] = values
    gain_grad_ref[...] = gain_grad


def call(kernel, name, out_shape, *operands, scratch=(), specs=None):
    return pl.pallas_call(
        kernel,
        out_shape=out_shape,
        in_specs=[VMEM] * len(operands) if specs is None else specs,
        out_specs=jax.tree.map(lambda _: VMEM, out_shape),
        scratch_shapes=list(scratch),
        compiler_params=params(),
        name=name,
    )(*operands)


def rope_tables(first):
    places = first + jnp.arange(ROWS, dtype=jnp.int32)
    pair_index = jnp.arange(HEAD // 2).astype(F32)
    frequency = rope_base ** (-2.0 * pair_index / HEAD)
    angles = places.astype(F32)[:, None] * frequency[None, :]
    cos, sin = jnp.cos(angles), jnp.sin(angles)
    return jnp.concatenate([cos] * 4, axis=1), jnp.concatenate([-sin, sin] * 2, axis=1)


def local(block_input, cotangent, segment_ids, *shards):
    section = lax.axis_index("section")
    ctx = lax.axis_index("ctx")
    x = lax.dynamic_index_in_dim(block_input[:, 0], section, 0, keepdims=False)
    late = lax.dynamic_index_in_dim(cotangent[:, 0], section, 0, keepdims=False)
    seg_row = lax.dynamic_index_in_dim(segment_ids[:, 0], section, 0)
    own_seg = lax.dynamic_slice_in_dim(seg_row, ctx * ROWS, ROWS, 1).reshape(ROWS, 1)
    cos, sin = rope_tables(ctx * ROWS)

    gathered = gather_weights(pack_shards(shards))
    wide, down, gains = unpack_weights(gathered)

    whole = like((ROWS, D), F32)
    half = like((ROWS, D), BF16)
    keys_shape = like((ROWS, 2 * KVD), BF16)
    hidden_shape = like((ROWS, FF), BF16)
    acts = like((ROWS, FF), F32)
    probs_shape = (KV_HEADS, GROUP * ROWS, SEQ)
    turned_shape = like((ROWS, D + KVD), BF16)
    values_shape = like((ROWS, KVD), BF16)
    row_shape = like((1, D), F32)
    parts_shape = like((8, 2 * KVD, ROWS), BF16)

    first_part = weight_scratch(*PROJECTION)
    second_part = weight_scratch(*REST)

    normed_1, query_1, joined_1 = call(
        start_kernel,
        "start",
        (half, half, keys_shape),
        x,
        gains,
        wide,
        cos,
        sin,
        specs=[VMEM, VMEM, ANY, VMEM, VMEM],
        scratch=first_part,
    )
    keys_1 = gather_keys(joined_1, 2)
    (
        probs_1,
        attended_1,
        midway_1,
        normed_two_1,
        gate_1,
        up_1,
        hidden_1,
        x_2,
        normed_2,
        query_2,
        joined_2,
    ) = call(
        middle_kernel,
        "middle",
        (
            like(probs_shape, BF16),
            half,
            whole,
            half,
            acts,
            acts,
            hidden_shape,
            half,
            half,
            half,
            keys_shape,
        ),
        x,
        gains,
        wide,
        down,
        cos,
        sin,
        query_1,
        keys_1,
        own_seg,
        seg_row,
        specs=[VMEM] * 2 + [ANY] * 2 + [VMEM] * 6,
        scratch=second_part + first_part,
    )
    keys_2 = gather_keys(joined_2, 3)
    (
        result,
        attended_2,
        normed_two_2,
        hidden_2,
        gate_grad_2,
        up_grad_2,
        mlp_gain_grad_2,
        midway_grad_2,
        out_grad_2,
        query_grad_2,
        parts_2,
    ) = call(
        turn_kernel,
        "turn",
        (
            whole,
            half,
            half,
            hidden_shape,
            hidden_shape,
            hidden_shape,
            row_shape,
            whole,
            half,
            whole,
            parts_shape,
        ),
        x_2,
        late,
        gains,
        wide,
        down,
        query_2,
        keys_2,
        own_seg,
        seg_row,
        scratch=[pltpu.VMEM(probs_shape, BF16)] + second_part,
        specs=[VMEM] * 3 + [ANY] * 2 + [VMEM] * 4,
    )
    key_grads_2 = scatter_key_grads(parts_2, 4)
    (
        turned_2,
        values_2,
        attn_gain_grad_2,
        down_grad_1,
        gate_grad_1,
        up_grad_1,
        mlp_gain_grad_1,
        midway_grad_1,
        out_grad_1,
        query_grad_1,
        parts_1,
    ) = call(
        back_kernel,
        "back",
        (
            turned_shape,
            values_shape,
            row_shape,
            half,
            hidden_shape,
            hidden_shape,
            row_shape,
            whole,
            half,
            whole,
            parts_shape,
        ),
        key_grads_2,
        query_grad_2,
        midway_grad_2,
        x_2,
        gains,
        cos,
        sin,
        wide,
        down,
        midway_1,
        gate_1,
        up_1,
        attended_1,
        query_1,
        keys_1,
        probs_1,
        specs=[VMEM] * 7 + [ANY] * 2 + [VMEM] * 7,
        scratch=first_part + second_part,
    )
    grads_shape = like((64, PACKED, LANES), BF16)
    grads_2 = call(
        grads_kernel,
        "grads",
        grads_shape,
        normed_2,
        turned_2,
        values_2,
        attended_2,
        out_grad_2,
        normed_two_2,
        gate_grad_2,
        up_grad_2,
        hidden_2,
        late,
        attn_gain_grad_2,
        mlp_gain_grad_2,
        scratch=GRAD_SCRATCH,
    )
    key_grads_1 = scatter_key_grads(parts_1, 5)
    grad_in, turned_1, values_1, attn_gain_grad_1 = call(
        end_kernel,
        "end",
        (whole, turned_shape, values_shape, row_shape),
        key_grads_1,
        query_grad_1,
        midway_grad_1,
        x,
        gains,
        cos,
        sin,
        wide,
        specs=[VMEM] * 7 + [ANY],
        scratch=first_part,
    )
    grads_1 = call(
        grads_kernel,
        "grads",
        grads_shape,
        normed_1,
        turned_1,
        values_1,
        attended_1,
        out_grad_1,
        normed_two_1,
        gate_grad_1,
        up_grad_1,
        hidden_1,
        down_grad_1,
        attn_gain_grad_1,
        mlp_gain_grad_1,
        scratch=GRAD_SCRATCH,
    )
    by_device = (4, 2, 2, 4, PACKED, LANES)
    leaving = jnp.where(section == 0, result, grad_in)
    staying = jnp.where(section == 0, grad_in, result)
    packed, came = scatter_grads(
        grads_1.reshape(by_device), grads_2.reshape(by_device), leaving
    )
    return finish(packed, staying, came)


def solution(mesh):
    shard = P("section", ("ctx", "fsdp"))
    matrix = P("section", ("ctx", "fsdp"), None)
    return jax.shard_map(
        local,
        mesh=mesh,
        in_specs=(
            P(None, "fsdp", "ctx", None),
            P(None, "fsdp", "ctx", None),
            P(None, "fsdp", None),
            shard,
            matrix,
            matrix,
            matrix,
            matrix,
            matrix,
            matrix,
            matrix,
            shard,
        ),
        out_specs=(
            P("section", None, "fsdp", "ctx", None),
            shard,
            matrix,
            matrix,
            matrix,
            matrix,
            matrix,
            matrix,
            matrix,
            shard,
        ),
        check_vma=False,
    )
```

```python
import functools

import jax
import jax.numpy as jnp
from jax import lax
from jax.experimental import pallas as pl
from jax.experimental.pallas import tpu as pltpu
from jax.sharding import PartitionSpec as P

MESH = pl.DeviceIdType.MESH
F32 = jnp.float32
BF16 = jnp.bfloat16
ANY = pl.BlockSpec(memory_space=pl.ANY)
VMEM = pl.BlockSpec(memory_space=pltpu.VMEM)

D = 576
FF = 1536
KVD = 192
HEAD = 64
GROUP = 3
KV_HEADS = 3
ROWS = 128
SEQ = 1024
LANES = 128

norm_eps = 1e-05
rope_base = 100000.0
masked_score = -1e30

WIDE = 4608
GATE_AT = 768
UP_AT = GATE_AT + FF
OUT_AT = UP_AT + FF
VALUE_AT = OUT_AT + D
TAIL_AT = VALUE_AT - HEAD
BLOCKS = WIDE // LANES

DOWN_ROWS = 24
TAIL_ROW = 4 * DOWN_ROWS
WIDE_ROW = TAIL_ROW + DOWN_ROWS // 2
GAIN_ROW = WIDE_ROW + 9 * BLOCKS
PACKED = GAIN_ROW + 16
THIRDS = ((0, 160), (160, 144), (304, 144))
AXIS_ORDERS = (("z", "x", "y"), ("x", "y", "z"), ("y", "z", "x"))
VMEM_BYTES = 60 * 1024 * 1024


def params(collective_id=None):
    if collective_id is None:
        return pltpu.CompilerParams(vmem_limit_bytes=VMEM_BYTES)
    return pltpu.CompilerParams(
        vmem_limit_bytes=VMEM_BYTES, collective_id=collective_id, has_side_effects=True
    )


def dot(left, right):
    return jnp.dot(left, right, preferred_element_type=F32)


def dot_nt(left, right):
    return lax.dot_general(left, right, (((1,), (1,)), ((), ())), preferred_element_type=F32)


def dot_tn(left, right):
    return lax.dot_general(left, right, (((0,), (0,)), ((), ())), preferred_element_type=F32)


class Place:
    def __init__(self):
        self.section = lax.axis_index("section")
        ctx = lax.axis_index("ctx")
        fsdp = lax.axis_index("fsdp")
        self.core = lax.rem(ctx, 2)
        self.at = {
            "x": lax.rem(fsdp, 4),
            "y": ctx // 2,
            "z": self.section * 2 + fsdp // 4,
        }

    def device(self, core=None, **moved):
        at = dict(self.at, **moved)
        core = self.core if core is None else core
        return (at["z"] // 2, at["y"] * 2 + core, lax.rem(at["z"], 2) * 4 + at["x"])

    def shifted(self, axis, step):
        return lax.rem(self.at[axis] + step + 4, 4)

    def neighbour(self, axis, step):
        return self.device(**{axis: self.shifted(axis, step)})

    def partner(self):
        return self.device(core=1 - self.core)


def greet(devices):
    barrier = pltpu.get_barrier_semaphore()
    for device in devices:
        pl.semaphore_signal(barrier, inc=1, device_id=device, device_id_type=MESH)
    pl.semaphore_wait(barrier, len(devices))


def torus_neighbours(place):
    return [place.neighbour(axis, step) for axis in "xyz" for step in (1, -1)]


def region(ref, coords, whole, rows, core):
    first, count = rows
    z_hi = slice(None) if "z" in whole else coords["z"] // 2
    z_lo = slice(None) if "z" in whole else lax.rem(coords["z"], 2)
    y = slice(None) if "y" in whole else coords["y"]
    x = slice(None) if "x" in whole else coords["x"]
    if core is None:
        return ref.at[z_hi, y, z_lo, x, pl.ds(first, count)]
    return ref.at[z_hi, y, core, z_lo, x, pl.ds(first, count)]


def halves(rows):
    first, count = rows
    upper = (count // 2 + 15) // 16 * 16
    return (first, upper), (first + upper, count - upper)


def gather_kernel(mine_ref, out_ref, local_sem, send_sems, recv_sems):
    place = Place()
    core = place.core
    greet(torus_neighbours(place) + [place.partner()])

    own = out_ref.at[place.section, place.at["y"], core, lax.rem(place.at["z"], 2), place.at["x"]]
    seed = pltpu.make_async_copy(mine_ref, own, local_sem)
    seed.start()
    seed.wait()

    counter = [0]
    unsent = []

    def send(ref, device):
        slot = counter[0]
        counter[0] += 1
        copy = pltpu.make_async_remote_copy(
            src_ref=ref,
            dst_ref=ref,
            send_sem=send_sems.at[slot],
            recv_sem=recv_sems.at[slot],
            device_id=device,
            device_id_type=MESH,
        )
        copy.start()
        unsent.append(copy)
        return copy

    to_partner = []
    for phase in range(3):
        arriving = []
        for third, rows in enumerate(THIRDS):
            axis = AXIS_ORDERS[third][phase]
            whole = AXIS_ORDERS[third][:phase]
            block = region(out_ref, place.at, whole, rows, core)
            arriving.append(
                [send(block, place.neighbour(axis, 1)), send(block, place.neighbour(axis, -1))]
            )
            if phase == 2:
                to_partner.append(send(block, place.partner()))
        second = []
        for third, rows in enumerate(THIRDS):
            axis = AXIS_ORDERS[third][phase]
            whole = AXIS_ORDERS[third][:phase]
            for copy in arriving[third]:
                copy.wait_recv()
            upper, lower = halves(rows)
            left = dict(place.at, **{axis: place.shifted(axis, -1)})
            right = dict(place.at, **{axis: place.shifted(axis, 1)})
            second.append(
                [
                    send(region(out_ref, left, whole, upper, core), place.neighbour(axis, 1)),
                    send(region(out_ref, right, whole, lower, core), place.neighbour(axis, -1)),
                ]
            )
            if phase == 2:
                for coords in (left, right):
                    to_partner.append(
                        send(region(out_ref, coords, whole, rows, core), place.partner())
                    )
        for third, rows in enumerate(THIRDS):
            axis = AXIS_ORDERS[third][phase]
            whole = AXIS_ORDERS[third][:phase]
            for copy in second[third]:
                copy.wait_recv()
            if phase == 2:
                far = dict(place.at, **{axis: place.shifted(axis, 2)})
                to_partner.append(send(region(out_ref, far, whole, rows, core), place.partner()))
    for copy in to_partner:
        copy.wait_recv()
    for copy in unsent:
        copy.wait_send()


def gather_weights(packed):
    slots = 3 * 3 * 4 + 3 * 4
    return pl.pallas_call(
        gather_kernel,
        out_shape=jax.ShapeDtypeStruct((2, 4, 2, 2, 4, PACKED, LANES), BF16),
        in_specs=[ANY],
        out_specs=ANY,
        scratch_shapes=[
            pltpu.SemaphoreType.DMA,
            pltpu.SemaphoreType.DMA((slots,)),
            pltpu.SemaphoreType.DMA((slots,)),
        ],
        compiler_params=params(0),
        name="gather_weights",
    )(packed)


def scatter_kernel(
    first_ref,
    second_ref,
    edge_ref,
    out_ref,
    edge_out_ref,
    total,
    swapped,
    arrivals_0,
    arrivals_1,
    arrivals_2,
    local_sems,
    swap_send,
    swap_recv,
    send_sems,
    recv_sems,
    edge_send,
    edge_recv,
):
    place = Place()
    core = place.core
    across = (1 - place.section, lax.axis_index("ctx"), lax.axis_index("fsdp"))
    greet(torus_neighbours(place) + [place.partner(), across])

    swaps = []
    loads = []
    for third, (first, count) in enumerate(THIRDS):
        rows = pl.ds(first, count)
        for layer, part_ref in enumerate((first_ref, second_ref)):
            slot = third * 2 + layer
            swap = pltpu.make_async_remote_copy(
                src_ref=part_ref.at[:, 1 - core, :, :, rows],
                dst_ref=swapped.at[layer, :, :, :, rows],
                send_sem=swap_send.at[slot],
                recv_sem=swap_recv.at[slot],
                device_id=place.partner(),
                device_id_type=MESH,
            )
            swap.start()
            load = pltpu.make_async_copy(
                part_ref.at[:, core, :, :, rows],
                total.at[layer, :, :, :, rows],
                local_sems.at[slot],
            )
            load.start()
            swaps.append(swap)
            loads.append(load)
    edge = pltpu.make_async_remote_copy(
        src_ref=edge_ref,
        dst_ref=edge_out_ref,
        send_sem=edge_send,
        recv_sem=edge_recv,
        device_id=across,
        device_id_type=MESH,
    )
    edge.start()

    counter = [0]
    unsent = []

    def send(source, target, device):
        slot = counter[0]
        counter[0] += 1
        copy = pltpu.make_async_remote_copy(
            src_ref=source,
            dst_ref=target,
            send_sem=send_sems.at[slot],
            recv_sem=recv_sems.at[slot],
            device_id=device,
            device_id_type=MESH,
        )
        copy.start()
        unsent.append(copy)
        return copy

    def add(coords, whole, rows, source, first=0):
        at, count = rows
        sizes = [4 if axis in whole else 1 for axis in "zyx"]

        def body(step, carry):
            z = step // (sizes[1] * sizes[2])
            y = lax.rem(step // sizes[2], sizes[1])
            x = lax.rem(step, sizes[2])
            spot = (
                z if "z" in whole else coords["z"],
                y if "y" in whole else coords["y"],
                x if "x" in whole else coords["x"],
            )
            here = (spot[0] // 2, spot[1], lax.rem(spot[0], 2), spot[2], pl.ds(at, count))
            total[here] = (
                total[here].astype(F32) + source(z, y, x, first, count).astype(F32)
            ).astype(BF16)
            return carry

        lax.fori_loop(0, sizes[0] * sizes[1] * sizes[2], body, 0)

    def swapped_part(rows):
        def load(z, y, x, first, count):
            return swapped[z // 2, y, lax.rem(z, 2), x, pl.ds(rows[0], count)]

        return load

    arrivals = (arrivals_0, arrivals_1, arrivals_2)
    used = [0, 0, 0]

    def ring(third, phase, step):
        rows = THIRDS[third]
        order = AXIS_ORDERS[third][::-1]
        axis = order[phase]
        whole = order[phase + 1 :]
        upper, lower = halves(rows)
        right = dict(place.at, **{axis: place.shifted(axis, 1)})
        left = dict(place.at, **{axis: place.shifted(axis, -1)})
        far = dict(place.at, **{axis: place.shifted(axis, 2)})
        if step == 0:
            plan = ((far, upper, 1, right), (far, lower, -1, left))
        else:
            plan = ((right, rows, 1, place.at), (left, rows, -1, place.at))
        started = []
        for source_at, part, way, lands in plan:
            device = place.neighbour(axis, way)
            first = used[third]
            used[third] += 1
            copy = send(
                region(total, source_at, whole, part, None),
                landing(third, first, whole, part[1]),
                device,
            )
            started.append((copy, lands, part, first, whole))
        return started

    def landing(third, slot, whole, count):
        z_hi = slice(None) if "z" in whole else 0
        z_lo = slice(None) if "z" in whole else 0
        y = slice(None) if "y" in whole else 0
        x = slice(None) if "x" in whole else 0
        return arrivals[third].at[slot, z_hi, y, z_lo, x, pl.ds(0, count)]

    def arrived_part(third, slot):
        def load(z, y, x, first, count):
            return arrivals[third][slot, z // 2, y, lax.rem(z, 2), x, pl.ds(0, count)]

        return load

    def finish(third, started):
        for copy, lands, part, slot, whole in started:
            copy.wait()
            add(lands, whole, part, arrived_part(third, slot))

    flights = []
    for third, rows in enumerate(THIRDS):
        for layer in range(2):
            loads[third * 2 + layer].wait()
            swaps[third * 2 + layer].wait()
        add(place.at, ("z", "y", "x"), rows, swapped_part(rows))
        flights.append(ring(third, 0, 0))
    for phase in range(3):
        for step in range(2):
            for third in range(3):
                finish(third, flights[third])
                if step == 0:
                    flights[third] = ring(third, phase, 1)
                elif phase < 2:
                    flights[third] = ring(third, phase + 1, 0)

    z, y, x = place.at["z"], place.at["y"], place.at["x"]
    out_ref[...] = total[z // 2, y, lax.rem(z, 2), x].astype(F32)
    edge.wait()


def scatter_grads(first, second, edge):
    slots = 3 * 3 * 4
    return pl.pallas_call(
        scatter_kernel,
        out_shape=(
            jax.ShapeDtypeStruct((PACKED, LANES), F32),
            jax.ShapeDtypeStruct((D, ROWS), F32),
        ),
        in_specs=[ANY, ANY, VMEM],
        out_specs=(VMEM, VMEM),
        scratch_shapes=[
            pltpu.VMEM((2, 4, 2, 4, PACKED, LANES), BF16),
            pltpu.VMEM((2, 4, 2, 4, PACKED, LANES), BF16),
            pltpu.VMEM((12, 2, 1, 2, 4, 160, LANES), BF16),
            pltpu.VMEM((12, 1, 4, 1, 4, 144, LANES), BF16),
            pltpu.VMEM((12, 2, 4, 2, 1, 144, LANES), BF16),
            pltpu.SemaphoreType.DMA((6,)),
            pltpu.SemaphoreType.DMA((6,)),
            pltpu.SemaphoreType.DMA((6,)),
            pltpu.SemaphoreType.DMA((slots,)),
            pltpu.SemaphoreType.DMA((slots,)),
            pltpu.SemaphoreType.DMA,
            pltpu.SemaphoreType.DMA,
        ],
        compiler_params=params(1),
        name="scatter_grads",
    )(first, second, edge)


class Exchange:
    def __init__(self, place, send_sems, recv_sems):
        self.place = place
        self.send_sems = send_sems
        self.recv_sems = recv_sems

    def copy(self, slot, source, target, device):
        return pltpu.make_async_remote_copy(
            src_ref=source,
            dst_ref=target,
            send_sem=self.send_sems.at[slot],
            recv_sem=self.recv_sems.at[slot],
            device_id=device,
            device_id_type=MESH,
        )

    def along_y(self, step):
        return self.place.device(y=lax.rem(self.place.at["y"] + step + 4, 4))


class KeyGather(Exchange):
    def __init__(self, place, keys_ref, send_sems, recv_sems):
        super().__init__(place, send_sems, recv_sems)
        self.keys_ref = keys_ref

    def direct(self, away):
        own = self.keys_ref.at[self.place.at["y"] * 2 + self.place.core]
        return self.copy(away, own, own, self.along_y(away))

    def passed_on(self, away):
        block = self.keys_ref.at[
            lax.rem(self.place.at["y"] - away + 4, 4) * 2 + self.place.core
        ]
        return self.copy(4 + away, block, block, self.place.partner())

    def start(self):
        y = self.place.at["y"]
        for away in (1, 3, 2):

            @pl.when(y + away < 4)
            def _():
                self.direct(away).start()

        self.passed_on(0).start()
        for away in range(1, 4):

            @pl.when(y + away < 4)
            def _():
                self.keys_ref[pl.ds((y + away) * 2, 2)] = jnp.zeros(
                    (2,) + self.keys_ref.shape[1:], self.keys_ref.dtype
                )

    def finish(self):
        y = self.place.at["y"]
        for away in range(1, 4):

            @pl.when(y - away >= 0)
            def _():
                self.direct(away).wait_recv()
                self.passed_on(away).start()

        self.passed_on(0).wait()
        for away in range(1, 4):

            @pl.when(y - away >= 0)
            def _():
                self.passed_on(away).wait()

            @pl.when(y + away < 4)
            def _():
                self.direct(away).wait_send()


class KeyGradSum(Exchange):
    def __init__(self, place, parts_ref, pair_ref, ring_ref, send_sems, recv_sems):
        super().__init__(place, send_sems, recv_sems)
        self.parts_ref = parts_ref
        self.pair_ref = pair_ref
        self.ring_ref = ring_ref

    def swap(self):
        return self.copy(
            0, self.parts_ref.at[1 - self.place.core], self.pair_ref, self.place.partner()
        )

    def direct(self, away):
        y = lax.rem(self.place.at["y"] - away + 4, 4)
        return self.copy(
            away,
            self.parts_ref.at[self.place.core, y],
            self.ring_ref.at[away],
            self.along_y(-away),
        )

    def start(self):
        self.swap().start()

    def middle(self):
        self.swap().wait()
        core = self.place.core
        for y in range(4):
            self.parts_ref[core, y] = (
                self.parts_ref[core, y].astype(F32) + self.pair_ref[y].astype(F32)
            ).astype(BF16)
        for away in (1, 3, 2):

            @pl.when(self.place.at["y"] - away >= 0)
            def _():
                self.direct(away).start()

    def finish(self, out_ref):
        y = self.place.at["y"]
        out_ref[...] = self.parts_ref[self.place.core, y].astype(F32)
        for away in range(1, 4):

            @pl.when(y + away < 4)
            def _():
                self.direct(away).wait_recv()
                out_ref[...] += self.ring_ref[away].astype(F32)

        for away in range(1, 4):

            @pl.when(y - away >= 0)
            def _():
                self.direct(away).wait_send()


def pack_kernel(
    attn_ref, query_ref, key_ref, value_ref, w_out_ref, gate_ref, up_ref, down_ref, mlp_ref, out_ref
):
    def wide(ref):
        return ref[0].astype(F32)

    joined = jnp.concatenate(
        [wide(r) for r in (query_ref, key_ref, gate_ref, up_ref, w_out_ref, value_ref)], axis=1
    )
    down = wide(down_ref)
    pieces = [down[:, i * LANES : (i + 1) * LANES] for i in range(4)]
    half = DOWN_ROWS // 2
    pieces.append(jnp.concatenate([down[:half, 4 * LANES :], down[half:, 4 * LANES :]], axis=1))
    pieces += [joined[:, i * LANES : (i + 1) * LANES] for i in range(BLOCKS)]
    for ref in (attn_ref, mlp_ref):
        gain = ref[...].astype(F32)
        pieces.append(jnp.concatenate([gain, jnp.zeros((1, LANES - 9), F32)], axis=1))
    pieces.append(jnp.zeros((14, LANES), F32))
    out_ref[...] = jnp.concatenate(pieces, axis=0).astype(BF16)


def pack_shards(shards):
    return pl.pallas_call(
        pack_kernel,
        out_shape=jax.ShapeDtypeStruct((PACKED, LANES), BF16),
        in_specs=[VMEM] * 9,
        out_specs=VMEM,
        compiler_params=params(),
        name="pack_shards",
    )(*shards)


def gain_masks(first_device, devices, rows_each):
    shape = (devices * rows_each, D)
    row = lax.broadcasted_iota(jnp.int32, shape, 0)
    owner = lax.broadcasted_iota(jnp.int32, shape, 1) // 9
    same = owner == first_device + row // rows_each
    place = lax.rem(row, rows_each)
    return same & (place == 0), same & (place == 1)


def lane_spread():
    lane = lax.broadcasted_iota(jnp.int32, (LANES, D), 0)
    feature = lax.broadcasted_iota(jnp.int32, (LANES, D), 1)
    return (lane == lax.rem(feature, 9)).astype(BF16)


def unpack_kernel(packed_ref, wide_ref, down_ref, gains_ref):
    block = pl.program_id(1)
    count = packed_ref.shape[0]
    held = [packed_ref[i].astype(F32) for i in range(count)]
    for column in range(BLOCKS):
        at = WIDE_ROW + 9 * column
        wide_ref[0, :, column * LANES : (column + 1) * LANES] = jnp.concatenate(
            [h[at : at + 9] for h in held], axis=0
        ).astype(BF16)
    for column in range(4):
        at = DOWN_ROWS * column
        down_ref[0, :, column * LANES : (column + 1) * LANES] = jnp.concatenate(
            [h[at : at + DOWN_ROWS] for h in held], axis=0
        ).astype(BF16)
    tails = []
    for h in held:
        tail = h[TAIL_ROW:WIDE_ROW]
        tails += [tail[:, :HEAD], tail[:, HEAD:]]
    down_ref[0, :, 4 * LANES :] = jnp.concatenate(tails, axis=0).astype(BF16)
    rows = packed_ref[:, GAIN_ROW:, :].reshape(count * 16, LANES)
    spread = dot(rows, lane_spread())
    first, second = gain_masks(block * count, count, 16)
    gains = [
        jnp.sum(jnp.where(mask, spread, 0.0), axis=0, keepdims=True) for mask in (first, second)
    ]

    @pl.when(block == 0)
    def _():
        gains_ref[...] = jnp.zeros_like(gains_ref)

    gains_ref[0, 0:1] += gains[0]
    gains_ref[0, 1:2] += gains[1]


def unpack_weights(gathered):
    count = 16
    return pl.pallas_call(
        unpack_kernel,
        grid=(2, 4),
        out_shape=(
            jax.ShapeDtypeStruct((2, D, WIDE), BF16),
            jax.ShapeDtypeStruct((2, FF, D), BF16),
            jax.ShapeDtypeStruct((2, 8, D), F32),
        ),
        in_specs=[pl.BlockSpec((count, PACKED, LANES), lambda s, y: (s * 4 + y, 0, 0))],
        out_specs=(
            pl.BlockSpec((1, 9 * count, WIDE), lambda s, y: (s, y, 0)),
            pl.BlockSpec((1, DOWN_ROWS * count, D), lambda s, y: (s, y, 0)),
            pl.BlockSpec((1, 8, D), lambda s, y: (s, 0, 0)),
        ),
        compiler_params=params(),
        name="unpack_weights",
    )(gathered.reshape(128, PACKED, LANES))


def finish_kernel(
    packed_ref,
    kept_ref,
    came_ref,
    edges_ref,
    attn_ref,
    query_ref,
    key_ref,
    value_ref,
    w_out_ref,
    gate_ref,
    up_ref,
    down_ref,
    mlp_ref,
):
    section = lax.axis_index("section")
    edges_ref[0, section, 0] = kept_ref[...]
    edges_ref[0, 1 - section, 0] = came_ref[...]
    packed = packed_ref[...]
    joined = jnp.concatenate(
        [packed[WIDE_ROW + 9 * i : WIDE_ROW + 9 * i + 9] for i in range(BLOCKS)], axis=1
    )
    query_ref[:, 0] = joined[:, :D]
    key_ref[:, 0] = joined[:, D:GATE_AT]
    gate_ref[:, 0] = joined[:, GATE_AT:UP_AT]
    up_ref[:, 0] = joined[:, UP_AT:OUT_AT]
    w_out_ref[:, 0] = joined[:, OUT_AT:VALUE_AT]
    value_ref[:, 0] = joined[:, VALUE_AT:]
    tail = packed[TAIL_ROW:WIDE_ROW]
    down_ref[0] = jnp.concatenate(
        [packed[DOWN_ROWS * i : DOWN_ROWS * (i + 1)] for i in range(4)]
        + [jnp.concatenate([tail[:, :HEAD], tail[:, HEAD:]], axis=0)],
        axis=1,
    )
    attn_ref[...] = packed[GAIN_ROW : GAIN_ROW + 1, :9]
    mlp_ref[...] = packed[GAIN_ROW + 1 : GAIN_ROW + 2, :9]


def finish(packed, kept, came):
    shapes = (
        (1, 2, 1, D, ROWS),
        (1, 9),
        (9, 1, D),
        (9, 1, KVD),
        (9, 1, KVD),
        (9, 1, D),
        (9, 1, FF),
        (9, 1, FF),
        (1, DOWN_ROWS, D),
        (1, 9),
    )
    edges, attn, *wide, down, mlp = pl.pallas_call(
        finish_kernel,
        out_shape=tuple(jax.ShapeDtypeStruct(shape, F32) for shape in shapes),
        in_specs=[VMEM] * 3,
        out_specs=(VMEM,) * len(shapes),
        compiler_params=params(),
        name="finish",
    )(packed, kept, came)
    wide = [grad.transpose(1, 0, 2) for grad in wide]
    return (edges.transpose(0, 1, 2, 4, 3), attn, *wide, down, mlp)


def swap_halves(block):
    lane = lax.broadcasted_iota(jnp.int32, block.shape, 1)
    return jnp.where(
        lax.rem(lane, HEAD) < HEAD // 2,
        pltpu.roll(block, LANES - HEAD // 2, 1),
        pltpu.roll(block, HEAD // 2, 1),
    )


def rotated(block, cos, sin):
    return block * cos + swap_halves(block) * sin


def project(current, gain, weights, cos, sin, normed_ref, query_ref):
    scale = lax.rsqrt(jnp.mean(current * current, axis=1, keepdims=True) + norm_eps)
    normed = (current * scale * gain).astype(BF16)
    normed_ref[...] = normed
    raw = dot(normed, weights.get("qk"))
    turned = [
        rotated(raw[:, i * LANES : (i + 1) * LANES], cos, sin).astype(BF16) for i in range(6)
    ]
    for i in range(4):
        query_ref[:, i * LANES : (i + 1) * LANES] = turned[i]
    query_ref[:, 4 * LANES :] = turned[4][:, :HEAD]
    values = dot(normed, weights.get("tail"))[:, HEAD:]
    return jnp.concatenate(
        [turned[4][:, HEAD:].astype(F32), turned[5].astype(F32), values], axis=1
    ).astype(BF16)


def heads_of(rows, group):
    return jnp.concatenate(
        [rows[:, (group * GROUP + r) * HEAD : (group * GROUP + r + 1) * HEAD] for r in range(GROUP)],
        axis=0,
    )


def attend(query_ref, keys_ref, own_seg_ref, seg_ref, probs_ref):
    first = lax.axis_index("ctx") * ROWS
    rows = first + lax.broadcasted_iota(jnp.int32, (ROWS, SEQ), 0)
    columns = lax.broadcasted_iota(jnp.int32, (ROWS, SEQ), 1)
    allowed = (columns <= rows) & (seg_ref[...] == own_seg_ref[...])
    bias = jnp.where(allowed, 0.0, masked_score)
    bias = jnp.concatenate([bias] * GROUP, axis=0)
    queries = query_ref[...]
    mixed = []
    for group in range(KV_HEADS):
        keys = keys_ref[:, :, group * HEAD : (group + 1) * HEAD].reshape(SEQ, HEAD)
        values = keys_ref[:, :, KVD + group * HEAD : KVD + (group + 1) * HEAD].reshape(SEQ, HEAD)
        scores = dot_nt(heads_of(queries, group), keys) * HEAD**-0.5 + bias
        shifted = jnp.exp(scores - jnp.max(scores, axis=1, keepdims=True))
        probs = (shifted / jnp.sum(shifted, axis=1, keepdims=True)).astype(BF16)
        probs_ref[group] = probs
        mixture = dot(probs, values)
        mixed += [mixture[r * ROWS : (r + 1) * ROWS] for r in range(GROUP)]
    return jnp.concatenate(mixed, axis=1).astype(BF16)


def feed_forward(current, attended, gain, weights):
    midway = current + dot(attended, weights.out())
    scale = lax.rsqrt(jnp.mean(midway * midway, axis=1, keepdims=True) + norm_eps)
    normed = (midway * scale * gain).astype(BF16)
    gate = dot(normed, weights.get("gate"))
    up = dot(normed, weights.get("up"))
    hidden = (gate / (1.0 + jnp.exp(-gate)) * up).astype(BF16)
    result = midway + dot(hidden, weights.get("down"))
    return midway, scale, normed, gate, up, hidden, result


def norm_backward(scaled, values, scale):
    return scale * scaled - values * scale**3 * jnp.mean(scaled * values, axis=1, keepdims=True)


def feed_forward_back(
    incoming, midway, gate, up, gain, weights
):
    scale = lax.rsqrt(jnp.mean(midway * midway, axis=1, keepdims=True) + norm_eps)
    down_grad = incoming.astype(BF16)
    hidden_grad = dot_nt(down_grad, weights.get("down"))
    sigmoid = 1.0 / (1.0 + jnp.exp(-gate))
    gate_grad = (hidden_grad * up * sigmoid * (1.0 + gate * (1.0 - sigmoid))).astype(BF16)
    up_grad = (hidden_grad * gate * sigmoid).astype(BF16)
    normed_grad = dot_nt(gate_grad, weights.get("gate")) + dot_nt(
        up_grad, weights.get("up")
    )
    gain_grad = jnp.sum(normed_grad * midway * scale, axis=0, keepdims=True)
    midway_grad = incoming + norm_backward(normed_grad * gain, midway, scale)
    out_grad = midway_grad.astype(BF16)
    mixed_grad = dot_nt(out_grad, weights.out()).astype(BF16)
    return down_grad, gate_grad, up_grad, gain_grad, midway_grad, out_grad, mixed_grad


def attend_back(mixed_grad, attended, query_ref, keys_ref, probs_ref, parts_ref):
    queries = query_ref[...]
    query_grads = []
    for group in range(KV_HEADS):
        keys = keys_ref[:, :, group * HEAD : (group + 1) * HEAD].reshape(SEQ, HEAD)
        values = keys_ref[:, :, KVD + group * HEAD : KVD + (group + 1) * HEAD].reshape(SEQ, HEAD)
        grads = heads_of(mixed_grad, group)
        delta = jnp.sum(
            grads.astype(F32) * heads_of(attended, group).astype(F32), axis=1, keepdims=True
        )
        probs = probs_ref[group]
        score_grad = (probs.astype(F32) * (dot_nt(grads, values) - delta)).astype(BF16)
        query_grad = dot(score_grad, keys) * HEAD**-0.5
        query_grads += [query_grad[r * ROWS : (r + 1) * ROWS] for r in range(GROUP)]
        key_part = (dot_tn(heads_of(queries, group), score_grad) * HEAD**-0.5).astype(BF16)
        value_part = dot_tn(grads, probs).astype(BF16)
        for block in range(8):
            columns = slice(block * ROWS, (block + 1) * ROWS)
            at = (block % 2, block // 2)
            parts_ref[*at, group * HEAD : (group + 1) * HEAD] = key_part[:, columns]
            parts_ref[*at, KVD + group * HEAD : KVD + (group + 1) * HEAD] = value_part[:, columns]
    return jnp.concatenate(query_grads, axis=1)


def project_back(
    query_grad, key_grads, midway_grad, current, gain, cos, sin, weights
):
    key_grads = key_grads.T
    joined = jnp.concatenate([query_grad, key_grads[:, :KVD]], axis=1)
    turned = jnp.concatenate(
        [rotated(joined[:, i * LANES : (i + 1) * LANES], cos, -sin) for i in range(6)], axis=1
    ).astype(BF16)
    values = key_grads[:, KVD:].astype(BF16)
    padded = jnp.concatenate([jnp.zeros((ROWS, HEAD), F32), key_grads[:, KVD:]], axis=1)
    normed_grad = dot_nt(turned, weights.get("qk")) + dot_nt(
        padded.astype(BF16), weights.get("tail")
    )
    scale = lax.rsqrt(jnp.mean(current * current, axis=1, keepdims=True) + norm_eps)
    gain_grad = jnp.sum(normed_grad * current * scale, axis=0, keepdims=True)
    grad_in = midway_grad + norm_backward(normed_grad * gain, current, scale)
    return turned, values, gain_grad, grad_in


GRAD_DEVICES = 16


def transposed(rows):
    return rows.astype(F32).T.astype(BF16)


class WeightGrads:
    def __init__(self, stage, lhs, hidden_lhs):
        self.stage = stage
        self.lhs = lhs
        self.hidden_lhs = hidden_lhs

    def place(self, step, column, product):
        for i in range(product.shape[1] // LANES):
            at = WIDE_ROW + 9 * (column + i)
            part = product[:, i * LANES : (i + 1) * LANES]
            for d in range(GRAD_DEVICES):
                self.stage[step * GRAD_DEVICES + d, at : at + 9] = part[9 * d : 9 * d + 9]

    def prepare(self, normed, normed_two, attended, hidden):
        self.lhs[0] = transposed(normed)
        self.lhs[1] = transposed(normed_two)
        self.lhs[2] = transposed(attended)
        self.hidden_lhs[...] = transposed(hidden)

    def rows(self, step, each):
        return pl.ds(pl.multiple_of(step * each * GRAD_DEVICES, 16), each * GRAD_DEVICES)

    def rest(self, gate_grad_ref, up_grad_ref, down_grad_ref):
        half = DOWN_ROWS // 2

        def body(step, carry):
            second = self.lhs[1, self.rows(step, 9)]
            self.place(step, GATE_AT // LANES, dot(second, gate_grad_ref[...]))
            self.place(step, UP_AT // LANES, dot(second, up_grad_ref[...]))
            down = dot(self.hidden_lhs[self.rows(step, DOWN_ROWS)], down_grad_ref[...])
            for d in range(GRAD_DEVICES):
                own = down[DOWN_ROWS * d : DOWN_ROWS * (d + 1)]
                at = step * GRAD_DEVICES + d
                for i in range(4):
                    self.stage[at, DOWN_ROWS * i : DOWN_ROWS * (i + 1)] = own[
                        :, i * LANES : (i + 1) * LANES
                    ]
                self.stage[at, TAIL_ROW:WIDE_ROW] = jnp.concatenate(
                    [own[:half, 4 * LANES :], own[half:, 4 * LANES :]], axis=1
                )
            return carry

        lax.fori_loop(0, 64 // GRAD_DEVICES, body, 0)

    def projections(self, turned_ref, values_ref, out_grad_ref):
        def body(step, carry):
            first = self.lhs[0, self.rows(step, 9)]
            self.place(step, 0, dot(first, turned_ref[...]))
            third = self.lhs[2, self.rows(step, 9)]
            self.place(
                step,
                OUT_AT // LANES,
                jnp.concatenate(
                    [dot(third, out_grad_ref[...]), dot(first, values_ref[...])], axis=1
                ),
            )
            return carry

        lax.fori_loop(0, 64 // GRAD_DEVICES, body, 0)

    def round(self, packed, attn_gain_grad, mlp_gain_grad):
        def body(step, carry):
            packed[step, :GAIN_ROW] = self.stage[step].astype(BF16)
            return carry

        lax.fori_loop(0, 64, body, 0)
        first, second = gain_masks(0, 64, 16)
        chosen = jnp.where(first, attn_gain_grad, 0.0) + jnp.where(second, mlp_gain_grad, 0.0)
        gathered = dot_nt(chosen.astype(BF16), lane_spread())
        packed[:, GAIN_ROW:] = gathered.astype(BF16).reshape(64, 16, LANES)


COLUMNS = {
    "qk": (0, GATE_AT),
    "gate": (GATE_AT, FF),
    "up": (UP_AT, FF),
    "out": (OUT_AT, D + KVD),
    "tail": (TAIL_AT, HEAD + KVD),
}
PROJECTION = ("qk", "tail")
REST = ("out", "gate", "up", "down")


def weight_scratch(*names):
    shapes = [(FF, D) if name == "down" else (D, COLUMNS[name][1]) for name in names]
    return [pltpu.VMEM(shape, BF16) for shape in shapes] + [pltpu.SemaphoreType.DMA((len(names),))]


class Weights:
    def __init__(self, wide_ref, down_ref, layer, names, scratch):
        *buffers, sems = scratch
        self.copies = {}
        self.buffers = dict(zip(names, buffers))
        for i, name in enumerate(names):
            if name == "down":
                source = down_ref.at[layer]
            else:
                first, width = COLUMNS[name]
                source = wide_ref.at[layer, :, pl.ds(first, width)]
            self.copies[name] = pltpu.make_async_copy(source, buffers[i], sems.at[i])
            self.copies[name].start()

    def get(self, name):
        if name in self.copies:
            self.copies.pop(name).wait()
        return self.buffers[name][...]

    def out(self):
        return self.get("out")[:, :D]


ROW = (ROWS, D)
KEPT = {
    "joined": ((2, 8, ROWS, 2 * KVD), BF16),
    "probs": ((2, KV_HEADS, GROUP * ROWS, SEQ), BF16),
    "parts": ((2, 2, 4, 2 * KVD, ROWS), BF16),
    "pair": ((2, 4, 2 * KVD, ROWS), BF16),
    "ring": ((2, 4, 2 * KVD, ROWS), BF16),
    "key_grads": ((2 * KVD, ROWS), F32),
    "normed": ((2, *ROW), BF16),
    "query": ((2, *ROW), BF16),
    "attended": ((2, *ROW), BF16),
    "normed_two": ((2, *ROW), BF16),
    "hidden": ((2, ROWS, FF), BF16),
    "midway": (ROW, F32),
    "gate": ((ROWS, FF), F32),
    "up": ((ROWS, FF), F32),
    "x_2": (ROW, BF16),
    "gate_grad": ((2, ROWS, FF), BF16),
    "up_grad": ((2, ROWS, FF), BF16),
    "down_grad": ((2, *ROW), BF16),
    "out_grad": ((2, *ROW), BF16),
    "midway_grad": (ROW, F32),
    "query_grad": (ROW, F32),
    "turned": ((2, ROWS, D + KVD), BF16),
    "values": ((2, ROWS, KVD), BF16),
    "lhs": ((2, 3, D, ROWS), BF16),
    "hidden_lhs": ((2, FF, ROWS), BF16),
    "stage": ((64, GAIN_ROW, LANES), F32),
    "packed": ((64, PACKED, LANES), BF16),
}


def layers_kernel(
    x_ref,
    late_ref,
    gains_ref,
    wide_ref,
    down_ref,
    cos_ref,
    sin_ref,
    own_seg_ref,
    seg_ref,
    result_ref,
    grad_in_ref,
    grads_1_ref,
    grads_2_ref,
    send_sems,
    recv_sems,
    out_sems,
    *scratch,
):
    place = Place()
    kept = dict(zip(KEPT, scratch))
    scratch = scratch[len(KEPT) :]
    first_1 = Weights(wide_ref, None, 0, PROJECTION, scratch[:3])
    rest_1 = Weights(wide_ref, down_ref, 0, REST, scratch[3:8])
    first_2 = Weights(wide_ref, None, 1, PROJECTION, scratch[8:11])
    rest_2 = Weights(wide_ref, down_ref, 1, REST, scratch[11:])
    greet([place.partner()] + [place.device(y=place.shifted("y", step)) for step in (1, 2, 3)])

    cos, sin = cos_ref[...], sin_ref[...]
    mine = lax.axis_index("ctx")
    gathers = [
        KeyGather(place, kept["joined"].at[i], send_sems.at[i], recv_sems.at[i]) for i in range(2)
    ]
    sums = [
        KeyGradSum(
            place,
            kept["parts"].at[i],
            kept["pair"].at[i],
            kept["ring"].at[i],
            send_sems.at[2 + i],
            recv_sems.at[2 + i],
        )
        for i in range(2)
    ]
    grads = [
        WeightGrads(kept["stage"], kept["lhs"].at[i], kept["hidden_lhs"].at[i]) for i in range(2)
    ]

    def start_layer(layer, current, weights):
        kept["joined"][layer, mine] = project(
            current,
            gains_ref[layer, 0:1],
            weights,
            cos,
            sin,
            kept["normed"].at[layer],
            kept["query"].at[layer],
        )
        gathers[layer].start()

    def rest_of_layer(layer, current, weights):
        gathers[layer].finish()
        attended = attend(
            kept["query"].at[layer],
            kept["joined"].at[layer],
            own_seg_ref,
            seg_ref,
            kept["probs"].at[layer],
        )
        kept["attended"][layer] = attended
        midway, scale, normed_two, gate, up, hidden, result = feed_forward(
            current, attended, gains_ref[layer, 1:2], weights
        )
        kept["normed_two"][layer] = normed_two
        kept["hidden"][layer] = hidden
        return midway, gate, up, result

    def back_of_layer(layer, incoming, midway, gate, up, weights):
        down_grad, gate_grad, up_grad, gain_grad, midway_grad, out_grad, mixed_grad = (
            feed_forward_back(incoming, midway, gate, up, gains_ref[layer, 1:2], weights)
        )
        kept["down_grad"][layer] = down_grad
        kept["gate_grad"][layer] = gate_grad
        kept["up_grad"][layer] = up_grad
        kept["out_grad"][layer] = out_grad
        kept["midway_grad"][...] = midway_grad
        kept["query_grad"][...] = attend_back(
            mixed_grad,
            kept["attended"][layer],
            kept["query"].at[layer],
            kept["joined"].at[layer],
            kept["probs"].at[layer],
            kept["parts"].at[layer],
        )
        sums[layer].start()
        return gain_grad

    def end_of_layer(layer, current, weights):
        sums[layer].finish(kept["key_grads"])
        turned, values, gain_grad, grad_in = project_back(
            kept["query_grad"][...],
            kept["key_grads"][...],
            kept["midway_grad"][...],
            current,
            gains_ref[layer, 0:1],
            cos,
            sin,
            weights,
        )
        kept["turned"][layer] = turned
        kept["values"][layer] = values
        return gain_grad, grad_in

    def prepare_grads(layer):
        grads[layer].prepare(
            kept["normed"][layer],
            kept["normed_two"][layer],
            kept["attended"][layer],
            kept["hidden"][layer],
        )

    def rest_grads(layer):
        grads[layer].rest(
            kept["gate_grad"].at[layer], kept["up_grad"].at[layer], kept["down_grad"].at[layer]
        )

    def projection_grads(layer):
        grads[layer].projections(
            kept["turned"].at[layer], kept["values"].at[layer], kept["out_grad"].at[layer]
        )

    x = x_ref[...].astype(F32)
    start_layer(0, x, first_1)
    midway, gate, up, result = rest_of_layer(0, x, rest_1)
    kept["midway"][...] = midway
    kept["gate"][...] = gate
    kept["up"][...] = up
    passed = result.astype(BF16)
    kept["x_2"][...] = passed
    start_layer(1, passed.astype(F32), first_2)
    midway, gate, up, result = rest_of_layer(1, kept["x_2"][...].astype(F32), rest_2)
    result_ref[...] = result.T

    mlp_gain_grad_2 = back_of_layer(1, late_ref[...].astype(F32), midway, gate, up, rest_2)
    prepare_grads(1)
    sums[1].middle()
    rest_grads(1)
    attn_gain_grad_2, grad_in = end_of_layer(1, kept["x_2"][...].astype(F32), first_2)
    mlp_gain_grad_1 = back_of_layer(
        0,
        grad_in.astype(BF16).astype(F32),
        kept["midway"][...],
        kept["gate"][...],
        kept["up"][...],
        rest_1,
    )
    prepare_grads(0)
    sums[0].middle()
    projection_grads(1)
    grads[1].round(kept["packed"], attn_gain_grad_2, mlp_gain_grad_2)
    leave_2 = pltpu.make_async_copy(kept["packed"], grads_2_ref, out_sems.at[0])
    leave_2.start()
    rest_grads(0)
    attn_gain_grad_1, grad_in = end_of_layer(0, x_ref[...].astype(F32), first_1)
    grad_in_ref[...] = grad_in.T
    projection_grads(0)
    leave_2.wait()
    grads[0].round(kept["packed"], attn_gain_grad_1, mlp_gain_grad_1)
    leave_1 = pltpu.make_async_copy(kept["packed"], grads_1_ref, out_sems.at[1])
    leave_1.start()
    leave_1.wait()


def run_layers(x, late, gains, wide, down, cos, sin, own_seg, seg_row):
    edge = jax.ShapeDtypeStruct((D, ROWS), F32)
    part = jax.ShapeDtypeStruct((64, PACKED, LANES), BF16)
    weights = weight_scratch(*PROJECTION) + weight_scratch(*REST)
    return pl.pallas_call(
        layers_kernel,
        out_shape=(edge, edge, part, part),
        in_specs=[VMEM] * 3 + [ANY] * 2 + [VMEM] * 4,
        out_specs=(VMEM, VMEM, ANY, ANY),
        scratch_shapes=[
            pltpu.SemaphoreType.DMA((4, 8)),
            pltpu.SemaphoreType.DMA((4, 8)),
            pltpu.SemaphoreType.DMA((2,)),
            *[pltpu.VMEM(shape, kind) for shape, kind in KEPT.values()],
            *weights,
            *weights,
        ],
        compiler_params=params(2),
        name="layers",
    )(x, late, gains, wide, down, cos, sin, own_seg, seg_row)


def rope_tables(first):
    places = first + jnp.arange(ROWS, dtype=jnp.int32)
    pair_index = jnp.arange(HEAD // 2).astype(F32)
    frequency = rope_base ** (-2.0 * pair_index / HEAD)
    angles = places.astype(F32)[:, None] * frequency[None, :]
    cos, sin = jnp.cos(angles), jnp.sin(angles)
    return jnp.concatenate([cos] * 4, axis=1), jnp.concatenate([-sin, sin] * 2, axis=1)


def local(block_input, cotangent, segment_ids, *shards):
    section = lax.axis_index("section")
    ctx = lax.axis_index("ctx")
    x = lax.dynamic_index_in_dim(block_input[:, 0], section, 0, keepdims=False)
    late = lax.dynamic_index_in_dim(cotangent[:, 0], section, 0, keepdims=False)
    seg_row = lax.dynamic_index_in_dim(segment_ids[:, 0], section, 0)
    own_seg = lax.dynamic_slice_in_dim(seg_row, ctx * ROWS, ROWS, 1).reshape(ROWS, 1)
    cos, sin = rope_tables(ctx * ROWS)

    gathered = gather_weights(pack_shards(shards))
    wide, down, gains = unpack_weights(gathered)

    result, grad_in, grads_1, grads_2 = run_layers(
        x, late, gains, wide, down, cos, sin, own_seg, seg_row
    )
    by_device = (4, 2, 2, 4, PACKED, LANES)
    leaving = jnp.where(section == 0, result, grad_in)
    staying = jnp.where(section == 0, grad_in, result)
    packed, came = scatter_grads(
        grads_1.reshape(by_device), grads_2.reshape(by_device), leaving
    )
    return finish(packed, staying, came)


def solution(mesh):
    shard = P("section", ("ctx", "fsdp"))
    matrix = P("section", ("ctx", "fsdp"), None)
    return jax.shard_map(
        local,
        mesh=mesh,
        in_specs=(
            P(None, "fsdp", "ctx", None),
            P(None, "fsdp", "ctx", None),
            P(None, "fsdp", None),
            shard,
            matrix,
            matrix,
            matrix,
            matrix,
            matrix,
            matrix,
            matrix,
            shard,
        ),
        out_specs=(
            P("section", None, "fsdp", "ctx", None),
            shard,
            matrix,
            matrix,
            matrix,
            matrix,
            matrix,
            matrix,
            matrix,
            shard,
        ),
        check_vma=False,
    )
```

```python
import functools

import jax
import jax.numpy as jnp
from jax import lax
from jax.experimental import pallas as pl
from jax.experimental.pallas import tpu as pltpu
from jax.sharding import PartitionSpec as P

MESH = pl.DeviceIdType.MESH
F32 = jnp.float32
BF16 = jnp.bfloat16
ANY = pl.BlockSpec(memory_space=pl.ANY)
VMEM = pl.BlockSpec(memory_space=pltpu.VMEM)

D = 576
FF = 1536
KVD = 192
HEAD = 64
GROUP = 3
KV_HEADS = 3
ROWS = 128
SEQ = 1024
LANES = 128

norm_eps = 1e-05
rope_base = 100000.0
masked_score = -1e30

WIDE = 4608
GATE_AT = 768
UP_AT = GATE_AT + FF
OUT_AT = UP_AT + FF
VALUE_AT = OUT_AT + D
TAIL_AT = VALUE_AT - HEAD
BLOCKS = WIDE // LANES

DOWN_ROWS = 24
TAIL_ROW = 4 * DOWN_ROWS
UPPER_ROW = TAIL_ROW + DOWN_ROWS // 2
LOWER_ROW = 336
GAIN_ROW = LOWER_ROW + 9 * 12
PACKED = 448
GAIN_TILE = 432
UPPER_COLUMNS = tuple(range(GATE_AT // LANES, OUT_AT // LANES))
LOWER_COLUMNS = tuple(range(GATE_AT // LANES)) + tuple(range(OUT_AT // LANES, BLOCKS))


def packed_row(column):
    if column in UPPER_COLUMNS:
        return UPPER_ROW + 9 * UPPER_COLUMNS.index(column)
    return LOWER_ROW + 9 * LOWER_COLUMNS.index(column)


GATHER_PARTS = (
    ((0, 336), (((0, 176), "xy"), ((176, 160), "yx"))),
    ((336, 112), (((336, 64), "xy"), ((400, 48), "yx"))),
)
VMEM_BYTES = 63 * 1024 * 1024


def params(collective_id=None):
    if collective_id is None:
        return pltpu.CompilerParams(vmem_limit_bytes=VMEM_BYTES)
    return pltpu.CompilerParams(
        vmem_limit_bytes=VMEM_BYTES, collective_id=collective_id, has_side_effects=True
    )


def dot(left, right):
    return jnp.dot(left, right, preferred_element_type=F32)


def dot_nt(left, right):
    return lax.dot_general(left, right, (((1,), (1,)), ((), ())), preferred_element_type=F32)


def dot_tn(left, right):
    return lax.dot_general(left, right, (((0,), (0,)), ((), ())), preferred_element_type=F32)


class Place:
    def __init__(self):
        self.section = lax.axis_index("section")
        ctx = lax.axis_index("ctx")
        fsdp = lax.axis_index("fsdp")
        self.core = lax.rem(ctx, 2)
        self.at = {
            "x": lax.rem(fsdp, 4),
            "y": ctx // 2,
            "z": self.section * 2 + fsdp // 4,
        }

    def device(self, core=None, **moved):
        at = dict(self.at, **moved)
        core = self.core if core is None else core
        return (at["z"] // 2, at["y"] * 2 + core, lax.rem(at["z"], 2) * 4 + at["x"])

    def shifted(self, axis, step):
        return lax.rem(self.at[axis] + step + 4, 4)

    def neighbour(self, axis, step):
        return self.device(**{axis: self.shifted(axis, step)})

    def partner(self):
        return self.device(core=1 - self.core)


def greet(devices):
    barrier = pltpu.get_barrier_semaphore()
    for device in devices:
        pl.semaphore_signal(barrier, inc=1, device_id=device, device_id_type=MESH)
    pl.semaphore_wait(barrier, len(devices))


def halves(rows):
    first, count = rows
    upper = (count // 2 + 15) // 16 * 16
    return (first, upper), (first + upper, count - upper)


def layer_region(ref, layer, coords, whole, rows, core):
    y = slice(None) if "y" in whole else coords["y"]
    x = slice(None) if "x" in whole else coords["x"]
    return ref.at[layer, y, core, :, x, pl.ds(*rows)]


GATHER_SLOTS = 3 + 2 * 2 * 4 + 2 * 4


def gather_steps(place, layer, part, held, send_sems, recv_sems):
    core = place.core
    all_rows, chunks = part
    plane = lax.rem(place.at["z"] + 4 - 2 * layer, 4)

    def copy(slot, ref, device):
        return pltpu.make_async_remote_copy(
            src_ref=ref,
            dst_ref=ref,
            send_sem=send_sems.at[slot],
            recv_sem=recv_sems.at[slot],
            device_id=device,
            device_id_type=MESH,
        )

    def shard(z_lo):
        return held.at[layer, place.at["y"], core, z_lo, place.at["x"], pl.ds(*all_rows)]

    def up(z_lo, slot):
        return copy(slot, shard(z_lo), place.neighbour("z", 1))

    def down(z_lo, slot):
        return copy(slot, shard(z_lo), place.neighbour("z", -1))

    for source in range(2):

        @pl.when(plane == source)
        def _():
            up(source, 0).start()
            down(source, 1).start()

    yield

    @pl.when((plane == 1) | (plane == 2))
    def _():
        up(0, 0).wait_recv()

    @pl.when((plane == 0) | (plane == 3))
    def _():
        down(0, 1).wait_recv()

    @pl.when(plane == 2)
    def _():
        up(1, 2).start()

    @pl.when(plane == 3)
    def _():
        down(0, 2).start()

    yield

    @pl.when(plane >= 2)
    def _():
        up(0, 2).wait_recv()

    counter = [3]
    sent = []

    def send(ref, device):
        made = copy(counter[0], ref, device)
        counter[0] += 1
        made.start()
        sent.append(made)
        return made

    to_partner = []
    for phase in range(2):
        first, second = [], []
        for rows, order in chunks:
            axis, whole = order[phase], order[:phase]
            block = layer_region(held, layer, place.at, whole, rows, core)
            first.append([send(block, place.neighbour(axis, way)) for way in (1, -1)])
            if phase == 1:
                to_partner.append(send(block, place.partner()))
        yield
        for copies, (rows, order) in zip(first, chunks):
            axis, whole = order[phase], order[:phase]
            for made in copies:
                made.wait_recv()
            left = dict(place.at, **{axis: place.shifted(axis, -1)})
            right = dict(place.at, **{axis: place.shifted(axis, 1)})
            upper, lower = halves(rows)
            second += [
                send(
                    layer_region(held, layer, left, whole, upper, core), place.neighbour(axis, 1)
                ),
                send(
                    layer_region(held, layer, right, whole, lower, core), place.neighbour(axis, -1)
                ),
            ]
            if phase == 1:
                for coords in (left, right):
                    to_partner.append(
                        send(layer_region(held, layer, coords, whole, rows, core), place.partner())
                    )
        yield
        for made in second:
            made.wait_recv()
    for rows, order in chunks:
        axis, whole = order[1], order[:1]
        far = dict(place.at, **{axis: place.shifted(axis, 2)})
        to_partner.append(send(layer_region(held, layer, far, whole, rows, core), place.partner()))
    yield
    for made in to_partner:
        made.wait_recv()
    for made in sent:
        made.wait_send()

    @pl.when(plane <= 1)
    def _():
        up(0, 0).wait_send()
        down(0, 1).wait_send()

    @pl.when(plane >= 2)
    def _():
        up(0, 2).wait_send()

    yield


SCATTER_PARTS = (
    ((0, 336), (((0, 176), "yx"), ((176, 160), "xy"))),
    ((336, 112), (((336, 64), "yx"), ((400, 48), "xy"))),
)
SCATTER_SLOTS = 1 + 2 * 2 * 4 + 2


def scatter_inboxes(part):
    (first, count), chunks = part
    boxes = []
    for (_, rows), order in chunks:
        others = (2, 4) if order == "yx" else (4, 2)
        boxes.append(pltpu.VMEM((3, *others, rows, LANES), BF16))
        boxes.append(pltpu.VMEM((3, 2, rows, LANES), BF16))
    boxes.append(pltpu.VMEM((2, count, LANES), BF16))
    return boxes


def scatter_steps(place, layer, part, held, boxes, send_sems, recv_sems, out_ref):
    core = place.core
    here_y, here_x = place.at["y"], place.at["x"]
    (first, count), chunks = part
    counter = [0]
    sent = []

    def copy(source, target, device):
        slot = counter[0]
        counter[0] += 1
        return pltpu.make_async_remote_copy(
            src_ref=source,
            dst_ref=target,
            send_sem=send_sems.at[slot],
            recv_sem=recv_sems.at[slot],
            device_id=device,
            device_id_type=MESH,
        )

    def send(source, target, device):
        made = copy(source, target, device)
        made.start()
        sent.append(made)
        return made

    def add(spot, source, rows):
        held[spot] = (held[spot].astype(F32) + source().astype(F32)).astype(BF16)

    all_rows = pl.ds(first, count)
    swap = copy(
        held.at[layer, :, 1 - core, :, :, all_rows],
        held.at[1 - layer, :, core, :, :, all_rows],
        place.partner(),
    )
    swap.start()
    yield
    swap.wait()

    def add_swapped(step, carry):
        y, z_lo, x = step // 8, lax.rem(step // 4, 2), lax.rem(step, 4)
        add(
            (layer, y, core, z_lo, x, all_rows),
            lambda: held[1 - layer, y, 1 - core, z_lo, x, all_rows],
            count,
        )
        return carry

    lax.fori_loop(0, 32, add_swapped, 0)

    def add_block(phase, axis, coords, rows, box, slot):
        at, size = rows

        def in_box(begin):
            return pl.ds(begin, size)

        begin = 0 if slot else at[1]
        here = pl.ds(at[0], size)
        if phase == 0:

            def body(step, carry):
                if axis == "y":
                    z_lo, x = step // 4, lax.rem(step, 4)
                    spot = (layer, coords["y"], core, z_lo, x, here)
                    add(spot, lambda: box[slot, z_lo, x, in_box(begin)], size)
                else:
                    y, z_lo = step // 2, lax.rem(step, 2)
                    spot = (layer, y, core, z_lo, coords["x"], here)
                    add(spot, lambda: box[slot, y, z_lo, in_box(begin)], size)
                return carry

            lax.fori_loop(0, 8, body, 0)
        else:
            for z_lo in range(2):
                spot = (layer, coords["y"], core, z_lo, coords["x"], here)
                add(spot, lambda: box[slot, z_lo, in_box(begin)], size)

    flights = [None, None]
    for phase in range(2):
        for step in range(2):
            for i, (rows, order) in enumerate(chunks):
                box = boxes[2 * i + phase]
                if flights[i] is not None:
                    for made, before_phase, before_axis, lands, spot_rows, before_box, slot in flights[i]:
                        made.wait_recv()
                        add_block(before_phase, before_axis, lands, spot_rows, before_box, slot)
                axis, whole = order[phase], order[phase + 1 :]
                right = dict(place.at, **{axis: place.shifted(axis, 1)})
                left = dict(place.at, **{axis: place.shifted(axis, -1)})
                far = dict(place.at, **{axis: place.shifted(axis, 2)})
                upper, lower = halves(rows)
                if step == 0:
                    plan = ((far, upper, 1, right, 0), (far, lower, -1, left, 0))
                else:
                    plan = ((right, rows, 1, place.at, 1), (left, rows, -1, place.at, 2))
                flights[i] = []
                for source_at, part_rows, way, lands, slot in plan:
                    begin = part_rows[0] - rows[0]
                    lead = (slice(None),) * (2 if phase == 0 else 1)
                    made = send(
                        layer_region(held, layer, source_at, whole, part_rows, core),
                        box.at[(slot, *lead, pl.ds(begin, part_rows[1]))],
                        place.neighbour(axis, way),
                    )
                    flights[i].append(
                        (made, phase, axis, lands, ((part_rows[0], begin), part_rows[1]), box, slot)
                    )
            yield
    for flight in flights:
        for made, phase, axis, lands, spot_rows, box, slot in flight:
            made.wait_recv()
            add_block(phase, axis, lands, spot_rows, box, slot)

    plane = lax.rem(place.at["z"] + 4 - 2 * layer, 4)
    odd = lax.rem(plane, 2)
    stays = lax.rem((plane + 1) // 2, 2)
    box = boxes[4]

    def shard(z_lo):
        return held.at[layer, here_y, core, z_lo, here_x, all_rows]

    def along_z(step):
        return place.device(z=lax.rem(place.at["z"] + step + 4, 4))

    pair = send(shard(1 - stays), box.at[0], along_z(1 - 2 * odd))
    last = copy(shard(stays), box.at[1], along_z(2 * odd - 1))
    yield
    pair.wait_recv()
    add((layer, here_y, core, stays, here_x, all_rows), lambda: box[0], count)

    @pl.when(plane >= 2)
    def _():
        last.start()

    yield

    @pl.when(plane < 2)
    def _():
        last.wait_recv()
        out_ref[all_rows] = held[layer, here_y, core, stays, here_x, all_rows].astype(
            F32
        ) + box[1].astype(F32)

    for made in sent:
        made.wait_send()

    @pl.when(plane >= 2)
    def _():
        last.wait_send()

    yield


class Exchange:
    def __init__(self, place, send_sems, recv_sems):
        self.place = place
        self.send_sems = send_sems
        self.recv_sems = recv_sems

    def copy(self, slot, source, target, device):
        return pltpu.make_async_remote_copy(
            src_ref=source,
            dst_ref=target,
            send_sem=self.send_sems.at[slot],
            recv_sem=self.recv_sems.at[slot],
            device_id=device,
            device_id_type=MESH,
        )

    def along_y(self, step):
        return self.place.device(y=lax.rem(self.place.at["y"] + step + 4, 4))


class KeyGather(Exchange):
    def __init__(self, place, keys_ref, send_sems, recv_sems):
        super().__init__(place, send_sems, recv_sems)
        self.keys_ref = keys_ref

    def direct(self, away):
        own = self.keys_ref.at[self.place.at["y"] * 2 + self.place.core]
        return self.copy(away, own, own, self.along_y(away))

    def passed_on(self, away):
        block = self.keys_ref.at[
            lax.rem(self.place.at["y"] - away + 4, 4) * 2 + self.place.core
        ]
        return self.copy(4 + away, block, block, self.place.partner())

    def start(self):
        y = self.place.at["y"]
        for away in (1, 3, 2):

            @pl.when(y + away < 4)
            def _():
                self.direct(away).start()

        self.passed_on(0).start()
        for away in range(1, 4):

            @pl.when(y + away < 4)
            def _():
                self.keys_ref[pl.ds((y + away) * 2, 2)] = jnp.zeros(
                    (2,) + self.keys_ref.shape[1:], self.keys_ref.dtype
                )

    def finish(self):
        y = self.place.at["y"]
        for away in range(1, 4):

            @pl.when(y - away >= 0)
            def _():
                self.direct(away).wait_recv()
                self.passed_on(away).start()

        self.passed_on(0).wait()
        for away in range(1, 4):

            @pl.when(y - away >= 0)
            def _():
                self.passed_on(away).wait()

            @pl.when(y + away < 4)
            def _():
                self.direct(away).wait_send()


class KeyGradSum(Exchange):
    def __init__(self, place, parts_ref, pair_ref, ring_ref, send_sems, recv_sems):
        super().__init__(place, send_sems, recv_sems)
        self.parts_ref = parts_ref
        self.pair_ref = pair_ref
        self.ring_ref = ring_ref

    def swap(self):
        return self.copy(
            0, self.parts_ref.at[1 - self.place.core], self.pair_ref, self.place.partner()
        )

    def direct(self, away):
        y = lax.rem(self.place.at["y"] - away + 4, 4)
        return self.copy(
            away,
            self.parts_ref.at[self.place.core, y],
            self.ring_ref.at[away],
            self.along_y(-away),
        )

    def start(self):
        self.swap().start()

    def middle(self):
        self.swap().wait()
        core = self.place.core
        for y in range(4):
            self.parts_ref[core, y] = (
                self.parts_ref[core, y].astype(F32) + self.pair_ref[y].astype(F32)
            ).astype(BF16)
        for away in (1, 3, 2):

            @pl.when(self.place.at["y"] - away >= 0)
            def _():
                self.direct(away).start()

    def finish(self, out_ref):
        y = self.place.at["y"]
        out_ref[...] = self.parts_ref[self.place.core, y].astype(F32)
        for away in range(1, 4):

            @pl.when(y + away < 4)
            def _():
                self.direct(away).wait_recv()
                out_ref[...] += self.ring_ref[away].astype(F32)

        for away in range(1, 4):

            @pl.when(y - away >= 0)
            def _():
                self.direct(away).wait_send()


def packed_shard(attn_ref, query_ref, key_ref, value_ref, w_out_ref, gate_ref, up_ref, down_ref, mlp_ref):
    def wide(ref):
        return ref[0].astype(F32)

    joined = jnp.concatenate(
        [wide(r) for r in (query_ref, key_ref, gate_ref, up_ref, w_out_ref, value_ref)], axis=1
    )
    down = wide(down_ref)
    pieces = [down[:, i * LANES : (i + 1) * LANES] for i in range(4)]
    half = DOWN_ROWS // 2
    pieces.append(jnp.concatenate([down[:half, 4 * LANES :], down[half:, 4 * LANES :]], axis=1))
    pieces += [joined[:, i * LANES : (i + 1) * LANES] for i in UPPER_COLUMNS]
    pieces.append(jnp.zeros((12, LANES), F32))
    pieces += [joined[:, i * LANES : (i + 1) * LANES] for i in LOWER_COLUMNS]
    for ref in (attn_ref, mlp_ref):
        gain = ref[...].astype(F32)
        pieces.append(jnp.concatenate([gain, jnp.zeros((1, LANES - 9), F32)], axis=1))
    pieces.append(jnp.zeros((2, LANES), F32))
    return jnp.concatenate(pieces, axis=0).astype(BF16)


def gain_masks(first_device, devices, rows_each, rows):
    shape = (devices * rows_each, D)
    row = lax.broadcasted_iota(jnp.int32, shape, 0)
    owner = lax.broadcasted_iota(jnp.int32, shape, 1) // 9
    same = owner == first_device + row // rows_each
    place = lax.rem(row, rows_each)
    return [same & (place == at) for at in rows]


def lane_spread():
    lane = lax.broadcasted_iota(jnp.int32, (LANES, D), 0)
    feature = lax.broadcasted_iota(jnp.int32, (LANES, D), 1)
    return (lane == lax.rem(feature, 9)).astype(BF16)


def packed_rows(held, layer, y, first, count):
    start = first // 16 * 16
    size = (first + count + 15) // 16 * 16 - start
    return [
        held[layer, y, core, z_lo, x, start : start + size].astype(F32)[
            first - start : first - start + count
        ]
        for core in range(2)
        for z_lo in range(2)
        for x in range(4)
    ]


def unpack_wide(held, layer, columns, wide):
    def body(y, carry):
        rows = pl.ds(pl.multiple_of(y * 144, 16), 144)
        for column in columns:
            wide[layer, rows, column * LANES : (column + 1) * LANES] = jnp.concatenate(
                packed_rows(held, layer, y, packed_row(column), 9), axis=0
            ).astype(BF16)
        return carry

    lax.fori_loop(0, 4, body, 0)


def unpack_down(held, layer, down):
    def body(y, carry):
        rows = pl.ds(pl.multiple_of(y * 384, 16), 384)
        for column in range(4):
            down[layer, rows, column * LANES : (column + 1) * LANES] = jnp.concatenate(
                packed_rows(held, layer, y, DOWN_ROWS * column, DOWN_ROWS), axis=0
            ).astype(BF16)
        tails = []
        for tail in packed_rows(held, layer, y, TAIL_ROW, DOWN_ROWS // 2):
            tails += [tail[:, :HEAD], tail[:, HEAD:]]
        down[layer, rows, 4 * LANES :] = jnp.concatenate(tails, axis=0).astype(BF16)
        return carry

    lax.fori_loop(0, 4, body, 0)


def unpack_gains(held, layer, gains):
    totals = [jnp.zeros((1, D), F32)] * 2
    spread_to = lane_spread()
    for y in range(4):
        rows = held[layer, y, :, :, :, GAIN_TILE:, :].reshape(16 * 16, LANES)
        spread = dot(rows, spread_to)
        masks = gain_masks(y * 16, 16, 16, (GAIN_ROW - GAIN_TILE, GAIN_ROW - GAIN_TILE + 1))
        totals = [
            total + jnp.sum(jnp.where(mask, spread, 0.0), axis=0, keepdims=True)
            for total, mask in zip(totals, masks)
        ]
    gains[layer, 0:1] = totals[0]
    gains[layer, 1:2] = totals[1]


def finish_kernel(
    packed_ref,
    kept_ref,
    came_ref,
    edges_ref,
    attn_ref,
    query_ref,
    key_ref,
    value_ref,
    w_out_ref,
    gate_ref,
    up_ref,
    down_ref,
    mlp_ref,
):
    section = lax.axis_index("section")
    edges_ref[0, section, 0] = kept_ref[...]
    edges_ref[0, 1 - section, 0] = came_ref[...]
    packed = packed_ref[...]
    joined = jnp.concatenate(
        [packed[packed_row(i) : packed_row(i) + 9] for i in range(BLOCKS)], axis=1
    )
    query_ref[:, 0] = joined[:, :D]
    key_ref[:, 0] = joined[:, D:GATE_AT]
    gate_ref[:, 0] = joined[:, GATE_AT:UP_AT]
    up_ref[:, 0] = joined[:, UP_AT:OUT_AT]
    w_out_ref[:, 0] = joined[:, OUT_AT:VALUE_AT]
    value_ref[:, 0] = joined[:, VALUE_AT:]
    tail = packed[TAIL_ROW:UPPER_ROW]
    down_ref[0] = jnp.concatenate(
        [packed[DOWN_ROWS * i : DOWN_ROWS * (i + 1)] for i in range(4)]
        + [jnp.concatenate([tail[:, :HEAD], tail[:, HEAD:]], axis=0)],
        axis=1,
    )
    attn_ref[...] = packed[GAIN_ROW : GAIN_ROW + 1, :9]
    mlp_ref[...] = packed[GAIN_ROW + 1 : GAIN_ROW + 2, :9]


def finish(packed, kept, came):
    shapes = (
        (1, 2, 1, D, ROWS),
        (1, 9),
        (9, 1, D),
        (9, 1, KVD),
        (9, 1, KVD),
        (9, 1, D),
        (9, 1, FF),
        (9, 1, FF),
        (1, DOWN_ROWS, D),
        (1, 9),
    )
    edges, attn, *wide, down, mlp = pl.pallas_call(
        finish_kernel,
        out_shape=tuple(jax.ShapeDtypeStruct(shape, F32) for shape in shapes),
        in_specs=[VMEM] * 3,
        out_specs=(VMEM,) * len(shapes),
        compiler_params=params(),
        name="finish",
    )(packed, kept, came)
    wide = [grad.transpose(1, 0, 2) for grad in wide]
    return (edges.transpose(0, 1, 2, 4, 3), attn, *wide, down, mlp)


def swap_halves(block):
    lane = lax.broadcasted_iota(jnp.int32, block.shape, 1)
    return jnp.where(
        lax.rem(lane, HEAD) < HEAD // 2,
        pltpu.roll(block, LANES - HEAD // 2, 1),
        pltpu.roll(block, HEAD // 2, 1),
    )


def rotated(block, cos, sin):
    return block * cos + swap_halves(block) * sin


def project(current, gain, weights, cos, sin, normed_ref, query_ref):
    scale = lax.rsqrt(jnp.mean(current * current, axis=1, keepdims=True) + norm_eps)
    normed = (current * scale * gain).astype(BF16)
    normed_ref[...] = normed
    raw = dot(normed, weights.get("qk"))
    turned = [
        rotated(raw[:, i * LANES : (i + 1) * LANES], cos, sin).astype(BF16) for i in range(6)
    ]
    for i in range(4):
        query_ref[:, i * LANES : (i + 1) * LANES] = turned[i]
    query_ref[:, 4 * LANES :] = turned[4][:, :HEAD]
    values = dot(normed, weights.get("tail"))[:, HEAD:]
    return jnp.concatenate(
        [turned[4][:, HEAD:].astype(F32), turned[5].astype(F32), values], axis=1
    ).astype(BF16)


def heads_of(rows, group):
    return jnp.concatenate(
        [rows[:, (group * GROUP + r) * HEAD : (group * GROUP + r + 1) * HEAD] for r in range(GROUP)],
        axis=0,
    )


def attend(query_ref, keys_ref, seg_row, probs_ref):
    first = lax.axis_index("ctx") * ROWS
    rows = first + lax.broadcasted_iota(jnp.int32, (ROWS, SEQ), 0)
    columns = lax.broadcasted_iota(jnp.int32, (ROWS, SEQ), 1)
    own_seg = jnp.sum(jnp.where(columns == rows, seg_row, 0), axis=1, keepdims=True)
    allowed = (columns <= rows) & (seg_row == own_seg)
    bias = jnp.where(allowed, 0.0, masked_score)
    bias = jnp.concatenate([bias] * GROUP, axis=0)
    queries = query_ref[...]
    mixed = []
    for group in range(KV_HEADS):
        keys = keys_ref[:, :, group * HEAD : (group + 1) * HEAD].reshape(SEQ, HEAD)
        values = keys_ref[:, :, KVD + group * HEAD : KVD + (group + 1) * HEAD].reshape(SEQ, HEAD)
        scores = dot_nt(heads_of(queries, group), keys) * HEAD**-0.5 + bias
        shifted = jnp.exp(scores - jnp.max(scores, axis=1, keepdims=True))
        probs = (shifted / jnp.sum(shifted, axis=1, keepdims=True)).astype(BF16)
        probs_ref[group] = probs
        mixture = dot(probs, values)
        mixed += [mixture[r * ROWS : (r + 1) * ROWS] for r in range(GROUP)]
    return jnp.concatenate(mixed, axis=1).astype(BF16)


def feed_forward(current, attended, gain, weights):
    midway = current + dot(attended, weights.get("out"))
    scale = lax.rsqrt(jnp.mean(midway * midway, axis=1, keepdims=True) + norm_eps)
    normed = (midway * scale * gain).astype(BF16)
    gate = dot(normed, weights.get("gate"))
    up = dot(normed, weights.get("up"))
    hidden = (gate / (1.0 + jnp.exp(-gate)) * up).astype(BF16)
    result = midway + dot(hidden, weights.get("down"))
    return midway, scale, normed, gate, up, hidden, result


def norm_backward(scaled, values, scale):
    return scale * scaled - values * scale**3 * jnp.mean(scaled * values, axis=1, keepdims=True)


def feed_forward_back(
    incoming, midway, gate, up, gain, weights
):
    scale = lax.rsqrt(jnp.mean(midway * midway, axis=1, keepdims=True) + norm_eps)
    down_grad = incoming.astype(BF16)
    hidden_grad = dot_nt(down_grad, weights.get("down"))
    sigmoid = 1.0 / (1.0 + jnp.exp(-gate))
    gate_grad = (hidden_grad * up * sigmoid * (1.0 + gate * (1.0 - sigmoid))).astype(BF16)
    up_grad = (hidden_grad * gate * sigmoid).astype(BF16)
    normed_grad = dot_nt(gate_grad, weights.get("gate")) + dot_nt(
        up_grad, weights.get("up")
    )
    gain_grad = jnp.sum(normed_grad * midway * scale, axis=0, keepdims=True)
    midway_grad = incoming + norm_backward(normed_grad * gain, midway, scale)
    out_grad = midway_grad.astype(BF16)
    mixed_grad = dot_nt(out_grad, weights.get("out")).astype(BF16)
    return down_grad, gate_grad, up_grad, gain_grad, midway_grad, out_grad, mixed_grad


def attend_back(mixed_grad, attended, query_ref, keys_ref, probs_ref, parts_ref, between):
    queries = query_ref[...]
    query_grads = []
    for group in range(KV_HEADS):
        keys = keys_ref[:, :, group * HEAD : (group + 1) * HEAD].reshape(SEQ, HEAD)
        values = keys_ref[:, :, KVD + group * HEAD : KVD + (group + 1) * HEAD].reshape(SEQ, HEAD)
        grads = heads_of(mixed_grad, group)
        delta = jnp.sum(
            grads.astype(F32) * heads_of(attended, group).astype(F32), axis=1, keepdims=True
        )
        probs = probs_ref[group]
        score_grad = (probs.astype(F32) * (dot_nt(grads, values) - delta)).astype(BF16)
        query_grad = dot(score_grad, keys) * HEAD**-0.5
        query_grads += [query_grad[r * ROWS : (r + 1) * ROWS] for r in range(GROUP)]
        key_part = (dot_tn(heads_of(queries, group), score_grad) * HEAD**-0.5).astype(BF16)
        value_part = dot_tn(grads, probs).astype(BF16)
        for block in range(8):
            columns = slice(block * ROWS, (block + 1) * ROWS)
            at = (block % 2, block // 2)
            parts_ref[*at, group * HEAD : (group + 1) * HEAD] = key_part[:, columns]
            parts_ref[*at, KVD + group * HEAD : KVD + (group + 1) * HEAD] = value_part[:, columns]
        between[group]()
    return jnp.concatenate(query_grads, axis=1)


def project_back(
    query_grad, key_grads, midway_grad, current, gain, cos, sin, weights
):
    key_grads = key_grads.T
    joined = jnp.concatenate([query_grad, key_grads[:, :KVD]], axis=1)
    turned = jnp.concatenate(
        [rotated(joined[:, i * LANES : (i + 1) * LANES], cos, -sin) for i in range(6)], axis=1
    ).astype(BF16)
    values = key_grads[:, KVD:].astype(BF16)
    padded = jnp.concatenate([jnp.zeros((ROWS, HEAD), F32), key_grads[:, KVD:]], axis=1)
    normed_grad = dot_nt(turned, weights.get("qk")) + dot_nt(
        padded.astype(BF16), weights.get("tail")
    )
    scale = lax.rsqrt(jnp.mean(current * current, axis=1, keepdims=True) + norm_eps)
    gain_grad = jnp.sum(normed_grad * current * scale, axis=0, keepdims=True)
    grad_in = midway_grad + norm_backward(normed_grad * gain, current, scale)
    return turned, values, gain_grad, grad_in


GRAD_DEVICES = 16


def transposed(rows):
    return rows.astype(F32).T.astype(BF16)


class WeightGrads:
    def __init__(self, packed, upper, lower, gain_rows, lhs, hidden_lhs):
        self.packed = packed
        self.upper = upper
        self.lower = lower
        self.gain_rows = gain_rows
        self.lhs = lhs
        self.hidden_lhs = hidden_lhs

    def place(self, stage, first_row, column, product):
        for i in range(product.shape[1] // LANES):
            at = packed_row(column + i) - first_row
            part = product[:, i * LANES : (i + 1) * LANES]
            for d in range(GRAD_DEVICES):
                stage[d, at : at + 9] = part[9 * d : 9 * d + 9]

    def prepare(self, normed, normed_two, attended, hidden):
        self.lhs[0] = transposed(normed)
        self.lhs[1] = transposed(normed_two)
        self.lhs[2] = transposed(attended)
        self.hidden_lhs[...] = transposed(hidden)

    def rows(self, step, each):
        return pl.ds(pl.multiple_of(step * each * GRAD_DEVICES, 16), each * GRAD_DEVICES)

    def round(self, stage, y, first_row):
        rounded = stage[...].astype(BF16)
        self.packed[y, :, :, :, first_row : first_row + stage.shape[1]] = rounded.reshape(
            (2, 2, 4) + rounded.shape[1:]
        )

    def rest(self, gate_grad_ref, up_grad_ref, down_grad_ref):
        half = DOWN_ROWS // 2
        self.upper[:, LOWER_ROW - 12 :] = jnp.zeros((GRAD_DEVICES, 12, LANES), F32)

        def body(y, carry):
            second = self.lhs[1, self.rows(y, 9)]
            self.place(self.upper, 0, GATE_AT // LANES, dot(second, gate_grad_ref[...]))
            self.place(self.upper, 0, UP_AT // LANES, dot(second, up_grad_ref[...]))
            down = dot(self.hidden_lhs[self.rows(y, DOWN_ROWS)], down_grad_ref[...])
            for d in range(GRAD_DEVICES):
                own = down[DOWN_ROWS * d : DOWN_ROWS * (d + 1)]
                for i in range(4):
                    self.upper[d, DOWN_ROWS * i : DOWN_ROWS * (i + 1)] = own[
                        :, i * LANES : (i + 1) * LANES
                    ]
                self.upper[d, TAIL_ROW:UPPER_ROW] = jnp.concatenate(
                    [own[:half, 4 * LANES :], own[half:, 4 * LANES :]], axis=1
                )
            self.round(self.upper, y, 0)
            return carry

        lax.fori_loop(0, 64 // GRAD_DEVICES, body, 0)

    def projections(
        self, turned_ref, values_ref, out_grad_ref, attn_gain_grad, mlp_gain_grad
    ):
        spread_to = lane_spread()
        (mask,) = gain_masks(0, 64, 1, (0,))
        for i, gain_grad in enumerate((attn_gain_grad, mlp_gain_grad)):
            chosen = jnp.where(mask, gain_grad, 0.0).astype(BF16)
            self.gain_rows[i] = dot_nt(chosen, spread_to)
        self.lower[:, GAIN_ROW + 2 - LOWER_ROW :] = jnp.zeros((GRAD_DEVICES, 2, LANES), F32)

        def body(y, carry):
            first = self.lhs[0, self.rows(y, 9)]
            self.place(self.lower, LOWER_ROW, 0, dot(first, turned_ref[...]))
            third = self.lhs[2, self.rows(y, 9)]
            self.place(
                self.lower,
                LOWER_ROW,
                OUT_AT // LANES,
                jnp.concatenate(
                    [dot(third, out_grad_ref[...]), dot(first, values_ref[...])], axis=1
                ),
            )
            for i in range(2):
                gains = self.gain_rows[i, self.rows(y, 1)]
                for d in range(GRAD_DEVICES):
                    at = GAIN_ROW + i - LOWER_ROW
                    self.lower[d, at : at + 1] = gains[d : d + 1]
            self.round(self.lower, y, LOWER_ROW)
            return carry

        lax.fori_loop(0, 64 // GRAD_DEVICES, body, 0)


COLUMNS = {
    "qk": (0, GATE_AT),
    "gate": (GATE_AT, UP_AT),
    "up": (UP_AT, OUT_AT),
    "out": (OUT_AT, VALUE_AT),
    "tail": (TAIL_AT, WIDE),
}


class Weights:
    def __init__(self, layer, wide, down):
        self.layer = layer
        self.wide = wide
        self.down = down

    def get(self, name):
        if name == "down":
            return self.down[self.layer]
        first, end = COLUMNS[name]
        return self.wide[self.layer, :, first:end]


ROW = (ROWS, D)
KEPT = {
    "joined": ((2, 8, ROWS, 2 * KVD), BF16),
    "probs": ((2, KV_HEADS, GROUP * ROWS, SEQ), BF16),
    "parts": ((2, 2, 4, 2 * KVD, ROWS), BF16),
    "pair": ((4, 2 * KVD, ROWS), BF16),
    "ring": ((2, 4, 2 * KVD, ROWS), BF16),
    "key_grads": ((2 * KVD, ROWS), F32),
    "normed": ((2, *ROW), BF16),
    "query": ((2, *ROW), BF16),
    "attended": ((2, *ROW), BF16),
    "normed_two": ((2, *ROW), BF16),
    "hidden": ((2, ROWS, FF), BF16),
    "midway": (ROW, F32),
    "gate": ((ROWS, FF), F32),
    "up": ((ROWS, FF), F32),
    "x_2": (ROW, BF16),
    "gate_grad": ((ROWS, FF), BF16),
    "up_grad": ((ROWS, FF), BF16),
    "down_grad": (ROW, BF16),
    "out_grad": (ROW, BF16),
    "midway_grad": (ROW, F32),
    "query_grad": (ROW, F32),
    "turned": ((ROWS, D + KVD), BF16),
    "values": ((ROWS, KVD), BF16),
    "lhs": ((3, D, ROWS), BF16),
    "hidden_lhs": ((FF, ROWS), BF16),
    "upper": ((GRAD_DEVICES, LOWER_ROW, LANES), F32),
    "lower": ((GRAD_DEVICES, PACKED - LOWER_ROW, LANES), F32),
    "gain_rows": ((2, 64, LANES), F32),
    "held": ((2, 4, 2, 2, 4, PACKED, LANES), BF16),
    "wide": ((2, D, WIDE), BF16),
    "down": ((2, FF, D), BF16),
    "gains": ((2, 8, D), F32),
    "edge": ((D, ROWS), F32),
}


def layers_kernel(
    x_ref,
    late_ref,
    cos_ref,
    sin_ref,
    seg_ref,
    *rest,
):
    shards = rest[:9]
    summed_ref, stays_ref, came_ref = rest[9:12]
    send_sems, recv_sems, gather_send, gather_recv, scatter_send, scatter_recv, edge_sems, credit_sem, *scratch = (
        rest[12:]
    )
    place = Place()
    kept = dict(zip(KEPT, scratch))
    boxes = scratch[len(KEPT) :]
    held, gains_ref = kept["held"], kept["gains"]
    weights = [Weights(i, kept["wide"], kept["down"]) for i in range(2)]
    held[
        place.section, place.at["y"], place.core, lax.rem(place.at["z"], 2), place.at["x"]
    ] = packed_shard(*shards)
    greet(
        [place.partner()]
        + [place.neighbour(axis, way) for axis in "xz" for way in (1, -1)]
        + [place.device(y=place.shifted("y", step)) for step in (1, 2, 3)]
        + [place.device(z=place.shifted("z", 2))]
    )
    leaving = [
        [
            scatter_steps(
                place,
                layer,
                part,
                held,
                boxes[(2 * layer + i) * 5 : (2 * layer + i) * 5 + 5],
                scatter_send.at[layer, i],
                scatter_recv.at[layer, i],
                summed_ref,
            )
            for i, part in enumerate(SCATTER_PARTS)
        ]
        for layer in range(2)
    ]
    edge = pltpu.make_async_remote_copy(
        src_ref=kept["edge"],
        dst_ref=came_ref,
        send_sem=edge_sems.at[0],
        recv_sem=edge_sems.at[1],
        device_id=place.device(z=place.shifted("z", 2)),
        device_id_type=MESH,
    )

    def finish_edge(section, mine):
        @pl.when(place.section == section)
        def _():
            stays_ref[...] = mine

        @pl.when(place.section != section)
        def _():
            kept["edge"][...] = mine
            edge.start()

    def go(layer, part):
        next(leaving[layer][part])

    arriving = [
        [
            gather_steps(
                place, layer, part, held, gather_send.at[layer, i], gather_recv.at[layer, i]
            )
            for i, part in enumerate(GATHER_PARTS)
        ]
        for layer in range(2)
    ]

    def come(layer, part, steps=1):
        for _ in range(steps):
            next(arriving[layer][part])

    cos, sin = cos_ref[...], sin_ref[...]
    mine = lax.axis_index("ctx")
    gathers = [
        KeyGather(place, kept["joined"].at[i], send_sems.at[i], recv_sems.at[i]) for i in range(2)
    ]
    sums = [
        KeyGradSum(
            place,
            kept["parts"].at[i],
            kept["pair"],
            kept["ring"].at[i],
            send_sems.at[2 + i],
            recv_sems.at[2 + i],
        )
        for i in range(2)
    ]
    grads = [
        WeightGrads(
            held.at[i],
            kept["upper"],
            kept["lower"],
            kept["gain_rows"],
            kept["lhs"],
            kept["hidden_lhs"],
        )
        for i in range(2)
    ]

    def start_layer(layer, current):
        unpack_gains(held, layer, gains_ref)
        unpack_wide(held, layer, LOWER_COLUMNS, kept["wide"])
        kept["joined"][layer, mine] = project(
            current,
            gains_ref[layer, 0:1],
            weights[layer],
            cos,
            sin,
            kept["normed"].at[layer],
            kept["query"].at[layer],
        )
        gathers[layer].start()

    def attention_of_layer(layer):
        gathers[layer].finish()
        attended = attend(
            kept["query"].at[layer],
            kept["joined"].at[layer],
            seg_ref[place.section],
            kept["probs"].at[layer],
        )
        kept["attended"][layer] = attended

    def rest_of_layer(layer, current):
        unpack_wide(held, layer, UPPER_COLUMNS, kept["wide"])
        unpack_down(held, layer, kept["down"])
        attended = kept["attended"][layer]
        midway, scale, normed_two, gate, up, hidden, result = feed_forward(
            current, attended, gains_ref[layer, 1:2], weights[layer]
        )
        kept["normed_two"][layer] = normed_two
        kept["hidden"][layer] = hidden
        return midway, gate, up, result

    def back_of_layer(layer, incoming, midway, gate, up, after, between):
        down_grad, gate_grad, up_grad, gain_grad, midway_grad, out_grad, mixed_grad = (
            feed_forward_back(incoming, midway, gate, up, gains_ref[layer, 1:2], weights[layer])
        )
        kept["down_grad"][...] = down_grad
        kept["gate_grad"][...] = gate_grad
        kept["up_grad"][...] = up_grad
        kept["out_grad"][...] = out_grad
        kept["midway_grad"][...] = midway_grad
        after()
        kept["query_grad"][...] = attend_back(
            mixed_grad,
            kept["attended"][layer],
            kept["query"].at[layer],
            kept["joined"].at[layer],
            kept["probs"].at[layer],
            kept["parts"].at[layer],
            between,
        )
        sums[layer].start()
        return gain_grad

    def end_of_layer(layer, current):
        sums[layer].finish(kept["key_grads"])
        turned, values, gain_grad, grad_in = project_back(
            kept["query_grad"][...],
            kept["key_grads"][...],
            kept["midway_grad"][...],
            current,
            gains_ref[layer, 0:1],
            cos,
            sin,
            weights[layer],
        )
        kept["turned"][...] = turned
        kept["values"][...] = values
        return gain_grad, grad_in

    def prepare_grads(layer):
        grads[layer].prepare(
            kept["normed"][layer],
            kept["normed_two"][layer],
            kept["attended"][layer],
            kept["hidden"][layer],
        )

    def rest_grads(layer):
        grads[layer].rest(
            kept["gate_grad"], kept["up_grad"], kept["down_grad"]
        )

    def projection_grads(layer, attn_gain_grad, mlp_gain_grad):
        grads[layer].projections(
            kept["turned"],
            kept["values"],
            kept["out_grad"],
            attn_gain_grad,
            mlp_gain_grad,
        )

    upper, lower = 0, 1
    come(0, lower, 2)
    come(0, upper)
    come(0, lower)
    come(0, upper)
    come(0, lower)
    come(0, upper)
    come(0, lower)
    come(0, upper)
    come(1, lower)
    come(1, upper)
    come(0, lower)
    come(0, upper)
    come(1, lower)
    come(1, upper)
    come(0, lower, 2)
    come(1, lower)
    come(1, upper)

    x = x_ref[place.section].astype(F32).T
    start_layer(0, x)
    come(1, lower)
    come(1, upper)
    come(0, upper)
    come(1, lower)
    attention_of_layer(0)
    come(0, upper)
    come(1, lower)
    come(1, upper)
    come(0, upper)
    midway, gate, up, result = rest_of_layer(0, x)
    kept["midway"][...] = midway
    kept["gate"][...] = gate
    kept["up"][...] = up
    passed = result.astype(BF16)
    kept["x_2"][...] = passed
    come(1, lower)
    come(1, lower)
    start_layer(1, passed.astype(F32))
    come(1, upper)
    attention_of_layer(1)
    come(1, upper)
    come(1, upper)
    midway, gate, up, result = rest_of_layer(1, kept["x_2"][...].astype(F32))
    finish_edge(1, result.T)

    def nothing():
        pass

    mlp_gain_grad_2 = back_of_layer(
        1, late_ref[place.section].astype(F32).T, midway, gate, up, nothing, [nothing] * 3
    )
    prepare_grads(1)
    sums[1].middle()
    rest_grads(1)
    go(1, upper)
    go(1, upper)
    attn_gain_grad_2, grad_in = end_of_layer(1, kept["x_2"][...].astype(F32))
    projection_grads(1, attn_gain_grad_2, mlp_gain_grad_2)
    go(1, lower)

    def after_feed_forward():
        go(1, lower)
        pl.semaphore_signal(
            credit_sem, inc=1, device_id=place.partner(), device_id_type=MESH
        )
        go(1, upper)
        prepare_grads(0)
        rest_grads(0)
        pl.semaphore_wait(credit_sem, 1)
        go(0, upper)

    mlp_gain_grad_1 = back_of_layer(
        0,
        grad_in.astype(BF16).astype(F32),
        kept["midway"][...],
        kept["gate"][...],
        kept["up"][...],
        after_feed_forward,
        [nothing] * 3,
    )
    go(1, lower)
    sums[0].middle()
    go(0, upper)
    go(1, upper)
    go(1, lower)
    attn_gain_grad_1, grad_in = end_of_layer(0, x_ref[place.section].astype(F32).T)
    projection_grads(0, attn_gain_grad_1, mlp_gain_grad_1)
    go(0, lower)
    go(1, upper)
    go(1, lower)
    go(0, upper)
    finish_edge(0, grad_in.T)
    go(0, lower)
    go(1, upper)
    go(1, lower)
    go(0, lower)
    go(1, upper)
    go(1, lower)
    go(0, upper)
    go(0, lower)
    go(0, upper)
    go(0, lower)
    go(0, upper)
    go(0, lower)
    go(0, upper)
    go(0, lower)
    go(1, upper)
    go(1, lower)
    go(0, upper)
    go(0, lower)
    edge.wait()


def run_layers(x, late, cos, sin, segments, shards):
    edge = jax.ShapeDtypeStruct((D, ROWS), F32)
    summed = jax.ShapeDtypeStruct((PACKED, LANES), F32)
    return pl.pallas_call(
        layers_kernel,
        out_shape=(summed, edge, edge),
        in_specs=[VMEM] * 14,
        out_specs=(VMEM, VMEM, VMEM),
        scratch_shapes=[
            pltpu.SemaphoreType.DMA((4, 8)),
            pltpu.SemaphoreType.DMA((4, 8)),
            pltpu.SemaphoreType.DMA((2, 2, GATHER_SLOTS)),
            pltpu.SemaphoreType.DMA((2, 2, GATHER_SLOTS)),
            pltpu.SemaphoreType.DMA((2, 2, SCATTER_SLOTS)),
            pltpu.SemaphoreType.DMA((2, 2, SCATTER_SLOTS)),
            pltpu.SemaphoreType.DMA((2,)),
            pltpu.SemaphoreType.REGULAR,
            *[pltpu.VMEM(shape, kind) for shape, kind in KEPT.values()],
            *[box for layer in range(2) for part in SCATTER_PARTS for box in scatter_inboxes(part)],
        ],
        compiler_params=params(2),
        name="layers",
    )(x, late, cos, sin, segments, *shards)


def rope_tables(first):
    places = first + jnp.arange(ROWS, dtype=jnp.int32)
    pair_index = jnp.arange(HEAD // 2).astype(F32)
    frequency = rope_base ** (-2.0 * pair_index / HEAD)
    angles = places.astype(F32)[:, None] * frequency[None, :]
    cos, sin = jnp.cos(angles), jnp.sin(angles)
    return jnp.concatenate([cos] * 4, axis=1), jnp.concatenate([-sin, sin] * 2, axis=1)


def local(block_input, cotangent, segment_ids, *shards):
    cos, sin = rope_tables(lax.axis_index("ctx") * ROWS)
    x = block_input[:, 0].transpose(0, 2, 1)
    late = cotangent[:, 0].transpose(0, 2, 1)
    return finish(*run_layers(x, late, cos, sin, segment_ids, shards))


def solution(mesh):
    shard = P("section", ("ctx", "fsdp"))
    matrix = P("section", ("ctx", "fsdp"), None)
    return jax.shard_map(
        local,
        mesh=mesh,
        in_specs=(
            P(None, "fsdp", "ctx", None),
            P(None, "fsdp", "ctx", None),
            P(None, "fsdp", None),
            shard,
            matrix,
            matrix,
            matrix,
            matrix,
            matrix,
            matrix,
            matrix,
            shard,
        ),
        out_specs=(
            P("section", None, "fsdp", "ctx", None),
            shard,
            matrix,
            matrix,
            matrix,
            matrix,
            matrix,
            matrix,
            matrix,
            shard,
        ),
        check_vma=False,
    )
```

```python
import functools

import jax
import jax.numpy as jnp
from jax import lax
from jax.experimental import pallas as pl
from jax.experimental.pallas import tpu as pltpu
from jax.sharding import PartitionSpec as P

MESH = pl.DeviceIdType.MESH
F32 = jnp.float32
BF16 = jnp.bfloat16
ANY = pl.BlockSpec(memory_space=pl.ANY)
VMEM = pl.BlockSpec(memory_space=pltpu.VMEM)

D = 576
FF = 1536
KVD = 192
HEAD = 64
GROUP = 3
KV_HEADS = 3
ROWS = 128
SEQ = 1024
LANES = 128

norm_eps = 1e-05
rope_base = 100000.0
masked_score = -1e30

WIDE = 4608
GATE_AT = 768
UP_AT = GATE_AT + FF
OUT_AT = UP_AT + FF
VALUE_AT = OUT_AT + D
TAIL_AT = VALUE_AT - HEAD
BLOCKS = WIDE // LANES

DOWN_ROWS = 24
TAIL_ROW = 4 * DOWN_ROWS
UPPER_ROW = 112
LOWER_ROW = 368
PACKED = 448
UPPER = tuple(range(6, 34))
LOWER = tuple(range(6)) + (34, 35)
GAIN_ROW = LOWER_ROW + 9 * len(LOWER)
GAIN_TILE = 432
EARLY = 4 * LANES


def packed_row(column):
    if column in UPPER:
        return UPPER_ROW + 9 * UPPER.index(column)
    return LOWER_ROW + 9 * LOWER.index(column)


GATHER_PARTS = (
    ((0, 368), (((0, 160), "xy"), ((160, 208), "yx"))),
    ((368, 80), (((368, 48), "xy"), ((416, 32), "yx"))),
)
SCATTER_PARTS = (
    ((0, 112), (((0, 48), "yx"), ((48, 64), "xy"))),
    ((112, 256), (((112, 112), "yx"), ((224, 144), "xy"))),
    ((368, 80), (((368, 48), "yx"), ((416, 32), "xy"))),
)
SCATTER_DIRECT = (((), (1,), (0, 1)), ((), (), (0, 1)))
VMEM_BYTES = 63 * 1024 * 1024


def params(collective_id=None):
    if collective_id is None:
        return pltpu.CompilerParams(vmem_limit_bytes=VMEM_BYTES)
    return pltpu.CompilerParams(
        vmem_limit_bytes=VMEM_BYTES, collective_id=collective_id, has_side_effects=True
    )


def dot(left, right):
    return jnp.dot(left, right, preferred_element_type=F32)


def dot_nt(left, right):
    return lax.dot_general(left, right, (((1,), (1,)), ((), ())), preferred_element_type=F32)


def dot_tn(left, right):
    return lax.dot_general(left, right, (((0,), (0,)), ((), ())), preferred_element_type=F32)


class Place:
    def __init__(self):
        self.section = lax.axis_index("section")
        ctx = lax.axis_index("ctx")
        fsdp = lax.axis_index("fsdp")
        self.core = lax.rem(ctx, 2)
        self.at = {
            "x": lax.rem(fsdp, 4),
            "y": ctx // 2,
            "z": self.section * 2 + fsdp // 4,
        }

    def device(self, core=None, **moved):
        at = dict(self.at, **moved)
        core = self.core if core is None else core
        return (at["z"] // 2, at["y"] * 2 + core, lax.rem(at["z"], 2) * 4 + at["x"])

    def shifted(self, axis, step):
        return lax.rem(self.at[axis] + step + 4, 4)

    def neighbour(self, axis, step):
        return self.device(**{axis: self.shifted(axis, step)})

    def partner(self):
        return self.device(core=1 - self.core)


def greet(devices):
    barrier = pltpu.get_barrier_semaphore()
    for device in devices:
        pl.semaphore_signal(barrier, inc=1, device_id=device, device_id_type=MESH)
    pl.semaphore_wait(barrier, len(devices))


def halves(rows):
    first, count = rows
    upper = (count // 2 + 15) // 16 * 16
    return (first, upper), (first + upper, count - upper)


def layer_region(ref, layer, coords, whole, rows, core):
    y = slice(None) if "y" in whole else coords["y"]
    x = slice(None) if "x" in whole else coords["x"]
    return ref.at[layer, y, core, :, x, pl.ds(*rows)]


GATHER_SLOTS = 3 + 2 * 2 * 4 + 2 * 4
WAYS = (1, -1, 2)


def gather_steps(place, layer, part, direct, held, send_sems, recv_sems):
    core = place.core
    all_rows, chunks = part
    plane = lax.rem(place.at["z"] + 4 - 2 * layer, 4)

    def copy(slot, ref, device):
        return pltpu.make_async_remote_copy(
            src_ref=ref,
            dst_ref=ref,
            send_sem=send_sems.at[slot],
            recv_sem=recv_sems.at[slot],
            device_id=device,
            device_id_type=MESH,
        )

    def across(z_lo, slot):
        shard = held.at[layer, place.at["y"], core, z_lo, place.at["x"], pl.ds(*all_rows)]
        return copy(slot, shard, place.neighbour("z", WAYS[slot]))

    for source in range(2):

        @pl.when(plane == source)
        def _():
            for slot in range(3):
                across(source, slot).start()

    yield

    @pl.when((plane == 1) | (plane == 2))
    def _():
        across(0, 0).wait_recv()

    @pl.when((plane == 0) | (plane == 3))
    def _():
        across(0, 1).wait_recv()

    @pl.when(plane >= 2)
    def _():
        across(0, 2).wait_recv()

    counter = [3]
    sent = []
    to_partner = []

    def send(ref, device):
        made = copy(counter[0], ref, device)
        counter[0] += 1
        made.start()
        sent.append(made)
        return made

    for phase in range(2):
        one_step = phase in direct
        first, second = [], []
        for rows, order in chunks:
            axis, whole = order[phase], order[:phase]
            block = layer_region(held, layer, place.at, whole, rows, core)
            ways = WAYS if one_step else WAYS[:2]
            first.append([send(block, place.neighbour(axis, way)) for way in ways])
            if phase == 1:
                to_partner.append(send(block, place.partner()))
        yield
        for copies, (rows, order) in zip(first, chunks):
            axis, whole = order[phase], order[:phase]
            for made in copies:
                made.wait_recv()
            left = dict(place.at, **{axis: place.shifted(axis, -1)})
            right = dict(place.at, **{axis: place.shifted(axis, 1)})
            far = dict(place.at, **{axis: place.shifted(axis, 2)})
            if not one_step:
                upper, lower = halves(rows)
                second += [
                    send(
                        layer_region(held, layer, left, whole, upper, core),
                        place.neighbour(axis, 1),
                    ),
                    send(
                        layer_region(held, layer, right, whole, lower, core),
                        place.neighbour(axis, -1),
                    ),
                ]
            if phase == 1:
                for coords in (left, right, far) if one_step else (left, right):
                    to_partner.append(
                        send(layer_region(held, layer, coords, whole, rows, core), place.partner())
                    )
        if not one_step:
            yield
            for made in second:
                made.wait_recv()
    if 1 not in direct:
        for rows, order in chunks:
            axis, whole = order[1], order[:1]
            far = dict(place.at, **{axis: place.shifted(axis, 2)})
            to_partner.append(
                send(layer_region(held, layer, far, whole, rows, core), place.partner())
            )
    yield
    for made in to_partner:
        made.wait_recv()
    for made in sent:
        made.wait_send()

    @pl.when(plane <= 1)
    def _():
        for slot in range(3):
            across(0, slot).wait_send()

    yield


SCATTER_SLOTS = 1 + 2 * 2 * 4 + 3


def scatter_inboxes(part):
    (first, count), chunks = part
    boxes = []
    for (_, rows), order in chunks:
        others = (2, 4) if order == "yx" else (4, 2)
        boxes.append(pltpu.VMEM((3, *others, rows, LANES), BF16))
        boxes.append(pltpu.VMEM((3, 2, rows, LANES), BF16))
    boxes.append(pltpu.VMEM((3, count, LANES), BF16))
    return boxes


def scatter_steps(place, layer, part, direct, held, boxes, send_sems, recv_sems, out_ref):
    core = place.core
    here_y, here_x = place.at["y"], place.at["x"]
    (first, count), chunks = part
    counter = [0]
    sent = []

    def copy(source, target, device):
        slot = counter[0]
        counter[0] += 1
        return pltpu.make_async_remote_copy(
            src_ref=source,
            dst_ref=target,
            send_sem=send_sems.at[slot],
            recv_sem=recv_sems.at[slot],
            device_id=device,
            device_id_type=MESH,
        )

    def send(source, target, device):
        made = copy(source, target, device)
        made.start()
        sent.append(made)
        return made

    def add(spot, source, rows):
        held[spot] = (held[spot].astype(F32) + source().astype(F32)).astype(BF16)

    all_rows = pl.ds(first, count)
    swap = copy(
        held.at[layer, :, 1 - core, :, :, all_rows],
        held.at[1 - layer, :, core, :, :, all_rows],
        place.partner(),
    )
    swap.start()
    yield
    swap.wait()

    def add_swapped(step, carry):
        y, z_lo, x = step // 8, lax.rem(step // 4, 2), lax.rem(step, 4)
        add(
            (layer, y, core, z_lo, x, all_rows),
            lambda: held[1 - layer, y, 1 - core, z_lo, x, all_rows],
            count,
        )
        return carry

    lax.fori_loop(0, 32, add_swapped, 0)

    def add_block(phase, axis, coords, rows, box, slot):
        at, size = rows

        def in_box(begin):
            return pl.ds(begin, size)

        begin = 0 if slot else at[1]
        here = pl.ds(at[0], size)
        if phase == 0:

            def body(step, carry):
                if axis == "y":
                    z_lo, x = step // 4, lax.rem(step, 4)
                    spot = (layer, coords["y"], core, z_lo, x, here)
                    add(spot, lambda: box[slot, z_lo, x, in_box(begin)], size)
                else:
                    y, z_lo = step // 2, lax.rem(step, 2)
                    spot = (layer, y, core, z_lo, coords["x"], here)
                    add(spot, lambda: box[slot, y, z_lo, in_box(begin)], size)
                return carry

            lax.fori_loop(0, 8, body, 0)
        else:
            for z_lo in range(2):
                spot = (layer, coords["y"], core, z_lo, coords["x"], here)
                add(spot, lambda: box[slot, z_lo, in_box(begin)], size)

    flights = [[], []]

    def land(flight):
        for made, phase, axis, lands, spot_rows, box, slot in flight:
            made.wait_recv()
            add_block(phase, axis, lands, spot_rows, box, slot)

    for phase in range(2):
        one_step = phase in direct
        for step in range(1 if one_step else 2):
            for i, (rows, order) in enumerate(chunks):
                box = boxes[2 * i + phase]
                land(flights[i])
                axis, whole = order[phase], order[phase + 1 :]
                right = dict(place.at, **{axis: place.shifted(axis, 1)})
                left = dict(place.at, **{axis: place.shifted(axis, -1)})
                far = dict(place.at, **{axis: place.shifted(axis, 2)})
                upper, lower = halves(rows)
                if one_step:
                    plan = (
                        (right, rows, 1, place.at, 0),
                        (left, rows, -1, place.at, 1),
                        (far, rows, 2, place.at, 2),
                    )
                elif step == 0:
                    plan = ((far, upper, 1, right, 0), (far, lower, -1, left, 0))
                else:
                    plan = ((right, rows, 1, place.at, 1), (left, rows, -1, place.at, 2))
                flights[i] = []
                for source_at, part_rows, way, lands, slot in plan:
                    begin = part_rows[0] - rows[0]
                    lead = (slice(None),) * (2 if phase == 0 else 1)
                    made = send(
                        layer_region(held, layer, source_at, whole, part_rows, core),
                        box.at[(slot, *lead, pl.ds(begin, part_rows[1]))],
                        place.neighbour(axis, way),
                    )
                    flights[i].append(
                        (made, phase, axis, lands, ((part_rows[0], begin), part_rows[1]), box, slot)
                    )
            yield
    for flight in flights:
        land(flight)

    plane = lax.rem(place.at["z"] + 4 - 2 * layer, 4)
    stays = lax.rem(plane, 2)
    box = boxes[4]
    shards = ((3 - plane) // 3, plane // 2, lax.rem(plane, 2))
    senders = ((plane == 0) | (plane == 3), (plane == 1) | (plane == 2), plane >= 2)
    last = [
        copy(
            held.at[layer, here_y, core, z_lo, here_x, all_rows],
            box.at[i],
            place.neighbour("z", WAYS[i]),
        )
        for i, z_lo in enumerate(shards)
    ]
    for made, sender in zip(last, senders):
        pl.when(sender)(made.start)
    yield

    @pl.when(plane < 2)
    def _():
        for made in last:
            made.wait_recv()
        total = held[layer, here_y, core, stays, here_x, all_rows].astype(F32)
        for i in range(3):
            total += box[i].astype(F32)
        out_ref[all_rows] = total

    for made in sent:
        made.wait_send()
    for made, sender in zip(last, senders):
        pl.when(sender)(made.wait_send)
    yield


class Exchange:
    def __init__(self, place, send_sems, recv_sems):
        self.place = place
        self.send_sems = send_sems
        self.recv_sems = recv_sems

    def copy(self, slot, source, target, device):
        return pltpu.make_async_remote_copy(
            src_ref=source,
            dst_ref=target,
            send_sem=self.send_sems.at[slot],
            recv_sem=self.recv_sems.at[slot],
            device_id=device,
            device_id_type=MESH,
        )

    def along_y(self, step):
        return self.place.device(y=lax.rem(self.place.at["y"] + step + 4, 4))


class KeyGather(Exchange):
    def __init__(self, place, keys_ref, send_sems, recv_sems):
        super().__init__(place, send_sems, recv_sems)
        self.keys_ref = keys_ref

    def direct(self, away):
        own = self.keys_ref.at[self.place.at["y"] * 2 + self.place.core]
        return self.copy(away, own, own, self.along_y(away))

    def passed_on(self, away):
        block = self.keys_ref.at[
            lax.rem(self.place.at["y"] - away + 4, 4) * 2 + self.place.core
        ]
        return self.copy(4 + away, block, block, self.place.partner())

    def start(self):
        y = self.place.at["y"]
        for away in (1, 3, 2):

            @pl.when(y + away < 4)
            def _():
                self.direct(away).start()

        self.passed_on(0).start()
        for away in range(1, 4):

            @pl.when(y + away < 4)
            def _():
                self.keys_ref[pl.ds((y + away) * 2, 2)] = jnp.zeros(
                    (2,) + self.keys_ref.shape[1:], self.keys_ref.dtype
                )

    def pass_on(self):
        y = self.place.at["y"]
        for away in (1, 3, 2):

            @pl.when(y - away >= 0)
            def _():
                self.direct(away).wait_recv()
                self.passed_on(away).start()

    def finish(self):
        y = self.place.at["y"]
        self.passed_on(0).wait()
        for away in range(1, 4):

            @pl.when(y - away >= 0)
            def _():
                self.passed_on(away).wait()

            @pl.when(y + away < 4)
            def _():
                self.direct(away).wait_send()


class KeyGradSum(Exchange):
    def __init__(self, place, parts_ref, pair_ref, ring_ref, send_sems, recv_sems):
        super().__init__(place, send_sems, recv_sems)
        self.parts_ref = parts_ref
        self.pair_ref = pair_ref
        self.ring_ref = ring_ref

    def swap(self):
        return self.copy(
            0, self.parts_ref.at[1 - self.place.core], self.pair_ref, self.place.partner()
        )

    def direct(self, away):
        y = lax.rem(self.place.at["y"] - away + 4, 4)
        return self.copy(
            away,
            self.parts_ref.at[self.place.core, y],
            self.ring_ref.at[away - 1],
            self.along_y(-away),
        )

    def start(self):
        self.swap().start()

    def middle(self):
        self.swap().wait()
        core = self.place.core
        for y in range(4):
            self.parts_ref[core, y] = (
                self.parts_ref[core, y].astype(F32) + self.pair_ref[y].astype(F32)
            ).astype(BF16)
        for away in (1, 3, 2):

            @pl.when(self.place.at["y"] - away >= 0)
            def _():
                self.direct(away).start()

    def finish(self, out_ref):
        y = self.place.at["y"]
        out_ref[...] = self.parts_ref[self.place.core, y].astype(F32)
        for away in range(1, 4):

            @pl.when(y + away < 4)
            def _():
                self.direct(away).wait_recv()
                out_ref[...] += self.ring_ref[away - 1].astype(F32)

        for away in range(1, 4):

            @pl.when(y - away >= 0)
            def _():
                self.direct(away).wait_send()


def packed_shard(attn_ref, query_ref, key_ref, value_ref, w_out_ref, gate_ref, up_ref, down_ref, mlp_ref):
    def wide(ref):
        return ref[0].astype(F32)

    joined = jnp.concatenate(
        [wide(r) for r in (query_ref, key_ref, gate_ref, up_ref, w_out_ref, value_ref)], axis=1
    )
    down = wide(down_ref)
    pieces = [down[:, i * LANES : (i + 1) * LANES] for i in range(4)]
    half = DOWN_ROWS // 2
    pieces.append(jnp.concatenate([down[:half, 4 * LANES :], down[half:, 4 * LANES :]], axis=1))
    pieces.append(jnp.zeros((4, LANES), F32))
    pieces += [joined[:, i * LANES : (i + 1) * LANES] for i in UPPER]
    pieces.append(jnp.zeros((4, LANES), F32))
    pieces += [joined[:, i * LANES : (i + 1) * LANES] for i in LOWER]
    for ref in (attn_ref, mlp_ref):
        gain = ref[...].astype(F32)
        pieces.append(jnp.concatenate([gain, jnp.zeros((1, LANES - 9), F32)], axis=1))
    pieces.append(jnp.zeros((PACKED - GAIN_ROW - 2, LANES), F32))
    return jnp.concatenate(pieces, axis=0).astype(BF16)


def gain_masks(first_device, devices, rows_each, rows):
    shape = (devices * rows_each, D)
    row = lax.broadcasted_iota(jnp.int32, shape, 0)
    owner = lax.broadcasted_iota(jnp.int32, shape, 1) // 9
    same = owner == first_device + row // rows_each
    place = lax.rem(row, rows_each)
    return [same & (place == at) for at in rows]


def lane_spread():
    lane = lax.broadcasted_iota(jnp.int32, (LANES, D), 0)
    feature = lax.broadcasted_iota(jnp.int32, (LANES, D), 1)
    return (lane == lax.rem(feature, 9)).astype(BF16)


def packed_rows(held, layer, y, first, count):
    start = first // 16 * 16
    size = (first + count + 15) // 16 * 16 - start
    return [
        held[layer, y, core, z_lo, x, start : start + size].astype(F32)[
            first - start : first - start + count
        ]
        for core in range(2)
        for z_lo in range(2)
        for x in range(4)
    ]


def unpack_wide(held, layer, columns, wide):
    def body(y, carry):
        rows = pl.ds(pl.multiple_of(y * 144, 16), 144)
        for column in columns:
            wide[layer, rows, column * LANES : (column + 1) * LANES] = jnp.concatenate(
                packed_rows(held, layer, y, packed_row(column), 9), axis=0
            ).astype(BF16)
        return carry

    lax.fori_loop(0, 4, body, 0)


def unpack_down(held, layer, down):
    def body(y, carry):
        rows = pl.ds(pl.multiple_of(y * 384, 16), 384)
        for column in range(4):
            down[layer, rows, column * LANES : (column + 1) * LANES] = jnp.concatenate(
                packed_rows(held, layer, y, DOWN_ROWS * column, DOWN_ROWS), axis=0
            ).astype(BF16)
        tails = []
        for tail in packed_rows(held, layer, y, TAIL_ROW, DOWN_ROWS // 2):
            tails += [tail[:, :HEAD], tail[:, HEAD:]]
        down[layer, rows, 4 * LANES :] = jnp.concatenate(tails, axis=0).astype(BF16)
        return carry

    lax.fori_loop(0, 4, body, 0)


def unpack_gains(held, layer, gains):
    totals = [jnp.zeros((1, D), F32)] * 2
    spread_to = lane_spread()
    for y in range(4):
        rows = held[layer, y, :, :, :, GAIN_TILE:, :].reshape(16 * 16, LANES)
        spread = dot(rows, spread_to)
        at = GAIN_ROW - GAIN_TILE
        masks = gain_masks(y * 16, 16, 16, (at, at + 1))
        totals = [
            total + jnp.sum(jnp.where(mask, spread, 0.0), axis=0, keepdims=True)
            for total, mask in zip(totals, masks)
        ]
    gains[layer, 0:1] = totals[0]
    gains[layer, 1:2] = totals[1]


def finish_kernel(
    all_ref,
    edges_ref,
    attn_ref,
    query_ref,
    key_ref,
    value_ref,
    w_out_ref,
    gate_ref,
    up_ref,
    down_ref,
    mlp_ref,
):
    section = lax.axis_index("section")
    edges_ref[0, section, 0] = all_ref[PACKED : PACKED + D]
    edges_ref[0, 1 - section, 0] = all_ref[PACKED + D :]
    packed = all_ref[:PACKED]
    joined = jnp.concatenate(
        [packed[packed_row(i) : packed_row(i) + 9] for i in range(BLOCKS)], axis=1
    )
    query_ref[:, 0] = joined[:, :D]
    key_ref[:, 0] = joined[:, D:GATE_AT]
    gate_ref[:, 0] = joined[:, GATE_AT:UP_AT]
    up_ref[:, 0] = joined[:, UP_AT:OUT_AT]
    w_out_ref[:, 0] = joined[:, OUT_AT:VALUE_AT]
    value_ref[:, 0] = joined[:, VALUE_AT:]
    tail = packed[TAIL_ROW : TAIL_ROW + DOWN_ROWS // 2]
    down_ref[0] = jnp.concatenate(
        [packed[DOWN_ROWS * i : DOWN_ROWS * (i + 1)] for i in range(4)]
        + [jnp.concatenate([tail[:, :HEAD], tail[:, HEAD:]], axis=0)],
        axis=1,
    )
    at = GAIN_ROW
    attn_ref[...] = packed[at : at + 1, :9]
    mlp_ref[...] = packed[at + 1 : at + 2, :9]


def finish(rows):
    shapes = (
        (1, 2, 1, D, ROWS),
        (1, 9),
        (9, 1, D),
        (9, 1, KVD),
        (9, 1, KVD),
        (9, 1, D),
        (9, 1, FF),
        (9, 1, FF),
        (1, DOWN_ROWS, D),
        (1, 9),
    )
    edges, attn, *wide, down, mlp = pl.pallas_call(
        finish_kernel,
        out_shape=tuple(jax.ShapeDtypeStruct(shape, F32) for shape in shapes),
        in_specs=[VMEM],
        out_specs=(VMEM,) * len(shapes),
        compiler_params=params(),
        name="finish",
    )(rows)
    wide = [grad.transpose(1, 0, 2) for grad in wide]
    return (edges.transpose(0, 1, 2, 4, 3), attn, *wide, down, mlp)


def swap_halves(block):
    lane = lax.broadcasted_iota(jnp.int32, block.shape, 1)
    return jnp.where(
        lax.rem(lane, HEAD) < HEAD // 2,
        pltpu.roll(block, LANES - HEAD // 2, 1),
        pltpu.roll(block, HEAD // 2, 1),
    )


def rotated(block, cos, sin):
    return block * cos + swap_halves(block) * sin


def project(current, gain, weights, cos, sin, normed_ref, query_ref):
    scale = lax.rsqrt(jnp.mean(current * current, axis=1, keepdims=True) + norm_eps)
    normed = (current * scale * gain).astype(BF16)
    normed_ref[...] = normed
    raw = dot(normed, weights.get("qk"))
    turned = [
        rotated(raw[:, i * LANES : (i + 1) * LANES], cos, sin).astype(BF16) for i in range(6)
    ]
    for i in range(4):
        query_ref[:, i * LANES : (i + 1) * LANES] = turned[i]
    query_ref[:, 4 * LANES :] = turned[4][:, :HEAD]
    values = dot(normed, weights.get("tail"))[:, HEAD:]
    return jnp.concatenate(
        [turned[4][:, HEAD:].astype(F32), turned[5].astype(F32), values], axis=1
    ).astype(BF16)


def heads_of(rows, group):
    return jnp.concatenate(
        [rows[:, (group * GROUP + r) * HEAD : (group * GROUP + r + 1) * HEAD] for r in range(GROUP)],
        axis=0,
    )


def attend(query_ref, keys_ref, seg_row, probs_ref):
    first = lax.axis_index("ctx") * ROWS
    rows = first + lax.broadcasted_iota(jnp.int32, (ROWS, SEQ), 0)
    columns = lax.broadcasted_iota(jnp.int32, (ROWS, SEQ), 1)
    own_seg = jnp.sum(jnp.where(columns == rows, seg_row, 0), axis=1, keepdims=True)
    allowed = (columns <= rows) & (seg_row == own_seg)
    bias = jnp.where(allowed, 0.0, masked_score)
    bias = jnp.concatenate([bias] * GROUP, axis=0)
    queries = query_ref[...]
    mixed = []
    for group in range(KV_HEADS):
        keys = keys_ref[:, :, group * HEAD : (group + 1) * HEAD].reshape(SEQ, HEAD)
        values = keys_ref[:, :, KVD + group * HEAD : KVD + (group + 1) * HEAD].reshape(SEQ, HEAD)
        scores = dot_nt(heads_of(queries, group), keys) * HEAD**-0.5 + bias
        shifted = jnp.exp(scores - jnp.max(scores, axis=1, keepdims=True))
        probs = (shifted / jnp.sum(shifted, axis=1, keepdims=True)).astype(BF16)
        probs_ref[group] = probs
        mixture = dot(probs, values)
        mixed += [mixture[r * ROWS : (r + 1) * ROWS] for r in range(GROUP)]
    return jnp.concatenate(mixed, axis=1).astype(BF16)


def feed_forward(current, attended, gain, weights):
    midway = current + dot(attended, weights.get("out"))
    scale = lax.rsqrt(jnp.mean(midway * midway, axis=1, keepdims=True) + norm_eps)
    normed = (midway * scale * gain).astype(BF16)
    gate = dot(normed, weights.get("gate"))
    up = dot(normed, weights.get("up"))
    hidden = (gate / (1.0 + jnp.exp(-gate)) * up).astype(BF16)
    result = midway + dot(hidden, weights.get("down"))
    return midway, scale, normed, gate, up, hidden, result


def norm_backward(scaled, values, scale):
    return scale * scaled - values * scale**3 * jnp.mean(scaled * values, axis=1, keepdims=True)


def feed_forward_back(
    incoming, midway, gate, up, gain, weights
):
    scale = lax.rsqrt(jnp.mean(midway * midway, axis=1, keepdims=True) + norm_eps)
    down_grad = incoming.astype(BF16)
    hidden_grad = dot_nt(down_grad, weights.get("down"))
    sigmoid = 1.0 / (1.0 + jnp.exp(-gate))
    gate_grad = (hidden_grad * up * sigmoid * (1.0 + gate * (1.0 - sigmoid))).astype(BF16)
    up_grad = (hidden_grad * gate * sigmoid).astype(BF16)
    normed_grad = dot_nt(gate_grad, weights.get("gate")) + dot_nt(
        up_grad, weights.get("up")
    )
    gain_grad = jnp.sum(normed_grad * midway * scale, axis=0, keepdims=True)
    midway_grad = incoming + norm_backward(normed_grad * gain, midway, scale)
    out_grad = midway_grad.astype(BF16)
    mixed_grad = dot_nt(out_grad, weights.get("out")).astype(BF16)
    return down_grad, gate_grad, up_grad, gain_grad, midway_grad, out_grad, mixed_grad


def attend_back(mixed_grad, attended, query_ref, keys_ref, probs_ref, parts_ref, between):
    queries = query_ref[...]
    query_grads = []
    for group in range(KV_HEADS):
        keys = keys_ref[:, :, group * HEAD : (group + 1) * HEAD].reshape(SEQ, HEAD)
        values = keys_ref[:, :, KVD + group * HEAD : KVD + (group + 1) * HEAD].reshape(SEQ, HEAD)
        grads = heads_of(mixed_grad, group)
        delta = jnp.sum(
            grads.astype(F32) * heads_of(attended, group).astype(F32), axis=1, keepdims=True
        )
        probs = probs_ref[group]
        score_grad = (probs.astype(F32) * (dot_nt(grads, values) - delta)).astype(BF16)
        query_grad = dot(score_grad, keys) * HEAD**-0.5
        query_grads += [query_grad[r * ROWS : (r + 1) * ROWS] for r in range(GROUP)]
        key_part = (dot_tn(heads_of(queries, group), score_grad) * HEAD**-0.5).astype(BF16)
        value_part = dot_tn(grads, probs).astype(BF16)
        for block in range(8):
            columns = slice(block * ROWS, (block + 1) * ROWS)
            at = (block % 2, block // 2)
            parts_ref[*at, group * HEAD : (group + 1) * HEAD] = key_part[:, columns]
            parts_ref[*at, KVD + group * HEAD : KVD + (group + 1) * HEAD] = value_part[:, columns]
        between[group]()
    return jnp.concatenate(query_grads, axis=1)


def project_back(
    query_grad, key_grads, midway_grad, current, gain, cos, sin, weights
):
    key_grads = key_grads.T
    joined = jnp.concatenate([query_grad, key_grads[:, :KVD]], axis=1)
    turned = jnp.concatenate(
        [rotated(joined[:, i * LANES : (i + 1) * LANES], cos, -sin) for i in range(6)], axis=1
    ).astype(BF16)
    values = key_grads[:, KVD:].astype(BF16)
    padded = jnp.concatenate([jnp.zeros((ROWS, HEAD), F32), key_grads[:, KVD:]], axis=1)
    normed_grad = dot_nt(turned, weights.get("qk")) + dot_nt(
        padded.astype(BF16), weights.get("tail")
    )
    scale = lax.rsqrt(jnp.mean(current * current, axis=1, keepdims=True) + norm_eps)
    gain_grad = jnp.sum(normed_grad * current * scale, axis=0, keepdims=True)
    grad_in = midway_grad + norm_backward(normed_grad * gain, current, scale)
    return turned, values, gain_grad, grad_in


GRAD_DEVICES = 16


def transposed(rows):
    return rows.astype(F32).T.astype(BF16)


class WeightGrads:
    def __init__(self, packed, stages, gain_rows, lhs, hidden_lhs):
        self.packed = packed
        self.first, self.second, self.third = stages
        self.gain_rows = gain_rows
        self.lhs = lhs
        self.hidden_lhs = hidden_lhs

    def place(self, stage, first_row, column, product):
        for i in range(product.shape[1] // LANES):
            at = packed_row(column + i) - first_row
            part = product[:, i * LANES : (i + 1) * LANES]
            for d in range(GRAD_DEVICES):
                stage[d, at : at + 9] = part[9 * d : 9 * d + 9]

    def rows(self, step, each):
        return pl.ds(pl.multiple_of(step * each * GRAD_DEVICES, 16), each * GRAD_DEVICES)

    def round(self, stage, y, first_row):
        rounded = stage[...].astype(BF16)
        self.packed[y, :, :, :, first_row : first_row + stage.shape[1]] = rounded.reshape(
            (2, 2, 4) + rounded.shape[1:]
        )

    def down(self, hidden, down_grad):
        half = DOWN_ROWS // 2
        self.hidden_lhs[...] = transposed(hidden)
        self.first[:, TAIL_ROW + half :] = jnp.zeros((GRAD_DEVICES, 4, LANES), F32)

        def body(y, carry):
            product = dot(self.hidden_lhs[self.rows(y, DOWN_ROWS)], down_grad)
            for d in range(GRAD_DEVICES):
                own = product[DOWN_ROWS * d : DOWN_ROWS * (d + 1)]
                for i in range(4):
                    self.first[d, DOWN_ROWS * i : DOWN_ROWS * (i + 1)] = own[
                        :, i * LANES : (i + 1) * LANES
                    ]
                self.first[d, TAIL_ROW : TAIL_ROW + half] = jnp.concatenate(
                    [own[:half, 4 * LANES :], own[half:, 4 * LANES :]], axis=1
                )
            self.round(self.first, y, 0)
            return carry

        lax.fori_loop(0, 64 // GRAD_DEVICES, body, 0)

    def middle(self, normed_two, attended, gate_grad_ref, up_grad_ref, out_grad_ref):
        self.lhs[1] = transposed(normed_two)
        self.lhs[2] = transposed(attended)
        self.second[:, 9 * len(UPPER) :] = jnp.zeros((GRAD_DEVICES, 4, LANES), F32)

        def body(y, carry):
            second = self.lhs[1, self.rows(y, 9)]
            self.place(self.second, UPPER_ROW, GATE_AT // LANES, dot(second, gate_grad_ref[...]))
            self.place(self.second, UPPER_ROW, UP_AT // LANES, dot(second, up_grad_ref[...]))
            third = self.lhs[2, self.rows(y, 9)]
            self.place(
                self.second, UPPER_ROW, OUT_AT // LANES, dot(third, out_grad_ref[:, :EARLY])
            )
            self.round(self.second, y, UPPER_ROW)
            return carry

        lax.fori_loop(0, 64 // GRAD_DEVICES, body, 0)

    def late(self, normed, turned_ref, values_ref, out_grad_ref, attn_gain_grad, mlp_gain_grad):
        self.lhs[0] = transposed(normed)
        spread_to = lane_spread()
        (mask,) = gain_masks(0, 64, 1, (0,))
        for i, gain_grad in enumerate((attn_gain_grad, mlp_gain_grad)):
            chosen = jnp.where(mask, gain_grad, 0.0).astype(BF16)
            self.gain_rows[i] = dot_nt(chosen, spread_to)
        self.third[:, GAIN_ROW + 2 - LOWER_ROW :] = jnp.zeros(
            (GRAD_DEVICES, PACKED - GAIN_ROW - 2, LANES), F32
        )

        def body(y, carry):
            first = self.lhs[0, self.rows(y, 9)]
            self.place(self.third, LOWER_ROW, 0, dot(first, turned_ref[...]))
            third = self.lhs[2, self.rows(y, 9)]
            self.place(
                self.third,
                LOWER_ROW,
                (OUT_AT + EARLY) // LANES,
                jnp.concatenate(
                    [dot(third, out_grad_ref[:, EARLY:]), dot(first, values_ref[...])], axis=1
                ),
            )
            for i in range(2):
                gains = self.gain_rows[i, self.rows(y, 1)]
                for d in range(GRAD_DEVICES):
                    at = GAIN_ROW + i - LOWER_ROW
                    self.third[d, at : at + 1] = gains[d : d + 1]
            self.round(self.third, y, LOWER_ROW)
            return carry

        lax.fori_loop(0, 64 // GRAD_DEVICES, body, 0)


COLUMNS = {
    "qk": (0, GATE_AT),
    "gate": (GATE_AT, UP_AT),
    "up": (UP_AT, OUT_AT),
    "out": (OUT_AT, VALUE_AT),
    "tail": (TAIL_AT, WIDE),
}


class Weights:
    def __init__(self, layer, wide, down):
        self.layer = layer
        self.wide = wide
        self.down = down

    def get(self, name):
        if name == "down":
            return self.down[self.layer]
        first, end = COLUMNS[name]
        return self.wide[self.layer, :, first:end]


ROW = (ROWS, D)
KEPT = {
    "joined": ((2, 8, ROWS, 2 * KVD), BF16),
    "probs": ((2, KV_HEADS, GROUP * ROWS, SEQ), BF16),
    "parts": ((2, 2, 4, 2 * KVD, ROWS), BF16),
    "pair": ((4, 2 * KVD, ROWS), BF16),
    "ring": ((2, 3, 2 * KVD, ROWS), BF16),
    "key_grads": ((2 * KVD, ROWS), F32),
    "normed": ((2, *ROW), BF16),
    "query": ((2, *ROW), BF16),
    "attended": ((2, *ROW), BF16),
    "normed_two": ((2, *ROW), BF16),
    "hidden": ((2, ROWS, FF), BF16),
    "midway": (ROW, F32),
    "gate": ((ROWS, FF), F32),
    "up": ((ROWS, FF), F32),
    "x_2": (ROW, BF16),
    "gate_grad": ((ROWS, FF), BF16),
    "up_grad": ((ROWS, FF), BF16),
    "down_grad": (ROW, BF16),
    "out_grad": (ROW, BF16),
    "midway_grad": (ROW, F32),
    "query_grad": (ROW, F32),
    "turned": ((ROWS, D + KVD), BF16),
    "values": ((ROWS, KVD), BF16),
    "lhs": ((3, D, ROWS), BF16),
    "hidden_lhs": ((FF, ROWS), BF16),
    "first": ((GRAD_DEVICES, UPPER_ROW, LANES), F32),
    "second": ((GRAD_DEVICES, LOWER_ROW - UPPER_ROW, LANES), F32),
    "third": ((GRAD_DEVICES, PACKED - LOWER_ROW, LANES), F32),
    "gain_rows": ((2, 64, LANES), F32),
    "held": ((2, 4, 2, 2, 4, PACKED, LANES), BF16),
    "wide": ((2, D, WIDE), BF16),
    "down": ((2, FF, D), BF16),
    "gains": ((2, 8, D), F32),
    "edge": ((D, ROWS), F32),
}


def layers_kernel(
    x_ref,
    late_ref,
    cos_ref,
    sin_ref,
    seg_ref,
    *rest,
):
    shards = rest[:9]
    out_ref = rest[9]
    summed_ref = out_ref.at[:PACKED]
    stays_ref = out_ref.at[PACKED : PACKED + D]
    came_ref = out_ref.at[PACKED + D :]
    send_sems, recv_sems, gather_send, gather_recv, scatter_send, scatter_recv, edge_sems, credits, *scratch = (
        rest[10:]
    )
    place = Place()
    kept = dict(zip(KEPT, scratch))
    boxes = scratch[len(KEPT) :]
    held, gains_ref = kept["held"], kept["gains"]
    weights = [Weights(i, kept["wide"], kept["down"]) for i in range(2)]
    held[
        place.section, place.at["y"], place.core, lax.rem(place.at["z"], 2), place.at["x"]
    ] = packed_shard(*shards)
    greet(
        [place.partner()]
        + [place.neighbour(axis, way) for axis in "xz" for way in (1, -1)]
        + [place.device(y=place.shifted("y", step)) for step in (1, 2, 3)]
        + [place.neighbour(axis, 2) for axis in "xz"]
    )
    leaving = [
        [
            scatter_steps(
                place,
                layer,
                part,
                SCATTER_DIRECT[layer][i],
                held,
                boxes[(3 * layer + i) * 5 : (3 * layer + i) * 5 + 5],
                scatter_send.at[layer, i],
                scatter_recv.at[layer, i],
                summed_ref,
            )
            for i, part in enumerate(SCATTER_PARTS)
        ]
        for layer in range(2)
    ]
    edge = pltpu.make_async_remote_copy(
        src_ref=kept["edge"],
        dst_ref=came_ref,
        send_sem=edge_sems.at[0],
        recv_sem=edge_sems.at[1],
        device_id=place.device(z=place.shifted("z", 2)),
        device_id_type=MESH,
    )

    def finish_edge(section, mine):
        @pl.when(place.section == section)
        def _():
            stays_ref[...] = mine

        @pl.when(place.section != section)
        def _():
            kept["edge"][...] = mine
            edge.start()

    def go(layer, part):
        next(leaving[layer][part])

    arriving = [
        [
            gather_steps(
                place,
                layer,
                part,
                (((), (0, 1)), ((), (1,)))[layer][i],
                held,
                gather_send.at[layer, i],
                gather_recv.at[layer, i],
            )
            for i, part in enumerate(GATHER_PARTS)
        ]
        for layer in range(2)
    ]

    def come(layer, part, steps=1):
        for _ in range(steps):
            next(arriving[layer][part])

    cos, sin = cos_ref[...], sin_ref[...]
    mine = lax.axis_index("ctx")
    gathers = [
        KeyGather(place, kept["joined"].at[i], send_sems.at[i], recv_sems.at[i]) for i in range(2)
    ]
    sums = [
        KeyGradSum(
            place,
            kept["parts"].at[i],
            kept["pair"],
            kept["ring"].at[i],
            send_sems.at[2 + i],
            recv_sems.at[2 + i],
        )
        for i in range(2)
    ]
    grads = [
        WeightGrads(
            held.at[i],
            [kept[name] for name in ("first", "second", "third")],
            kept["gain_rows"],
            kept["lhs"],
            kept["hidden_lhs"],
        )
        for i in range(2)
    ]

    def start_layer(layer, current):
        unpack_gains(held, layer, gains_ref)
        unpack_wide(held, layer, LOWER, kept["wide"])
        kept["joined"][layer, mine] = project(
            current,
            gains_ref[layer, 0:1],
            weights[layer],
            cos,
            sin,
            kept["normed"].at[layer],
            kept["query"].at[layer],
        )
        gathers[layer].start()

    def attention_of_layer(layer):
        gathers[layer].finish()
        attended = attend(
            kept["query"].at[layer],
            kept["joined"].at[layer],
            seg_ref[place.section],
            kept["probs"].at[layer],
        )
        kept["attended"][layer] = attended

    def rest_of_layer(layer, current):
        unpack_wide(held, layer, UPPER, kept["wide"])
        unpack_down(held, layer, kept["down"])
        attended = kept["attended"][layer]
        midway, scale, normed_two, gate, up, hidden, result = feed_forward(
            current, attended, gains_ref[layer, 1:2], weights[layer]
        )
        kept["normed_two"][layer] = normed_two
        kept["hidden"][layer] = hidden
        return midway, gate, up, result

    def back_of_layer(layer, incoming, midway, gate, up, after, between):
        down_grad, gate_grad, up_grad, gain_grad, midway_grad, out_grad, mixed_grad = (
            feed_forward_back(incoming, midway, gate, up, gains_ref[layer, 1:2], weights[layer])
        )
        kept["down_grad"][...] = down_grad
        kept["gate_grad"][...] = gate_grad
        kept["up_grad"][...] = up_grad
        kept["out_grad"][...] = out_grad
        kept["midway_grad"][...] = midway_grad
        after()
        kept["query_grad"][...] = attend_back(
            mixed_grad,
            kept["attended"][layer],
            kept["query"].at[layer],
            kept["joined"].at[layer],
            kept["probs"].at[layer],
            kept["parts"].at[layer],
            between,
        )
        sums[layer].start()
        return gain_grad

    def end_of_layer(layer, current):
        sums[layer].finish(kept["key_grads"])
        turned, values, gain_grad, grad_in = project_back(
            kept["query_grad"][...],
            kept["key_grads"][...],
            kept["midway_grad"][...],
            current,
            gains_ref[layer, 0:1],
            cos,
            sin,
            weights[layer],
        )
        kept["turned"][...] = turned
        kept["values"][...] = values
        return gain_grad, grad_in

    def down_grads(layer, down_grad):
        grads[layer].down(kept["hidden"][layer], down_grad.astype(BF16))

    def middle_grads(layer):
        grads[layer].middle(
            kept["normed_two"][layer],
            kept["attended"][layer],
            kept["gate_grad"],
            kept["up_grad"],
            kept["out_grad"],
        )

    def late_grads(layer, attn_gain_grad, mlp_gain_grad):
        grads[layer].late(
            kept["normed"][layer],
            kept["turned"],
            kept["values"],
            kept["out_grad"],
            attn_gain_grad,
            mlp_gain_grad,
        )

    def give(part):
        pl.semaphore_signal(
            credits.at[part], inc=1, device_id=place.partner(), device_id_type=MESH
        )

    def begin(part):
        pl.semaphore_wait(credits.at[part], 1)
        go(0, part)

    upper, lower = 0, 1
    come(0, lower)
    come(0, upper)
    come(0, lower)
    come(0, upper)
    come(0, lower)
    come(1, lower)
    come(1, upper)
    come(0, upper)
    come(0, lower)
    come(0, upper)
    come(0, lower)

    x = x_ref[place.section].astype(F32).T
    start_layer(0, x)
    come(1, lower)
    come(1, upper)
    come(0, upper)
    gathers[0].pass_on()
    come(1, lower)
    come(1, upper)
    attention_of_layer(0)
    come(1, lower)
    come(0, upper)
    come(1, upper)
    come(0, upper)
    midway, gate, up, result = rest_of_layer(0, x)
    kept["midway"][...] = midway
    kept["gate"][...] = gate
    kept["up"][...] = up
    passed = result.astype(BF16)
    kept["x_2"][...] = passed
    come(1, lower)
    come(1, lower)
    start_layer(1, passed.astype(F32))
    come(1, upper)
    gathers[1].pass_on()
    attention_of_layer(1)
    come(1, upper)
    come(1, upper)
    midway, gate, up, result = rest_of_layer(1, kept["x_2"][...].astype(F32))
    finish_edge(1, result.T)

    first, second, third = 0, 1, 2
    incoming = late_ref[place.section].astype(F32).T
    down_grads(1, incoming)
    go(1, first)

    def nothing():
        pass

    def after_last_feed_forward():
        go(1, first)
        give(first)
        middle_grads(1)
        go(1, second)

    mlp_gain_grad_2 = back_of_layer(
        1, incoming, midway, gate, up, after_last_feed_forward, [nothing] * 3
    )
    sums[1].middle()
    go(1, first)
    go(1, second)
    give(second)
    attn_gain_grad_2, grad_in = end_of_layer(1, kept["x_2"][...].astype(F32))
    go(1, first)
    late_grads(1, attn_gain_grad_2, mlp_gain_grad_2)
    go(1, third)
    incoming = grad_in.astype(BF16).astype(F32)
    down_grads(0, incoming)
    begin(first)
    go(1, second)

    def after_feed_forward():
        go(1, third)
        give(third)
        go(1, first)
        go(0, first)
        middle_grads(0)
        begin(second)

    mlp_gain_grad_1 = back_of_layer(
        0,
        incoming,
        kept["midway"][...],
        kept["gate"][...],
        kept["up"][...],
        after_feed_forward,
        [nothing] * 3,
    )
    go(1, second)
    go(1, third)
    go(1, first)
    sums[0].middle()
    go(0, second)
    go(0, first)
    go(1, second)
    go(1, third)
    go(0, second)
    attn_gain_grad_1, grad_in = end_of_layer(0, x_ref[place.section].astype(F32).T)
    late_grads(0, attn_gain_grad_1, mlp_gain_grad_1)
    begin(third)
    go(1, second)
    finish_edge(0, grad_in.T)
    go(0, first)
    go(0, third)
    go(0, first)
    go(0, second)
    go(0, third)
    go(0, first)
    go(0, second)
    go(0, third)
    go(1, first)
    go(1, second)
    go(1, third)
    go(0, first)
    go(0, third)
    go(0, second)
    edge.wait()


def run_layers(x, late, cos, sin, segments, shards):
    return pl.pallas_call(
        layers_kernel,
        out_shape=jax.ShapeDtypeStruct((PACKED + 2 * D, LANES), F32),
        in_specs=[VMEM] * 14,
        out_specs=VMEM,
        scratch_shapes=[
            pltpu.SemaphoreType.DMA((4, 8)),
            pltpu.SemaphoreType.DMA((4, 8)),
            pltpu.SemaphoreType.DMA((2, 2, GATHER_SLOTS)),
            pltpu.SemaphoreType.DMA((2, 2, GATHER_SLOTS)),
            pltpu.SemaphoreType.DMA((2, 3, SCATTER_SLOTS)),
            pltpu.SemaphoreType.DMA((2, 3, SCATTER_SLOTS)),
            pltpu.SemaphoreType.DMA((2,)),
            pltpu.SemaphoreType.REGULAR((3,)),
            *[pltpu.VMEM(shape, kind) for shape, kind in KEPT.values()],
            *[box for layer in range(2) for part in SCATTER_PARTS for box in scatter_inboxes(part)],
        ],
        compiler_params=params(2),
        name="layers",
    )(x, late, cos, sin, segments, *shards)


def rope_tables(first):
    places = first + jnp.arange(ROWS, dtype=jnp.int32)
    pair_index = jnp.arange(HEAD // 2).astype(F32)
    frequency = rope_base ** (-2.0 * pair_index / HEAD)
    angles = places.astype(F32)[:, None] * frequency[None, :]
    cos, sin = jnp.cos(angles), jnp.sin(angles)
    return jnp.concatenate([cos] * 4, axis=1), jnp.concatenate([-sin, sin] * 2, axis=1)


def local(block_input, cotangent, segment_ids, *shards):
    cos, sin = rope_tables(lax.axis_index("ctx") * ROWS)
    x = block_input[:, 0].transpose(0, 2, 1)
    late = cotangent[:, 0].transpose(0, 2, 1)
    return finish(run_layers(x, late, cos, sin, segment_ids, shards))


def solution(mesh):
    shard = P("section", ("ctx", "fsdp"))
    matrix = P("section", ("ctx", "fsdp"), None)
    return jax.shard_map(
        local,
        mesh=mesh,
        in_specs=(
            P(None, "fsdp", "ctx", None),
            P(None, "fsdp", "ctx", None),
            P(None, "fsdp", None),
            shard,
            matrix,
            matrix,
            matrix,
            matrix,
            matrix,
            matrix,
            matrix,
            shard,
        ),
        out_specs=(
            P("section", None, "fsdp", "ctx", None),
            shard,
            matrix,
            matrix,
            matrix,
            matrix,
            matrix,
            matrix,
            matrix,
            shard,
        ),
        check_vma=False,
    )
```

```python
import functools

import jax
import jax.numpy as jnp
from jax import lax
from jax.experimental import pallas as pl
from jax.experimental.pallas import tpu as pltpu
from jax.sharding import PartitionSpec as P

MESH = pl.DeviceIdType.MESH
F32 = jnp.float32
BF16 = jnp.bfloat16
ANY = pl.BlockSpec(memory_space=pl.ANY)
VMEM = pl.BlockSpec(memory_space=pltpu.VMEM)

D = 576
FF = 1536
KVD = 192
HEAD = 64
GROUP = 3
KV_HEADS = 3
ROWS = 128
SEQ = 1024
LANES = 128

norm_eps = 1e-05
rope_base = 100000.0
masked_score = -1e30

WIDE = 4608
GATE_AT = 768
UP_AT = GATE_AT + FF
OUT_AT = UP_AT + FF
VALUE_AT = OUT_AT + D
TAIL_AT = VALUE_AT - HEAD
BLOCKS = WIDE // LANES

DOWN_ROWS = 24
TAIL_ROW = 4 * DOWN_ROWS
UPPER_ROW = 112
LOWER_ROW = 368
PACKED = 448
UPPER = tuple(range(6, 34))
LOWER = tuple(range(6)) + (34, 35)
GAIN_ROW = LOWER_ROW + 9 * len(LOWER)
GAIN_TILE = 432
EARLY = 4 * LANES


def packed_row(column):
    if column in UPPER:
        return UPPER_ROW + 9 * UPPER.index(column)
    return LOWER_ROW + 9 * LOWER.index(column)


GATHER_PARTS = (
    ((0, 368), (((0, 160), "xy"), ((160, 208), "yx"))),
    ((368, 80), (((368, 48), "xy"), ((416, 32), "yx"))),
)
SCATTER_PARTS = (
    ((0, 112), (((0, 48), "yx"), ((48, 64), "xy"))),
    ((112, 256), (((112, 112), "yx"), ((224, 144), "xy"))),
    ((368, 80), (((368, 48), "yx"), ((416, 32), "xy"))),
)
SCATTER_DIRECT = (((1,), (1,), (0, 1)), ((), (), (0, 1)))
VMEM_BYTES = 63 * 1024 * 1024


def params(collective_id=None):
    if collective_id is None:
        return pltpu.CompilerParams(vmem_limit_bytes=VMEM_BYTES)
    return pltpu.CompilerParams(
        vmem_limit_bytes=VMEM_BYTES, collective_id=collective_id, has_side_effects=True
    )


def dot(left, right):
    return jnp.dot(left, right, preferred_element_type=F32)


def dot_nt(left, right):
    return lax.dot_general(left, right, (((1,), (1,)), ((), ())), preferred_element_type=F32)


def dot_tn(left, right):
    return lax.dot_general(left, right, (((0,), (0,)), ((), ())), preferred_element_type=F32)


class Place:
    def __init__(self):
        self.section = lax.axis_index("section")
        ctx = lax.axis_index("ctx")
        fsdp = lax.axis_index("fsdp")
        self.core = lax.rem(ctx, 2)
        self.at = {
            "x": lax.rem(fsdp, 4),
            "y": ctx // 2,
            "z": self.section * 2 + fsdp // 4,
        }

    def device(self, core=None, **moved):
        at = dict(self.at, **moved)
        core = self.core if core is None else core
        return (at["z"] // 2, at["y"] * 2 + core, lax.rem(at["z"], 2) * 4 + at["x"])

    def shifted(self, axis, step):
        return lax.rem(self.at[axis] + step + 4, 4)

    def neighbour(self, axis, step):
        return self.device(**{axis: self.shifted(axis, step)})

    def partner(self):
        return self.device(core=1 - self.core)


def greet(devices):
    barrier = pltpu.get_barrier_semaphore()
    for device in devices:
        pl.semaphore_signal(barrier, inc=1, device_id=device, device_id_type=MESH)
    pl.semaphore_wait(barrier, len(devices))


def halves(rows):
    first, count = rows
    upper = (count // 2 + 15) // 16 * 16
    return (first, upper), (first + upper, count - upper)


def layer_region(ref, layer, coords, whole, rows, core):
    y = slice(None) if "y" in whole else coords["y"]
    x = slice(None) if "x" in whole else coords["x"]
    return ref.at[layer, y, core, :, x, pl.ds(*rows)]


GATHER_DIRECT = (((), (0, 1)), ((), (1,)))


def gather_slots(direct):
    phases = sum(3 if phase in direct else 4 for phase in range(2))
    return 3 + 2 * phases + 2 * (1 if 1 in direct else 4)


WAYS = (1, -1, 2)


def gather_steps(place, layer, part, direct, held, send_sems, recv_sems):
    core = place.core
    all_rows, chunks = part
    plane = lax.rem(place.at["z"] + 4 - 2 * layer, 4)

    def copy(slot, ref, device):
        return pltpu.make_async_remote_copy(
            src_ref=ref,
            dst_ref=ref,
            send_sem=send_sems.at[slot],
            recv_sem=recv_sems.at[slot],
            device_id=device,
            device_id_type=MESH,
        )

    def across(z_lo, slot):
        shard = held.at[layer, place.at["y"], core, z_lo, place.at["x"], pl.ds(*all_rows)]
        return copy(slot, shard, place.neighbour("z", WAYS[slot]))

    for source in range(2):

        @pl.when(plane == source)
        def _():
            for slot in range(3):
                across(source, slot).start()

    yield

    @pl.when((plane == 1) | (plane == 2))
    def _():
        across(0, 0).wait_recv()

    @pl.when((plane == 0) | (plane == 3))
    def _():
        across(0, 1).wait_recv()

    @pl.when(plane >= 2)
    def _():
        across(0, 2).wait_recv()

    counter = [3]
    sent = []
    to_partner = []

    def send(ref, device):
        made = copy(counter[0], ref, device)
        counter[0] += 1
        made.start()
        sent.append(made)
        return made

    for phase in range(2):
        one_step = phase in direct
        first, second = [], []
        for rows, order in chunks:
            axis, whole = order[phase], order[:phase]
            block = layer_region(held, layer, place.at, whole, rows, core)
            ways = WAYS if one_step else WAYS[:2]
            first.append([send(block, place.neighbour(axis, way)) for way in ways])
            if phase == 1 and not one_step:
                to_partner.append(send(block, place.partner()))
        yield
        for copies, (rows, order) in zip(first, chunks):
            axis, whole = order[phase], order[:phase]
            for made in copies:
                made.wait_recv()
            left = dict(place.at, **{axis: place.shifted(axis, -1)})
            right = dict(place.at, **{axis: place.shifted(axis, 1)})
            if not one_step:
                upper, lower = halves(rows)
                second += [
                    send(
                        layer_region(held, layer, left, whole, upper, core),
                        place.neighbour(axis, 1),
                    ),
                    send(
                        layer_region(held, layer, right, whole, lower, core),
                        place.neighbour(axis, -1),
                    ),
                ]
            if phase == 1 and one_step:
                to_partner.append(
                    send(layer_region(held, layer, left, order, rows, core), place.partner())
                )
            elif phase == 1:
                for coords in (left, right):
                    to_partner.append(
                        send(layer_region(held, layer, coords, whole, rows, core), place.partner())
                    )
        if not one_step:
            yield
            for made in second:
                made.wait_recv()
    if 1 not in direct:
        for rows, order in chunks:
            axis, whole = order[1], order[:1]
            far = dict(place.at, **{axis: place.shifted(axis, 2)})
            to_partner.append(
                send(layer_region(held, layer, far, whole, rows, core), place.partner())
            )
    yield
    for made in to_partner:
        made.wait_recv()
    for made in sent:
        made.wait_send()

    @pl.when(plane <= 1)
    def _():
        for slot in range(3):
            across(0, slot).wait_send()

    yield


def scatter_slots(direct):
    return 1 + 2 * sum(3 if phase in direct else 4 for phase in range(2)) + 3


def scatter_inboxes(part):
    (first, count), chunks = part
    boxes = []
    for (_, rows), order in chunks:
        others = (2, 4) if order == "yx" else (4, 2)
        boxes.append(pltpu.VMEM((3, *others, rows, LANES), BF16))
        boxes.append(pltpu.VMEM((3, 2, rows, LANES), BF16))
    boxes.append(pltpu.VMEM((3, count, LANES), BF16))
    return boxes


def scatter_steps(place, layer, part, direct, held, boxes, send_sems, recv_sems, out_ref):
    core = place.core
    here_y, here_x = place.at["y"], place.at["x"]
    (first, count), chunks = part
    counter = [0]
    sent = []

    def copy(source, target, device):
        slot = counter[0]
        counter[0] += 1
        return pltpu.make_async_remote_copy(
            src_ref=source,
            dst_ref=target,
            send_sem=send_sems.at[slot],
            recv_sem=recv_sems.at[slot],
            device_id=device,
            device_id_type=MESH,
        )

    def send(source, target, device):
        made = copy(source, target, device)
        made.start()
        sent.append(made)
        return made

    def add(spot, source, rows):
        held[spot] = (held[spot].astype(F32) + source().astype(F32)).astype(BF16)

    all_rows = pl.ds(first, count)
    swap = copy(
        held.at[layer, :, 1 - core, :, :, all_rows],
        held.at[1 - layer, :, core, :, :, all_rows],
        place.partner(),
    )
    swap.start()
    yield
    swap.wait()

    def add_swapped(step, carry):
        y, z_lo, x = step // 8, lax.rem(step // 4, 2), lax.rem(step, 4)
        add(
            (layer, y, core, z_lo, x, all_rows),
            lambda: held[1 - layer, y, 1 - core, z_lo, x, all_rows],
            count,
        )
        return carry

    lax.fori_loop(0, 32, add_swapped, 0)

    def add_block(phase, axis, coords, rows, box, slot):
        at, size = rows

        def in_box(begin):
            return pl.ds(begin, size)

        begin = 0 if slot else at[1]
        here = pl.ds(at[0], size)
        if phase == 0:

            def body(step, carry):
                if axis == "y":
                    z_lo, x = step // 4, lax.rem(step, 4)
                    spot = (layer, coords["y"], core, z_lo, x, here)
                    add(spot, lambda: box[slot, z_lo, x, in_box(begin)], size)
                else:
                    y, z_lo = step // 2, lax.rem(step, 2)
                    spot = (layer, y, core, z_lo, coords["x"], here)
                    add(spot, lambda: box[slot, y, z_lo, in_box(begin)], size)
                return carry

            lax.fori_loop(0, 8, body, 0)
        else:
            for z_lo in range(2):
                spot = (layer, coords["y"], core, z_lo, coords["x"], here)
                add(spot, lambda: box[slot, z_lo, in_box(begin)], size)

    flights = [[], []]

    def land(flight):
        for made, phase, axis, lands, spot_rows, box, slot in flight:
            made.wait_recv()
            add_block(phase, axis, lands, spot_rows, box, slot)

    for phase in range(2):
        one_step = phase in direct
        for step in range(1 if one_step else 2):
            for i, (rows, order) in enumerate(chunks):
                box = boxes[2 * i + phase]
                land(flights[i])
                axis, whole = order[phase], order[phase + 1 :]
                right = dict(place.at, **{axis: place.shifted(axis, 1)})
                left = dict(place.at, **{axis: place.shifted(axis, -1)})
                far = dict(place.at, **{axis: place.shifted(axis, 2)})
                upper, lower = halves(rows)
                if one_step:
                    plan = (
                        (right, rows, 1, place.at, 0),
                        (left, rows, -1, place.at, 1),
                        (far, rows, 2, place.at, 2),
                    )
                elif step == 0:
                    plan = ((far, upper, 1, right, 0), (far, lower, -1, left, 0))
                else:
                    plan = ((right, rows, 1, place.at, 1), (left, rows, -1, place.at, 2))
                flights[i] = []
                for source_at, part_rows, way, lands, slot in plan:
                    begin = part_rows[0] - rows[0]
                    lead = (slice(None),) * (2 if phase == 0 else 1)
                    made = send(
                        layer_region(held, layer, source_at, whole, part_rows, core),
                        box.at[(slot, *lead, pl.ds(begin, part_rows[1]))],
                        place.neighbour(axis, way),
                    )
                    flights[i].append(
                        (made, phase, axis, lands, ((part_rows[0], begin), part_rows[1]), box, slot)
                    )
            yield
    for flight in flights:
        land(flight)

    plane = lax.rem(place.at["z"] + 4 - 2 * layer, 4)
    stays = lax.rem(plane, 2)
    box = boxes[4]
    shards = ((3 - plane) // 3, plane // 2, lax.rem(plane, 2))
    senders = ((plane == 0) | (plane == 3), (plane == 1) | (plane == 2), plane >= 2)
    last = [
        copy(
            held.at[layer, here_y, core, z_lo, here_x, all_rows],
            box.at[i],
            place.neighbour("z", WAYS[i]),
        )
        for i, z_lo in enumerate(shards)
    ]
    for made, sender in zip(last, senders):
        pl.when(sender)(made.start)
    yield

    @pl.when(plane < 2)
    def _():
        for made in last:
            made.wait_recv()
        total = held[layer, here_y, core, stays, here_x, all_rows].astype(F32)
        for i in range(3):
            total += box[i].astype(F32)
        out_ref[all_rows] = total

    for made in sent:
        made.wait_send()
    for made, sender in zip(last, senders):
        pl.when(sender)(made.wait_send)
    yield


class Exchange:
    def __init__(self, place, send_sems, recv_sems):
        self.place = place
        self.send_sems = send_sems
        self.recv_sems = recv_sems

    def copy(self, slot, source, target, device):
        return pltpu.make_async_remote_copy(
            src_ref=source,
            dst_ref=target,
            send_sem=self.send_sems.at[slot],
            recv_sem=self.recv_sems.at[slot],
            device_id=device,
            device_id_type=MESH,
        )

    def along_y(self, step):
        return self.place.device(y=lax.rem(self.place.at["y"] + step + 4, 4))


class KeyGather(Exchange):
    def __init__(self, place, keys_ref, send_sems, recv_sems):
        super().__init__(place, send_sems, recv_sems)
        self.keys_ref = keys_ref

    def direct(self, away):
        own = self.keys_ref.at[self.place.at["y"] * 2 + self.place.core]
        return self.copy(away, own, own, self.along_y(away))

    def passed_on(self, away):
        block = self.keys_ref.at[
            lax.rem(self.place.at["y"] - away + 4, 4) * 2 + self.place.core
        ]
        return self.copy(4 + away, block, block, self.place.partner())

    def start(self):
        y = self.place.at["y"]
        for away in (1, 3, 2):

            @pl.when(y + away < 4)
            def _():
                self.direct(away).start()

        self.passed_on(0).start()
        for away in range(1, 4):

            @pl.when(y + away < 4)
            def _():
                self.keys_ref[pl.ds((y + away) * 2, 2)] = jnp.zeros(
                    (2,) + self.keys_ref.shape[1:], self.keys_ref.dtype
                )

    def pass_on(self):
        y = self.place.at["y"]
        for away in (1, 3, 2):

            @pl.when(y - away >= 0)
            def _():
                self.direct(away).wait_recv()
                self.passed_on(away).start()

    def finish(self):
        y = self.place.at["y"]
        self.passed_on(0).wait()
        for away in range(1, 4):

            @pl.when(y - away >= 0)
            def _():
                self.passed_on(away).wait()

            @pl.when(y + away < 4)
            def _():
                self.direct(away).wait_send()


class KeyGradSum(Exchange):
    def __init__(self, place, parts_ref, pair_ref, ring_ref, send_sems, recv_sems):
        super().__init__(place, send_sems, recv_sems)
        self.parts_ref = parts_ref
        self.pair_ref = pair_ref
        self.ring_ref = ring_ref

    def swap(self):
        return self.copy(
            0, self.parts_ref.at[1 - self.place.core], self.pair_ref, self.place.partner()
        )

    def direct(self, away):
        y = lax.rem(self.place.at["y"] - away + 4, 4)
        return self.copy(
            away,
            self.parts_ref.at[self.place.core, y],
            self.ring_ref.at[away - 1],
            self.along_y(-away),
        )

    def start(self):
        self.swap().start()

    def middle(self):
        self.swap().wait()
        core = self.place.core
        for y in range(4):
            self.parts_ref[core, y] = (
                self.parts_ref[core, y].astype(F32) + self.pair_ref[y].astype(F32)
            ).astype(BF16)
        for away in (1, 3, 2):

            @pl.when(self.place.at["y"] - away >= 0)
            def _():
                self.direct(away).start()

    def finish(self, out_ref):
        y = self.place.at["y"]
        out_ref[...] = self.parts_ref[self.place.core, y].astype(F32)
        for away in range(1, 4):

            @pl.when(y + away < 4)
            def _():
                self.direct(away).wait_recv()
                out_ref[...] += self.ring_ref[away - 1].astype(F32)

        for away in range(1, 4):

            @pl.when(y - away >= 0)
            def _():
                self.direct(away).wait_send()


def packed_shard(attn_ref, query_ref, key_ref, value_ref, w_out_ref, gate_ref, up_ref, down_ref, mlp_ref):
    def wide(ref):
        return ref[0].astype(F32)

    joined = jnp.concatenate(
        [wide(r) for r in (query_ref, key_ref, gate_ref, up_ref, w_out_ref, value_ref)], axis=1
    )
    down = wide(down_ref)
    pieces = [down[:, i * LANES : (i + 1) * LANES] for i in range(4)]
    half = DOWN_ROWS // 2
    pieces.append(jnp.concatenate([down[:half, 4 * LANES :], down[half:, 4 * LANES :]], axis=1))
    pieces.append(jnp.zeros((4, LANES), F32))
    pieces += [joined[:, i * LANES : (i + 1) * LANES] for i in UPPER]
    pieces.append(jnp.zeros((4, LANES), F32))
    pieces += [joined[:, i * LANES : (i + 1) * LANES] for i in LOWER]
    for ref in (attn_ref, mlp_ref):
        gain = ref[...].astype(F32)
        pieces.append(jnp.concatenate([gain, jnp.zeros((1, LANES - 9), F32)], axis=1))
    pieces.append(jnp.zeros((PACKED - GAIN_ROW - 2, LANES), F32))
    return jnp.concatenate(pieces, axis=0).astype(BF16)


def gain_masks(first_device, devices, rows_each, rows):
    shape = (devices * rows_each, D)
    row = lax.broadcasted_iota(jnp.int32, shape, 0)
    owner = lax.broadcasted_iota(jnp.int32, shape, 1) // 9
    same = owner == first_device + row // rows_each
    place = lax.rem(row, rows_each)
    return [same & (place == at) for at in rows]


def lane_spread():
    lane = lax.broadcasted_iota(jnp.int32, (LANES, D), 0)
    feature = lax.broadcasted_iota(jnp.int32, (LANES, D), 1)
    return (lane == lax.rem(feature, 9)).astype(BF16)


def packed_rows(held, layer, y, first, count):
    start = first // 16 * 16
    size = (first + count + 15) // 16 * 16 - start
    return [
        held[layer, y, core, z_lo, x, start : start + size].astype(F32)[
            first - start : first - start + count
        ]
        for core in range(2)
        for z_lo in range(2)
        for x in range(4)
    ]


def unpack_wide(held, layer, columns, wide):
    def body(y, carry):
        rows = pl.ds(pl.multiple_of(y * 144, 16), 144)
        for column in columns:
            wide[layer, rows, column * LANES : (column + 1) * LANES] = jnp.concatenate(
                packed_rows(held, layer, y, packed_row(column), 9), axis=0
            ).astype(BF16)
        return carry

    lax.fori_loop(0, 4, body, 0)


def unpack_down(held, layer, down):
    def body(y, carry):
        rows = pl.ds(pl.multiple_of(y * 384, 16), 384)
        for column in range(4):
            down[layer, rows, column * LANES : (column + 1) * LANES] = jnp.concatenate(
                packed_rows(held, layer, y, DOWN_ROWS * column, DOWN_ROWS), axis=0
            ).astype(BF16)
        tails = []
        for tail in packed_rows(held, layer, y, TAIL_ROW, DOWN_ROWS // 2):
            tails += [tail[:, :HEAD], tail[:, HEAD:]]
        down[layer, rows, 4 * LANES :] = jnp.concatenate(tails, axis=0).astype(BF16)
        return carry

    lax.fori_loop(0, 4, body, 0)


def unpack_gains(held, layer, gains):
    totals = [jnp.zeros((1, D), F32)] * 2
    spread_to = lane_spread()
    for y in range(4):
        rows = held[layer, y, :, :, :, GAIN_TILE:, :].reshape(16 * 16, LANES)
        spread = dot(rows, spread_to)
        at = GAIN_ROW - GAIN_TILE
        masks = gain_masks(y * 16, 16, 16, (at, at + 1))
        totals = [
            total + jnp.sum(jnp.where(mask, spread, 0.0), axis=0, keepdims=True)
            for total, mask in zip(totals, masks)
        ]
    gains[layer, 0:1] = totals[0]
    gains[layer, 1:2] = totals[1]


def finish_kernel(
    all_ref,
    edges_ref,
    attn_ref,
    query_ref,
    key_ref,
    value_ref,
    w_out_ref,
    gate_ref,
    up_ref,
    down_ref,
    mlp_ref,
):
    section = lax.axis_index("section")
    edges_ref[0, section, 0] = all_ref[PACKED : PACKED + D]
    edges_ref[0, 1 - section, 0] = all_ref[PACKED + D :]
    packed = all_ref[:PACKED]
    joined = jnp.concatenate(
        [packed[packed_row(i) : packed_row(i) + 9] for i in range(BLOCKS)], axis=1
    )
    query_ref[:, 0] = joined[:, :D]
    key_ref[:, 0] = joined[:, D:GATE_AT]
    gate_ref[:, 0] = joined[:, GATE_AT:UP_AT]
    up_ref[:, 0] = joined[:, UP_AT:OUT_AT]
    w_out_ref[:, 0] = joined[:, OUT_AT:VALUE_AT]
    value_ref[:, 0] = joined[:, VALUE_AT:]
    tail = packed[TAIL_ROW : TAIL_ROW + DOWN_ROWS // 2]
    down_ref[0] = jnp.concatenate(
        [packed[DOWN_ROWS * i : DOWN_ROWS * (i + 1)] for i in range(4)]
        + [jnp.concatenate([tail[:, :HEAD], tail[:, HEAD:]], axis=0)],
        axis=1,
    )
    at = GAIN_ROW
    attn_ref[...] = packed[at : at + 1, :9]
    mlp_ref[...] = packed[at + 1 : at + 2, :9]


def finish(rows):
    shapes = (
        (1, 2, 1, D, ROWS),
        (1, 9),
        (9, 1, D),
        (9, 1, KVD),
        (9, 1, KVD),
        (9, 1, D),
        (9, 1, FF),
        (9, 1, FF),
        (1, DOWN_ROWS, D),
        (1, 9),
    )
    edges, attn, *wide, down, mlp = pl.pallas_call(
        finish_kernel,
        out_shape=tuple(jax.ShapeDtypeStruct(shape, F32) for shape in shapes),
        in_specs=[VMEM],
        out_specs=(VMEM,) * len(shapes),
        compiler_params=params(),
        name="finish",
    )(rows)
    wide = [grad.transpose(1, 0, 2) for grad in wide]
    return (edges.transpose(0, 1, 2, 4, 3), attn, *wide, down, mlp)


def swap_halves(block):
    lane = lax.broadcasted_iota(jnp.int32, block.shape, 1)
    return jnp.where(
        lax.rem(lane, HEAD) < HEAD // 2,
        pltpu.roll(block, LANES - HEAD // 2, 1),
        pltpu.roll(block, HEAD // 2, 1),
    )


def rotated(block, cos, sin):
    return block * cos + swap_halves(block) * sin


def project(current, gain, weights, cos, sin, normed_ref, query_ref):
    scale = lax.rsqrt(jnp.mean(current * current, axis=1, keepdims=True) + norm_eps)
    normed = (current * scale * gain).astype(BF16)
    normed_ref[...] = normed
    raw = dot(normed, weights.get("qk"))
    turned = [
        rotated(raw[:, i * LANES : (i + 1) * LANES], cos, sin).astype(BF16) for i in range(6)
    ]
    for i in range(4):
        query_ref[:, i * LANES : (i + 1) * LANES] = turned[i]
    query_ref[:, 4 * LANES :] = turned[4][:, :HEAD]
    values = dot(normed, weights.get("tail"))[:, HEAD:]
    return jnp.concatenate(
        [turned[4][:, HEAD:].astype(F32), turned[5].astype(F32), values], axis=1
    ).astype(BF16)


def heads_of(rows, group):
    return jnp.concatenate(
        [rows[:, (group * GROUP + r) * HEAD : (group * GROUP + r + 1) * HEAD] for r in range(GROUP)],
        axis=0,
    )


def attend(query_ref, keys_ref, seg_row, probs_ref):
    first = lax.axis_index("ctx") * ROWS
    rows = first + lax.broadcasted_iota(jnp.int32, (ROWS, SEQ), 0)
    columns = lax.broadcasted_iota(jnp.int32, (ROWS, SEQ), 1)
    own_seg = jnp.sum(jnp.where(columns == rows, seg_row, 0), axis=1, keepdims=True)
    allowed = (columns <= rows) & (seg_row == own_seg)
    bias = jnp.where(allowed, 0.0, masked_score)
    bias = jnp.concatenate([bias] * GROUP, axis=0)
    queries = query_ref[...]
    mixed = []
    for group in range(KV_HEADS):
        keys = keys_ref[:, :, group * HEAD : (group + 1) * HEAD].reshape(SEQ, HEAD)
        values = keys_ref[:, :, KVD + group * HEAD : KVD + (group + 1) * HEAD].reshape(SEQ, HEAD)
        scores = dot_nt(heads_of(queries, group), keys) * HEAD**-0.5 + bias
        shifted = jnp.exp(scores - jnp.max(scores, axis=1, keepdims=True))
        probs = (shifted / jnp.sum(shifted, axis=1, keepdims=True)).astype(BF16)
        probs_ref[group] = probs
        mixture = dot(probs, values)
        mixed += [mixture[r * ROWS : (r + 1) * ROWS] for r in range(GROUP)]
    return jnp.concatenate(mixed, axis=1).astype(BF16)


def feed_forward(current, attended, gain, weights):
    midway = current + dot(attended, weights.get("out"))
    scale = lax.rsqrt(jnp.mean(midway * midway, axis=1, keepdims=True) + norm_eps)
    normed = (midway * scale * gain).astype(BF16)
    gate = dot(normed, weights.get("gate"))
    up = dot(normed, weights.get("up"))
    hidden = (gate / (1.0 + jnp.exp(-gate)) * up).astype(BF16)
    result = midway + dot(hidden, weights.get("down"))
    return midway, scale, normed, gate, up, hidden, result


def norm_backward(scaled, values, scale):
    return scale * scaled - values * scale**3 * jnp.mean(scaled * values, axis=1, keepdims=True)


def feed_forward_back(
    incoming, midway, gate, up, gain, weights
):
    scale = lax.rsqrt(jnp.mean(midway * midway, axis=1, keepdims=True) + norm_eps)
    down_grad = incoming.astype(BF16)
    hidden_grad = dot_nt(down_grad, weights.get("down"))
    sigmoid = 1.0 / (1.0 + jnp.exp(-gate))
    gate_grad = (hidden_grad * up * sigmoid * (1.0 + gate * (1.0 - sigmoid))).astype(BF16)
    up_grad = (hidden_grad * gate * sigmoid).astype(BF16)
    normed_grad = dot_nt(gate_grad, weights.get("gate")) + dot_nt(
        up_grad, weights.get("up")
    )
    gain_grad = jnp.sum(normed_grad * midway * scale, axis=0, keepdims=True)
    midway_grad = incoming + norm_backward(normed_grad * gain, midway, scale)
    out_grad = midway_grad.astype(BF16)
    mixed_grad = dot_nt(out_grad, weights.get("out")).astype(BF16)
    return down_grad, gate_grad, up_grad, gain_grad, midway_grad, out_grad, mixed_grad


def attend_back(mixed_grad, attended, query_ref, keys_ref, probs_ref, parts_ref, between):
    queries = query_ref[...]
    query_grads = []
    for group in range(KV_HEADS):
        keys = keys_ref[:, :, group * HEAD : (group + 1) * HEAD].reshape(SEQ, HEAD)
        values = keys_ref[:, :, KVD + group * HEAD : KVD + (group + 1) * HEAD].reshape(SEQ, HEAD)
        grads = heads_of(mixed_grad, group)
        delta = jnp.sum(
            grads.astype(F32) * heads_of(attended, group).astype(F32), axis=1, keepdims=True
        )
        probs = probs_ref[group]
        score_grad = (probs.astype(F32) * (dot_nt(grads, values) - delta)).astype(BF16)
        query_grad = dot(score_grad, keys) * HEAD**-0.5
        query_grads += [query_grad[r * ROWS : (r + 1) * ROWS] for r in range(GROUP)]
        key_part = (dot_tn(heads_of(queries, group), score_grad) * HEAD**-0.5).astype(BF16)
        value_part = dot_tn(grads, probs).astype(BF16)
        for block in range(8):
            columns = slice(block * ROWS, (block + 1) * ROWS)
            at = (block % 2, block // 2)
            parts_ref[*at, group * HEAD : (group + 1) * HEAD] = key_part[:, columns]
            parts_ref[*at, KVD + group * HEAD : KVD + (group + 1) * HEAD] = value_part[:, columns]
        between[group]()
    return jnp.concatenate(query_grads, axis=1)


def project_back(
    query_grad, key_grads, midway_grad, current, gain, cos, sin, weights
):
    key_grads = key_grads.T
    joined = jnp.concatenate([query_grad, key_grads[:, :KVD]], axis=1)
    turned = jnp.concatenate(
        [rotated(joined[:, i * LANES : (i + 1) * LANES], cos, -sin) for i in range(6)], axis=1
    ).astype(BF16)
    values = key_grads[:, KVD:].astype(BF16)
    padded = jnp.concatenate([jnp.zeros((ROWS, HEAD), F32), key_grads[:, KVD:]], axis=1)
    normed_grad = dot_nt(turned, weights.get("qk")) + dot_nt(
        padded.astype(BF16), weights.get("tail")
    )
    scale = lax.rsqrt(jnp.mean(current * current, axis=1, keepdims=True) + norm_eps)
    gain_grad = jnp.sum(normed_grad * current * scale, axis=0, keepdims=True)
    grad_in = midway_grad + norm_backward(normed_grad * gain, current, scale)
    return turned, values, gain_grad, grad_in


GRAD_DEVICES = 16


def transposed(rows):
    return rows.astype(F32).T.astype(BF16)


class WeightGrads:
    def __init__(self, packed, stages, gain_rows, lhs, hidden_lhs):
        self.packed = packed
        self.first, self.second, self.third = stages
        self.gain_rows = gain_rows
        self.lhs = lhs
        self.hidden_lhs = hidden_lhs

    def place(self, stage, first_row, column, product):
        for i in range(product.shape[1] // LANES):
            at = packed_row(column + i) - first_row
            part = product[:, i * LANES : (i + 1) * LANES]
            for d in range(GRAD_DEVICES):
                stage[d, at : at + 9] = part[9 * d : 9 * d + 9]

    def rows(self, step, each):
        return pl.ds(pl.multiple_of(step * each * GRAD_DEVICES, 16), each * GRAD_DEVICES)

    def round(self, stage, y, first_row):
        rounded = stage[...].astype(BF16)
        self.packed[y, :, :, :, first_row : first_row + stage.shape[1]] = rounded.reshape(
            (2, 2, 4) + rounded.shape[1:]
        )

    def down(self, hidden, down_grad):
        half = DOWN_ROWS // 2
        self.hidden_lhs[...] = transposed(hidden)
        self.first[:, TAIL_ROW + half :] = jnp.zeros((GRAD_DEVICES, 4, LANES), F32)

        def body(y, carry):
            product = dot(self.hidden_lhs[self.rows(y, DOWN_ROWS)], down_grad)
            for d in range(GRAD_DEVICES):
                own = product[DOWN_ROWS * d : DOWN_ROWS * (d + 1)]
                for i in range(4):
                    self.first[d, DOWN_ROWS * i : DOWN_ROWS * (i + 1)] = own[
                        :, i * LANES : (i + 1) * LANES
                    ]
                self.first[d, TAIL_ROW : TAIL_ROW + half] = jnp.concatenate(
                    [own[:half, 4 * LANES :], own[half:, 4 * LANES :]], axis=1
                )
            self.round(self.first, y, 0)
            return carry

        lax.fori_loop(0, 64 // GRAD_DEVICES, body, 0)

    def middle(self, normed_two, attended, gate_grad_ref, up_grad_ref, out_grad_ref):
        self.lhs[1] = transposed(normed_two)
        self.lhs[2] = transposed(attended)
        self.second[:, 9 * len(UPPER) :] = jnp.zeros((GRAD_DEVICES, 4, LANES), F32)

        def body(y, carry):
            second = self.lhs[1, self.rows(y, 9)]
            self.place(self.second, UPPER_ROW, GATE_AT // LANES, dot(second, gate_grad_ref[...]))
            self.place(self.second, UPPER_ROW, UP_AT // LANES, dot(second, up_grad_ref[...]))
            third = self.lhs[2, self.rows(y, 9)]
            self.place(
                self.second, UPPER_ROW, OUT_AT // LANES, dot(third, out_grad_ref[:, :EARLY])
            )
            self.round(self.second, y, UPPER_ROW)
            return carry

        lax.fori_loop(0, 64 // GRAD_DEVICES, body, 0)

    def late(self, normed, turned_ref, values_ref, out_grad_ref, attn_gain_grad, mlp_gain_grad):
        self.lhs[0] = transposed(normed)
        spread_to = lane_spread()
        (mask,) = gain_masks(0, 64, 1, (0,))
        for i, gain_grad in enumerate((attn_gain_grad, mlp_gain_grad)):
            chosen = jnp.where(mask, gain_grad, 0.0).astype(BF16)
            self.gain_rows[i] = dot_nt(chosen, spread_to)
        self.third[:, GAIN_ROW + 2 - LOWER_ROW :] = jnp.zeros(
            (GRAD_DEVICES, PACKED - GAIN_ROW - 2, LANES), F32
        )

        def body(y, carry):
            first = self.lhs[0, self.rows(y, 9)]
            self.place(self.third, LOWER_ROW, 0, dot(first, turned_ref[...]))
            third = self.lhs[2, self.rows(y, 9)]
            self.place(
                self.third,
                LOWER_ROW,
                (OUT_AT + EARLY) // LANES,
                jnp.concatenate(
                    [dot(third, out_grad_ref[:, EARLY:]), dot(first, values_ref[...])], axis=1
                ),
            )
            for i in range(2):
                gains = self.gain_rows[i, self.rows(y, 1)]
                for d in range(GRAD_DEVICES):
                    at = GAIN_ROW + i - LOWER_ROW
                    self.third[d, at : at + 1] = gains[d : d + 1]
            self.round(self.third, y, LOWER_ROW)
            return carry

        lax.fori_loop(0, 64 // GRAD_DEVICES, body, 0)


COLUMNS = {
    "qk": (0, GATE_AT),
    "gate": (GATE_AT, UP_AT),
    "up": (UP_AT, OUT_AT),
    "out": (OUT_AT, VALUE_AT),
    "tail": (TAIL_AT, WIDE),
}


class Weights:
    def __init__(self, layer, wide, down):
        self.layer = layer
        self.wide = wide
        self.down = down

    def get(self, name):
        if name == "down":
            return self.down[self.layer]
        first, end = COLUMNS[name]
        return self.wide[self.layer, :, first:end]


ROW = (ROWS, D)
KEPT = {
    "joined": ((2, 8, ROWS, 2 * KVD), BF16),
    "probs": ((2, KV_HEADS, GROUP * ROWS, SEQ), BF16),
    "parts": ((2, 2, 4, 2 * KVD, ROWS), BF16),
    "pair": ((4, 2 * KVD, ROWS), BF16),
    "ring": ((2, 3, 2 * KVD, ROWS), BF16),
    "key_grads": ((2 * KVD, ROWS), F32),
    "normed": ((2, *ROW), BF16),
    "query": ((2, *ROW), BF16),
    "attended": ((2, *ROW), BF16),
    "normed_two": ((2, *ROW), BF16),
    "hidden": ((2, ROWS, FF), BF16),
    "midway": (ROW, F32),
    "gate": ((ROWS, FF), F32),
    "up": ((ROWS, FF), F32),
    "x_2": (ROW, BF16),
    "gate_grad": ((ROWS, FF), BF16),
    "up_grad": ((ROWS, FF), BF16),
    "down_grad": (ROW, BF16),
    "out_grad": (ROW, BF16),
    "midway_grad": (ROW, F32),
    "query_grad": (ROW, F32),
    "turned": ((ROWS, D + KVD), BF16),
    "values": ((ROWS, KVD), BF16),
    "lhs": ((3, D, ROWS), BF16),
    "hidden_lhs": ((FF, ROWS), BF16),
    "first": ((GRAD_DEVICES, UPPER_ROW, LANES), F32),
    "second": ((GRAD_DEVICES, LOWER_ROW - UPPER_ROW, LANES), F32),
    "third": ((GRAD_DEVICES, PACKED - LOWER_ROW, LANES), F32),
    "gain_rows": ((2, 64, LANES), F32),
    "held": ((2, 4, 2, 2, 4, PACKED, LANES), BF16),
    "wide": ((2, D, WIDE), BF16),
    "down": ((2, FF, D), BF16),
    "gains": ((2, 8, D), F32),
    "edge": ((2, D, ROWS), BF16),
}


def layers_kernel(
    x_ref,
    late_ref,
    cos_ref,
    sin_ref,
    seg_ref,
    *rest,
):
    shards = rest[:9]
    out_ref = rest[9]
    summed_ref = out_ref.at[:PACKED]
    stays_ref = out_ref.at[PACKED : PACKED + D]
    came_ref = out_ref.at[PACKED + D :]
    edge_sems, credits, *scratch = rest[10:]
    key_sems, gather_sems, scatter_sems = scratch[:8], scratch[8:16], scratch[16:28]
    scratch = scratch[28:]
    place = Place()
    kept = dict(zip(KEPT, scratch))
    boxes = scratch[len(KEPT) :]
    held, gains_ref = kept["held"], kept["gains"]
    weights = [Weights(i, kept["wide"], kept["down"]) for i in range(2)]
    held[
        place.section, place.at["y"], place.core, lax.rem(place.at["z"], 2), place.at["x"]
    ] = packed_shard(*shards)
    greet(
        [place.partner()]
        + [place.neighbour(axis, way) for axis in "xz" for way in (1, -1)]
        + [place.device(y=place.shifted("y", step)) for step in (1, 2, 3)]
        + [place.neighbour(axis, 2) for axis in "xz"]
    )
    leaving = [
        [
            scatter_steps(
                place,
                layer,
                part,
                SCATTER_DIRECT[layer][i],
                held,
                boxes[(3 * layer + i) * 5 : (3 * layer + i) * 5 + 5],
                scatter_sems[3 * layer + i],
                scatter_sems[6 + 3 * layer + i],
                summed_ref,
            )
            for i, part in enumerate(SCATTER_PARTS)
        ]
        for layer in range(2)
    ]
    edge = pltpu.make_async_remote_copy(
        src_ref=kept["edge"].at[0],
        dst_ref=kept["edge"].at[1],
        send_sem=edge_sems.at[0],
        recv_sem=edge_sems.at[1],
        device_id=place.device(z=place.shifted("z", 2)),
        device_id_type=MESH,
    )

    def finish_edge(section, mine):
        @pl.when(place.section == section)
        def _():
            stays_ref[...] = mine

        @pl.when(place.section != section)
        def _():
            kept["edge"][0] = mine.astype(BF16)
            edge.start()

    def go(layer, part):
        next(leaving[layer][part])

    arriving = [
        [
            gather_steps(
                place,
                layer,
                part,
                GATHER_DIRECT[layer][i],
                held,
                gather_sems[2 * layer + i],
                gather_sems[4 + 2 * layer + i],
            )
            for i, part in enumerate(GATHER_PARTS)
        ]
        for layer in range(2)
    ]

    def come(layer, part, steps=1):
        for _ in range(steps):
            next(arriving[layer][part])

    cos, sin = cos_ref[...], sin_ref[...]
    mine = lax.axis_index("ctx")
    gathers = [
        KeyGather(place, kept["joined"].at[i], key_sems[i], key_sems[4 + i]) for i in range(2)
    ]
    sums = [
        KeyGradSum(
            place,
            kept["parts"].at[i],
            kept["pair"],
            kept["ring"].at[i],
            key_sems[2 + i],
            key_sems[6 + i],
        )
        for i in range(2)
    ]
    grads = [
        WeightGrads(
            held.at[i],
            [kept[name] for name in ("first", "second", "third")],
            kept["gain_rows"],
            kept["lhs"],
            kept["hidden_lhs"],
        )
        for i in range(2)
    ]

    def start_layer(layer, current):
        unpack_gains(held, layer, gains_ref)
        unpack_wide(held, layer, LOWER, kept["wide"])
        kept["joined"][layer, mine] = project(
            current,
            gains_ref[layer, 0:1],
            weights[layer],
            cos,
            sin,
            kept["normed"].at[layer],
            kept["query"].at[layer],
        )
        gathers[layer].start()

    def attention_of_layer(layer):
        gathers[layer].finish()
        attended = attend(
            kept["query"].at[layer],
            kept["joined"].at[layer],
            seg_ref[place.section],
            kept["probs"].at[layer],
        )
        kept["attended"][layer] = attended

    def rest_of_layer(layer, current):
        unpack_wide(held, layer, UPPER, kept["wide"])
        unpack_down(held, layer, kept["down"])
        attended = kept["attended"][layer]
        midway, scale, normed_two, gate, up, hidden, result = feed_forward(
            current, attended, gains_ref[layer, 1:2], weights[layer]
        )
        kept["normed_two"][layer] = normed_two
        kept["hidden"][layer] = hidden
        return midway, gate, up, result

    def back_of_layer(layer, incoming, midway, gate, up, after, between):
        down_grad, gate_grad, up_grad, gain_grad, midway_grad, out_grad, mixed_grad = (
            feed_forward_back(incoming, midway, gate, up, gains_ref[layer, 1:2], weights[layer])
        )
        kept["down_grad"][...] = down_grad
        kept["gate_grad"][...] = gate_grad
        kept["up_grad"][...] = up_grad
        kept["out_grad"][...] = out_grad
        kept["midway_grad"][...] = midway_grad
        after()
        kept["query_grad"][...] = attend_back(
            mixed_grad,
            kept["attended"][layer],
            kept["query"].at[layer],
            kept["joined"].at[layer],
            kept["probs"].at[layer],
            kept["parts"].at[layer],
            between,
        )
        sums[layer].start()
        return gain_grad

    def end_of_layer(layer, current):
        sums[layer].finish(kept["key_grads"])
        turned, values, gain_grad, grad_in = project_back(
            kept["query_grad"][...],
            kept["key_grads"][...],
            kept["midway_grad"][...],
            current,
            gains_ref[layer, 0:1],
            cos,
            sin,
            weights[layer],
        )
        kept["turned"][...] = turned
        kept["values"][...] = values
        return gain_grad, grad_in

    def down_grads(layer, down_grad):
        grads[layer].down(kept["hidden"][layer], down_grad.astype(BF16))

    def middle_grads(layer):
        grads[layer].middle(
            kept["normed_two"][layer],
            kept["attended"][layer],
            kept["gate_grad"],
            kept["up_grad"],
            kept["out_grad"],
        )

    def late_grads(layer, attn_gain_grad, mlp_gain_grad):
        grads[layer].late(
            kept["normed"][layer],
            kept["turned"],
            kept["values"],
            kept["out_grad"],
            attn_gain_grad,
            mlp_gain_grad,
        )

    def give(part):
        pl.semaphore_signal(
            credits.at[part], inc=1, device_id=place.partner(), device_id_type=MESH
        )

    def begin(part):
        pl.semaphore_wait(credits.at[part], 1)
        go(0, part)

    upper, lower = 0, 1
    come(0, lower)
    come(0, upper)
    come(0, lower)
    come(0, upper)
    come(0, lower)
    come(1, lower)
    come(1, upper)
    come(0, upper)
    come(0, lower)
    come(0, upper)
    come(0, lower)

    x = x_ref[place.section].astype(F32).T
    start_layer(0, x)
    come(1, lower)
    come(1, upper)
    come(0, upper)
    gathers[0].pass_on()
    come(1, lower)
    come(1, upper)
    attention_of_layer(0)
    come(0, upper)
    come(1, lower)
    come(1, upper)
    come(0, upper)
    midway, gate, up, result = rest_of_layer(0, x)
    kept["midway"][...] = midway
    kept["gate"][...] = gate
    kept["up"][...] = up
    passed = result.astype(BF16)
    kept["x_2"][...] = passed
    come(1, lower)
    come(1, lower)
    start_layer(1, passed.astype(F32))
    come(1, upper)
    gathers[1].pass_on()
    attention_of_layer(1)
    come(1, upper)
    come(1, upper)
    midway, gate, up, result = rest_of_layer(1, kept["x_2"][...].astype(F32))
    finish_edge(1, result.T)

    first, second, third = 0, 1, 2
    incoming = late_ref[place.section].astype(F32).T
    down_grads(1, incoming)
    go(1, first)

    def nothing():
        pass

    def after_last_feed_forward():
        go(1, first)
        give(first)
        middle_grads(1)
        go(1, second)

    mlp_gain_grad_2 = back_of_layer(
        1, incoming, midway, gate, up, after_last_feed_forward, [nothing] * 3
    )
    sums[1].middle()
    go(1, first)
    go(1, second)
    give(second)
    attn_gain_grad_2, grad_in = end_of_layer(1, kept["x_2"][...].astype(F32))
    go(1, first)
    late_grads(1, attn_gain_grad_2, mlp_gain_grad_2)
    go(1, third)
    incoming = grad_in.astype(BF16).astype(F32)
    down_grads(0, incoming)
    begin(first)
    go(1, second)

    def after_feed_forward():
        go(1, third)
        give(third)
        go(1, first)
        go(0, first)
        middle_grads(0)
        begin(second)

    mlp_gain_grad_1 = back_of_layer(
        0,
        incoming,
        kept["midway"][...],
        kept["gate"][...],
        kept["up"][...],
        after_feed_forward,
        [nothing] * 3,
    )
    go(0, second)
    sums[0].middle()
    go(1, second)
    go(1, third)
    go(1, first)
    go(0, first)
    go(0, second)
    go(1, second)
    go(1, third)
    attn_gain_grad_1, grad_in = end_of_layer(0, x_ref[place.section].astype(F32).T)
    late_grads(0, attn_gain_grad_1, mlp_gain_grad_1)
    begin(third)
    finish_edge(0, grad_in.T)
    go(0, first)
    go(0, third)
    go(0, second)
    go(0, first)
    go(0, third)
    go(0, second)
    go(0, third)
    go(1, second)
    go(1, first)
    go(1, second)
    go(1, third)
    go(0, first)
    go(0, third)
    go(0, second)
    edge.wait()
    came_ref[...] = kept["edge"][1].astype(F32)


def run_layers(x, late, cos, sin, segments, shards):
    return pl.pallas_call(
        layers_kernel,
        out_shape=jax.ShapeDtypeStruct((PACKED + 2 * D, LANES), F32),
        in_specs=[VMEM] * 14,
        out_specs=VMEM,
        scratch_shapes=[
            pltpu.SemaphoreType.DMA((2,)),
            pltpu.SemaphoreType.REGULAR((3,)),
            *[pltpu.SemaphoreType.DMA((n,)) for n in (8, 8, 4, 4) * 2],
            *[pltpu.SemaphoreType.DMA((gather_slots(d),)) for row in GATHER_DIRECT for d in row] * 2,
            *[pltpu.SemaphoreType.DMA((scatter_slots(d),)) for row in SCATTER_DIRECT for d in row] * 2,
            *[pltpu.VMEM(shape, kind) for shape, kind in KEPT.values()],
            *[box for layer in range(2) for part in SCATTER_PARTS for box in scatter_inboxes(part)],
        ],
        compiler_params=params(2),
        name="layers",
    )(x, late, cos, sin, segments, *shards)


def rope_tables(first):
    places = first + jnp.arange(ROWS, dtype=jnp.int32)
    pair_index = jnp.arange(HEAD // 2).astype(F32)
    frequency = rope_base ** (-2.0 * pair_index / HEAD)
    angles = places.astype(F32)[:, None] * frequency[None, :]
    cos, sin = jnp.cos(angles), jnp.sin(angles)
    return jnp.concatenate([cos] * 4, axis=1), jnp.concatenate([-sin, sin] * 2, axis=1)


def local(block_input, cotangent, segment_ids, *shards):
    cos, sin = rope_tables(lax.axis_index("ctx") * ROWS)
    x = block_input[:, 0].transpose(0, 2, 1)
    late = cotangent[:, 0].transpose(0, 2, 1)
    return finish(run_layers(x, late, cos, sin, segment_ids, shards))


def solution(mesh):
    shard = P("section", ("ctx", "fsdp"))
    matrix = P("section", ("ctx", "fsdp"), None)
    return jax.shard_map(
        local,
        mesh=mesh,
        in_specs=(
            P(None, "fsdp", "ctx", None),
            P(None, "fsdp", "ctx", None),
            P(None, "fsdp", None),
            shard,
            matrix,
            matrix,
            matrix,
            matrix,
            matrix,
            matrix,
            matrix,
            shard,
        ),
        out_specs=(
            P("section", None, "fsdp", "ctx", None),
            shard,
            matrix,
            matrix,
            matrix,
            matrix,
            matrix,
            matrix,
            matrix,
            shard,
        ),
        check_vma=False,
    )
```
